32 devices in a mesh: gz: 16 (over z, y, x), gy: 2 (over core).
Axes of the slice: x: 2, y: 2, z: 4, core: 2. Of those that a mesh axis runs over, the one named last changes fastest.
Arguments:
- probe_fields: float32 [1, 32, 256, 1024], P(None, 'gz', 'gy'), may hold values from -24 to 24
- root_one: float32 [32, 1024], P('gz'), may hold values from 0.5 to 0.999
- root_two: float32 [32, 1024], P('gz'), may hold values from 0.3 to 0.8
- lateral_kernel_taps: float32 [2, 3], replicated, may hold values from 0.2 to 1
- dilations: int32 [2], replicated, may hold values from 1 to 8, as said below
Outputs:
- covariance_image: float32 [1, 32, 256, 1024], P(None, 'gz', 'gy')
The draws below stay inside these ranges and needn't reach their ends.
Inputs may be any that keep to these rules, and one draw needn't show every extreme that they name: `dilations`: one entry equals 8 and the other is smaller.
All inputs are finite; a program needn't handle non-finite values.
Results may differ from the reference program's by a relative error of at most 0.000044.
Values sent between devices are 32-bit elements; how exact they have to be, the bound alone decides.
No kernel may reach another device: no remote copies, remote signals or barrier semaphores. Data moves between devices by JAX's collectives and lax.ppermute only.
A program may use at most 64 MiB of HBM per device.

```python
import math
import jax
import jax.numpy as jnp
from jax import lax

PROBES = 1
NX = 1024
RADIUS = 2
DMAX = 8
DEPTH_PLANES = 32
NY = 256


def draw_root_one(key, part):
    key_base = jax.random.fold_in(key, 11)
    key_jitter = jax.random.fold_in(key, 12)
    random_key_group = jax.random.fold_in(key, 13)
    base = jnp.exp(jax.random.uniform(key_base, (NX,), jnp.float32, math.log(0.003), math.log(0.08)))
    jitter = jnp.exp(jax.random.uniform(key_jitter, (DEPTH_PLANES, NX), jnp.float32, math.log(0.7), math.log(1.4)))
    roots = 1.0 - base[None, :] * jitter
    position_slots = jax.random.randint(random_key_group, (3,), 0, DEPTH_PLANES)
    planes = jnp.arange(DEPTH_PLANES)
    hit = jnp.any(planes[:, None] == position_slots[None, :], axis=1)
    roots = jnp.where(hit[:, None], roots * 0.6, roots)
    return roots.astype(jnp.float32)


def draw_dilations(key, part):
    other = jax.random.randint(jax.random.fold_in(key, 21), (), 1, DMAX)
    which = jax.random.randint(jax.random.fold_in(key, 22), (), 0, 2)
    slots = jnp.arange(2)
    return jnp.where(slots == which, DMAX, other).astype(jnp.int32)


def steps_of(own_key, shape, pieces, low, top_value):
    level, own = 1.0, jax.random.fold_in(own_key, 6)
    for axis_at, blocks in pieces:
        draws = jnp.exp(jax.random.uniform(jax.random.fold_in(own, axis_at), (blocks,), jnp.float32, low / len(pieces), top_value / len(pieces)))
        level = level * jnp.repeat(draws, shape[axis_at] // blocks).reshape([-1 if axis == axis_at else 1 for axis in range(len(shape))])
    return level


def bell_draw(own_key, extent, width, most, split=(), held_as=jnp.bfloat16):
    level = steps_of(own_key, extent, split, -0.22, 0.18) if split else 1.0
    array = jax.random.normal(own_key, extent, jnp.float32) * width * level
    return jnp.minimum(jnp.maximum(array, -most), most).astype(held_as)


def setup_inputs(seed: int = 0) -> dict:
    keys = jax.random.split(jax.random.key(seed), 6)
    probe_fields = bell_draw(keys[0], (PROBES, DEPTH_PLANES, NY, NX), 4.0, 24.0, ((1, 16), (2, 2)), jnp.float32)
    root_one = draw_root_one(jax.random.fold_in(keys[5], 71), 0)
    root_two = jnp.clip(0.3 + 0.5 * jax.random.uniform(keys[2], (DEPTH_PLANES, NX), jnp.float32) ** steps_of(keys[2], (DEPTH_PLANES, NX), ((0, 16),), -0.2, 0.2), 0.3, 0.8)
    lateral_kernel_taps = jnp.clip(jnp.exp(jax.random.uniform(keys[3], (2, RADIUS + 1), jnp.float32, math.log(0.2), math.log(1.0))), 0.2, 1.0)
    dilations = draw_dilations(jax.random.fold_in(keys[5], 71), 0)
    return dict(probe_fields=probe_fields, root_one=root_one, root_two=root_two, lateral_kernel_taps=lateral_kernel_taps, dilations=dilations)


def filter_coefficients(root_one, root_two):
    first = root_one + root_two
    second = -root_one * root_two
    gain = (1.0 - root_one) * (1.0 - root_two)
    return first, second, gain


def adjoint_coefficients(first, second):
    first_next = jnp.concatenate([first[1:], jnp.zeros_like(first[:1])], 0)
    second_next = jnp.concatenate([second[2:], jnp.zeros_like(second[:2])], 0)
    return first_next, second_next


def depth_scan(fields, first, second, pre_gain, post_gain, reverse):
    moved = jnp.moveaxis(fields, 1, 0)
    zero = jnp.zeros(moved.shape[1:], jnp.float32)

    def advance(carry, inputs):
        latest, earlier = carry
        plane, coef_one, coef_two, before, after = inputs
        value = before * plane + coef_one * latest + coef_two * earlier
        return (value, latest), after * value

    _, outputs = lax.scan(advance, (zero, zero), (moved, first, second, pre_gain, post_gain), reverse=reverse)
    return jnp.moveaxis(outputs, 0, 1)


def lateral_padded(padded, weights, dilation, axis, margin, length):
    total = weights[0] + 2.0 * jnp.sum(weights[1:])
    scaled = weights / total
    result = scaled[0] * lax.dynamic_slice_in_dim(padded, margin, length, axis)
    for offset_tap in range(1, weights.shape[0]):
        offset = dilation * offset_tap
        upper = lax.dynamic_slice_in_dim(padded, margin + offset, length, axis)
        lower = lax.dynamic_slice_in_dim(padded, margin - offset, length, axis)
        result = result + scaled[offset_tap] * (upper + lower)
    return result


def lateral(fields, weights, dilation, axis):
    margin = RADIUS * DMAX
    widths = [(0, 0)] * fields.ndim
    widths[axis] = (margin, margin)
    padded = jnp.pad(fields, widths)
    return lateral_padded(padded, weights, dilation, axis, margin, fields.shape[axis])


def reference(probe_fields, root_one, root_two, lateral_kernel_taps, dilations):
    first, second, gain = filter_coefficients(root_one, root_two)
    unity = jnp.ones_like(gain)
    first_next, second_next = adjoint_coefficients(first, second)
    field = depth_scan(probe_fields, first_next, second_next, unity, gain, True)
    field = lateral(field, lateral_kernel_taps[0], dilations[0], 3)
    field = lateral(field, lateral_kernel_taps[1], dilations[1], 2)
    field = lateral(field, lateral_kernel_taps[1], dilations[1], 2)
    field = lateral(field, lateral_kernel_taps[0], dilations[0], 3)
    return depth_scan(field, first, second, gain, unity, False)
```

```python
import functools

import jax
import jax.numpy as jnp
from jax import lax
from jax.experimental import pallas as pl
from jax.experimental.pallas import tpu as pltpu
from jax.sharding import PartitionSpec as P

RADIUS = 2
DMAX = 8
MARGIN = RADIUS * DMAX
LANES = 128
SUB = 8


def padded_y(array, width):
    size, length = lax.axis_size("gy"), array.shape[2]
    up = [(i, (i + 1) % size) for i in range(size - 1)]
    down = [(j, i) for i, j in up]
    last = lax.slice_in_dim(array, length - width, length, axis=2)
    leading = lax.slice_in_dim(array, 0, width, axis=2)
    before = lax.ppermute(last, "gy", up)
    after = lax.ppermute(leading, "gy", down)
    return jnp.concatenate([before, array, after], axis=2)


def filter_coefficients(root_one, root_two):
    first = root_one + root_two
    second = -root_one * root_two
    gain = (1.0 - root_one) * (1.0 - root_two)
    return (first, second, gain)


def depth_scan(fields, first, second, pre_gain, post_gain, reverse):
    moved = jnp.moveaxis(fields, 1, 0)
    zero = jnp.zeros(moved.shape[1:], jnp.float32)

    def advance(carry, inputs):
        latest, earlier = carry
        plane, coef_one, coef_two, before, after = inputs
        value = before * plane + coef_one * latest + coef_two * earlier
        return ((value, latest), after * value)

    _, outputs = lax.scan(
        advance, (zero, zero), (moved, first, second, pre_gain, post_gain), reverse=reverse
    )
    return jnp.moveaxis(outputs, 0, 1)


def normalised(weights):
    return weights / (weights[..., :1] + 2.0 * jnp.sum(weights[..., 1:], -1, keepdims=True))


def lateral_padded(padded, scaled, dilation, axis, margin, length):
    result = scaled[0] * lax.dynamic_slice_in_dim(padded, margin, length, axis)
    for offset_tap in range(1, scaled.shape[0]):
        offset = dilation * offset_tap
        upper = lax.dynamic_slice_in_dim(padded, margin + offset, length, axis)
        lower = lax.dynamic_slice_in_dim(padded, margin - offset, length, axis)
        result = result + scaled[offset_tap] * (upper + lower)
    return result


def lateral_x(fields, scaled, dilation):
    padded = jnp.pad(fields, ((0, 0), (0, 0), (0, 0), (MARGIN, MARGIN)))
    return lateral_padded(padded, scaled, dilation, 3, MARGIN, fields.shape[3])


def lateral_y_twice(fields, scaled, dilation):
    rows = fields.shape[2]
    padded = padded_y(fields, 2 * MARGIN)
    middle = lateral_padded(padded, scaled, dilation, 2, MARGIN, rows + 2 * MARGIN)
    global_row = lax.axis_index("gy") * rows - MARGIN + jnp.arange(rows + 2 * MARGIN)
    inside = (global_row >= 0) & (global_row < rows * lax.axis_size("gy"))
    middle = jnp.where(inside[None, None, :, None], middle, 0.0)
    return lateral_padded(middle, scaled, dilation, 2, MARGIN, rows)


def plain_body(probe_fields, root_one, root_two, lateral_kernel_taps, dilations):
    roots = lax.all_gather(jnp.stack([root_one, root_two], 1), "gz", axis=0, tiled=True)
    first, second, gain = filter_coefficients(roots[:, 0], roots[:, 1])
    unity = jnp.ones_like(gain)
    first_next = jnp.concatenate([first[1:], jnp.zeros_like(first[:1])], 0)
    second_next = jnp.concatenate([second[2:], jnp.zeros_like(second[:2])], 0)
    scaled = normalised(lateral_kernel_taps)
    field = lateral_y_twice(probe_fields, scaled[1], dilations[1])
    field = lax.all_to_all(field, "gz", split_axis=2, concat_axis=1, tiled=True)
    field = depth_scan(field, first_next, second_next, unity, gain, True)
    field = lateral_x(field, scaled[0], dilations[0])
    field = lateral_x(field, scaled[0], dilations[0])
    field = depth_scan(field, first, second, gain, unity, False)
    return lax.all_to_all(field, "gz", split_axis=1, concat_axis=2, tiled=True)


def call(kernel, outs, scratch, scalars, arrays, flops=1 << 20):
    arrays = [pltpu.with_memory_space_constraint(a, pltpu.VMEM) for a in arrays]
    return pl.pallas_call(
        kernel,
        out_shape=[pltpu.VMEM(shape, jnp.float32) for shape in outs],
        in_specs=[pl.BlockSpec(memory_space=pltpu.SMEM)] * len(scalars)
        + [pl.BlockSpec(memory_space=pltpu.VMEM)] * len(arrays),
        out_specs=[pl.BlockSpec(memory_space=pltpu.VMEM)] * len(outs),
        scratch_shapes=[pltpu.VMEM(shape, jnp.float32) for shape in scratch],
        compiler_params=pltpu.CompilerParams(vmem_limit_bytes=24 << 20),
        cost_estimate=pl.CostEstimate(flops=flops, bytes_accessed=1 << 20, transcendentals=0),
    )(*scalars, *arrays)


def weighted(centre, pairs, taps):
    total = taps[0] * centre
    for tap, (upper, lower) in zip(taps[1:], pairs):
        total = total + tap * (upper + lower)
    return total


def y_twice_kernel(groups, sizes, ints, taps, x_ref, top_ref, bottom_ref, *rest):
    outs, (wide, middle) = rest[:groups], rest[groups:]
    planes, rows, columns = x_ref.shape
    step, mine, row_at, row_places = ints[1], ints[2] % groups, ints[3], sizes
    taps = [taps[1, i] for i in range(RADIUS + 1)]
    inner = rows + 2 * MARGIN
    row_id = lax.broadcasted_iota(jnp.int32, (inner, LANES), 0) + (row_at * rows - MARGIN)
    inside = (row_id >= 0) & (row_id < rows * row_places)
    has_top, has_bottom = row_at > 0, row_at < row_places - 1
    each = rows // groups

    def block(b, _):
        lanes = pl.ds(pl.multiple_of(b * LANES, LANES), LANES)
        for p in range(planes):
            top, bottom = top_ref[p, :, lanes], bottom_ref[p, :, lanes]
            wide[p, 0 : 2 * MARGIN] = jnp.where(has_top, top, jnp.zeros_like(top))
            wide[p, 2 * MARGIN : 2 * MARGIN + rows] = x_ref[p, :, lanes]
            wide[p, 2 * MARGIN + rows :] = jnp.where(has_bottom, bottom, jnp.zeros_like(bottom))
        for p in range(planes):
            pairs = [
                (
                    wide[p, pl.ds(MARGIN + t * step, inner)],
                    wide[p, pl.ds(MARGIN - t * step, inner)],
                )
                for t in range(1, RADIUS + 1)
            ]
            value = weighted(wide[p, MARGIN : MARGIN + inner], pairs, taps)
            middle[p] = jnp.where(inside, value, jnp.zeros_like(value))
        for p in range(planes):
            for m, out in enumerate(outs):
                at = (mine ^ m) * each + MARGIN
                pairs = [
                    (
                        middle[p, pl.ds(at + t * step, each)],
                        middle[p, pl.ds(at - t * step, each)],
                    )
                    for t in range(1, RADIUS + 1)
                ]
                centre = middle[p, pl.ds(pl.multiple_of(at, SUB), each)]
                out[p, :, lanes] = weighted(centre, pairs, taps)
        return 0

    lax.fori_loop(0, columns // LANES, block, 0)


def x_twice(blocks, step, taps):
    lane = lax.broadcasted_iota(jnp.int32, (SUB, LANES), 1)
    zero = jnp.zeros((SUB, LANES), jnp.float32)
    count = len(blocks)
    for _ in range(2):
        sums = [taps[0] * block for block in blocks]
        for t in range(1, RADIUS + 1):
            shift = t * step
            right = [pltpu.roll(block, shift, 1) for block in blocks]
            left = [pltpu.roll(block, LANES - shift, 1) for block in blocks]
            from_right, from_left = lane >= shift, lane < LANES - shift
            for i in range(count):
                lower = jnp.where(from_right, right[i], right[i - 1] if i else zero)
                upper = jnp.where(from_left, left[i], left[i + 1] if i + 1 < count else zero)
                sums[i] = sums[i] + taps[t] * (upper + lower)
        blocks = sums
    return blocks


def get(ref, *at):
    columns = ref.shape[-1]
    return [ref[(*at, slice(i, i + LANES))] for i in range(0, columns, LANES)]


def put(ref, blocks, *at):
    for i, block in enumerate(blocks):
        ref[(*at, slice(i * LANES, (i + 1) * LANES))] = block


def fma(*terms):
    products = [[x * y for x, y in zip(xs, ys)] for xs, ys in terms]
    return functools.reduce(add, products)


def add(a, b):
    return [x + y for x, y in zip(a, b)]


def store_coefficients(roots, planes, mine, first, second, gain):
    groups = roots.shape[0] // (2 * planes)
    count, columns = groups * planes, roots.shape[1]
    for extra in range(2):
        first[count + extra] = jnp.zeros((SUB, columns), jnp.float32)
        second[count + extra] = jnp.zeros((SUB, columns), jnp.float32)
    for e in range(groups):
        for p in range(planes):
            at = (mine ^ e) * planes + p
            one = roots[pl.ds(2 * planes * e + p, 1), :]
            two = roots[pl.ds(2 * planes * e + planes + p, 1), :]
            wide = (SUB, columns)
            first[at] = jnp.broadcast_to(one + two, wide)
            second[at] = jnp.broadcast_to(-one * two, wide)
            gain[at] = jnp.broadcast_to((1.0 - one) * (1.0 - two), wide)


def down_and_up(count, tile, source, middle, first, second, gain, step, taps, finish, extra=None):
    zeros = get(first, count, slice(None))

    def back(i, carry):
        k = count - 1 - i
        latest, earlier = carry
        value = fma((get(first, k + 1, slice(None)), latest), (get(second, k + 2, slice(None)), earlier))
        if source is not None:
            value = add(value, source(k))
        scaled = [g * v for g, v in zip(get(gain, k, slice(None)), value)]
        put(middle, x_twice(scaled, step, taps), k, slice(None))
        return value, latest

    start = (zeros, zeros)
    begin = 0
    if extra is not None:
        a, b = extra
        k = count - 1
        scaled = [g * v for g, v in zip(get(gain, k, slice(None)), a)]
        put(middle, x_twice(scaled, step, taps), k, slice(None))
        k = count - 2
        value = add(fma((get(first, k + 1, slice(None)), a)), b)
        scaled = [g * v for g, v in zip(get(gain, k, slice(None)), value)]
        put(middle, x_twice(scaled, step, taps), k, slice(None))
        start, begin = (value, a), 2
    back_last = lax.fori_loop(begin, count, back, start)

    def forth(k, carry):
        latest, earlier = carry
        value = fma(
            (get(gain, k, slice(None)), get(middle, k, slice(None))),
            (get(first, k, slice(None)), latest),
            (get(second, k, slice(None)), earlier),
        )
        if finish is not None:
            finish(k, value)
        return value, latest

    forth_last = lax.fori_loop(0, count, forth, (zeros, zeros))
    return back_last, forth_last


def local_kernel(groups, planes, ints, taps, roots, *rest):
    pieces, (result, message, first, second, gain, field, middle) = rest[:groups], rest[groups:]
    mine, half = ints[2] % groups, ints[2] // groups
    step, taps = ints[0], [taps[0, i] for i in range(RADIUS + 1)]
    count = groups * planes
    rows = pieces[0].shape[1]
    store_coefficients(roots, planes, mine, first, second, gain)
    for m, piece in enumerate(pieces):
        for p in range(planes):
            field[(mine ^ m) * planes + p] = piece[p]
    everywhere = slice(None)

    def tile_at(tile, _):
        tile_rows = pl.ds(pl.multiple_of(tile * SUB, SUB), SUB)
        (z0, z1), (y1, y2) = down_and_up(
            count,
            tile,
            lambda k: get(field, k, tile_rows),
            middle,
            first,
            second,
            gain,
            step,
            taps,
            lambda k, value: put(result, value, k, tile_rows),
        )

        @pl.when(half > 0)
        def _():
            ahead = fma(
                (get(first, 0, everywhere), z0),
                (get(second, 1, everywhere), z1),
            )
            put(message, ahead, 0, tile_rows)
            put(message, fma((get(second, 0, everywhere), z0)), 1, tile_rows)

        @pl.when(half == 0)
        def _():
            put(message, y1, 0, tile_rows)
            put(message, y2, 1, tile_rows)

        return 0

    lax.fori_loop(0, rows // SUB, tile_at, 0)


def forward_kernel(groups, planes, ints, taps, roots, message, state, first, second, gain, middle):
    mine, half = ints[2] % groups, ints[2] // groups
    step, taps = ints[0], [taps[0, i] for i in range(RADIUS + 1)]
    count = groups * planes
    rows = message.shape[1]

    @pl.when(half > 0)
    def _():
        store_coefficients(roots, planes, mine, first, second, gain)

        def tile_at(tile, _):
            tile_rows = pl.ds(pl.multiple_of(tile * SUB, SUB), SUB)
            carried = (get(message, 0, tile_rows), get(message, 1, tile_rows))
            _, (y1, y2) = down_and_up(
                count, tile, None, middle, first, second, gain, step, taps, None, carried
            )
            put(state, y1, 0, tile_rows)
            put(state, y2, 1, tile_rows)
            return 0

        lax.fori_loop(0, rows // SUB, tile_at, 0)

    @pl.when(half == 0)
    def _():
        state[...] = jnp.zeros(state.shape, jnp.float32)


def join_kernel(groups, planes, ints, taps, local, received, state, first, second, gain, *rest):
    outs, (total, middle) = rest[:groups], rest[groups:]
    mine, half = ints[2] % groups, ints[2] // groups
    step, taps = ints[0], [taps[0, i] for i in range(RADIUS + 1)]
    count = groups * planes
    rows = received.shape[1]
    everywhere = slice(None)

    def tile_at(tile, _):
        tile_rows = pl.ds(pl.multiple_of(tile * SUB, SUB), SUB)
        a, b = get(received, 0, tile_rows), get(received, 1, tile_rows)

        @pl.when(half == 0)
        def _():
            def finish(k, value):
                put(total, add(value, get(local, k, tile_rows)), k, tile_rows)

            down_and_up(
                count, tile, None, middle, first, second, gain, step, taps, finish, (a, b)
            )

        @pl.when(half > 0)
        def _():
            def forth(k, carry):
                latest, earlier = carry
                value = fma(
                    (get(first, k, everywhere), latest), (get(second, k, everywhere), earlier)
                )
                put(total, add(value, get(local, k, tile_rows)), k, tile_rows)
                return value, latest

            start = (add(a, get(state, 0, tile_rows)), add(b, get(state, 1, tile_rows)))
            lax.fori_loop(0, count, forth, start)

        return 0

    lax.fori_loop(0, rows // SUB, tile_at, 0)
    for m, out in enumerate(outs):
        for p in range(planes):
            out[p] = total[(mine ^ m) * planes + p]


def place_kernel(groups, ints, *rest):
    pieces, out = rest[:groups], rest[groups]
    mine = ints[2] % groups
    each = pieces[0].shape[1]
    for m, piece in enumerate(pieces):
        out[:, pl.ds(pl.multiple_of((mine ^ m) * each, SUB), each), :] = piece[...]


def grouped_body(probe_fields, root_one, root_two, lateral_kernel_taps, dilations):
    _, planes, rows, columns = probe_fields.shape
    places, row_places = lax.axis_size("gz"), lax.axis_size("gy")
    groups = places // 2
    each, count = rows // groups, groups * planes
    at, row_at = lax.axis_index("gz"), lax.axis_index("gy")
    ints = jnp.stack([dilations[0], dilations[1], at, row_at]).astype(jnp.int32)
    taps = normalised(lateral_kernel_taps)

    def across(array, m):
        return lax.ppermute(array, "gz", [(i, i ^ m) for i in range(places)])

    field = probe_fields[0]
    width = 2 * MARGIN
    start = jnp.where(row_at == 0, rows - width, 0)
    edge = lax.dynamic_slice_in_dim(field, start, width, axis=1)
    edge = lax.ppermute(edge, "gy", [(0, 1), (1, 0)])

    roots = jnp.concatenate([root_one, root_two], 0)
    for bit in range(groups.bit_length() - 1):
        roots = jnp.concatenate([roots, across(roots, 1 << bit)], 0)
    other_roots = across(roots, groups)

    piece, tile = (planes, each, columns), (count, SUB, columns)
    coefficients = (count + 2, SUB, columns)
    pieces = call(
        functools.partial(y_twice_kernel, groups, row_places),
        [piece] * groups,
        [(planes, rows + 4 * MARGIN, LANES), (planes, rows + 2 * MARGIN, LANES)],
        [ints, taps],
        [field, edge, edge],
    )
    pieces = [pieces[0]] + [across(pieces[m], m) for m in range(1, groups)]
    local, message, first, second, gain = call(
        functools.partial(local_kernel, groups, planes),
        [(count, each, columns), (2, each, columns), coefficients, coefficients, coefficients],
        [(count, each, columns), tile],
        [ints, taps],
        [roots, *pieces],
    )
    received = across(message, groups)
    (state,) = call(
        functools.partial(forward_kernel, groups, planes),
        [(2, each, columns)],
        [coefficients, coefficients, coefficients, tile],
        [ints, taps],
        [other_roots, message],
    )
    pieces = call(
        functools.partial(join_kernel, groups, planes),
        [piece] * groups,
        [(count, each, columns), tile],
        [ints, taps],
        [local, received, state, first, second, gain],
    )
    pieces = [pieces[0]] + [across(pieces[m], m) for m in range(1, groups)]
    (out,) = call(
        functools.partial(place_kernel, groups),
        [(planes, rows, columns)],
        [],
        [ints],
        pieces,
    )
    return out[None]


def body(*arrays):
    probes, planes, rows, columns = arrays[0].shape
    places, row_places = lax.axis_size("gz"), lax.axis_size("gy")
    fits = (
        probes == 1
        and row_places == 2
        and places >= 4
        and places & (places - 1) == 0
        and rows % (SUB * (places // 2)) == 0
        and rows >= 2 * MARGIN
        and columns % LANES == 0
        and planes * places >= 4
    )
    return grouped_body(*arrays) if fits else plain_body(*arrays)


def solution(mesh):
    placed = (P(None, "gz", "gy", None), P("gz", None), P("gz", None), P(), P())
    return jax.shard_map(
        body, mesh=mesh, in_specs=placed, out_specs=P(None, "gz", "gy", None), check_vma=False
    )
```

```python
import functools

import jax
import jax.numpy as jnp
from jax import lax
from jax.experimental import pallas as pl
from jax.experimental.pallas import tpu as pltpu
from jax.sharding import PartitionSpec as P

RADIUS = 2
DMAX = 8
MARGIN = RADIUS * DMAX
LANES = 128
SUB = 8


def padded_y(array, width):
    size, length = lax.axis_size("gy"), array.shape[2]
    up = [(i, (i + 1) % size) for i in range(size - 1)]
    down = [(j, i) for i, j in up]
    last = lax.slice_in_dim(array, length - width, length, axis=2)
    leading = lax.slice_in_dim(array, 0, width, axis=2)
    before = lax.ppermute(last, "gy", up)
    after = lax.ppermute(leading, "gy", down)
    return jnp.concatenate([before, array, after], axis=2)


def filter_coefficients(root_one, root_two):
    first = root_one + root_two
    second = -root_one * root_two
    gain = (1.0 - root_one) * (1.0 - root_two)
    return (first, second, gain)


def depth_scan(fields, first, second, pre_gain, post_gain, reverse):
    moved = jnp.moveaxis(fields, 1, 0)
    zero = jnp.zeros(moved.shape[1:], jnp.float32)

    def advance(carry, inputs):
        latest, earlier = carry
        plane, coef_one, coef_two, before, after = inputs
        value = before * plane + coef_one * latest + coef_two * earlier
        return ((value, latest), after * value)

    _, outputs = lax.scan(
        advance, (zero, zero), (moved, first, second, pre_gain, post_gain), reverse=reverse
    )
    return jnp.moveaxis(outputs, 0, 1)


def normalised(weights):
    return weights / (weights[..., :1] + 2.0 * jnp.sum(weights[..., 1:], -1, keepdims=True))


def lateral_padded(padded, scaled, dilation, axis, margin, length):
    result = scaled[0] * lax.dynamic_slice_in_dim(padded, margin, length, axis)
    for offset_tap in range(1, scaled.shape[0]):
        offset = dilation * offset_tap
        upper = lax.dynamic_slice_in_dim(padded, margin + offset, length, axis)
        lower = lax.dynamic_slice_in_dim(padded, margin - offset, length, axis)
        result = result + scaled[offset_tap] * (upper + lower)
    return result


def lateral_x(fields, scaled, dilation):
    padded = jnp.pad(fields, ((0, 0), (0, 0), (0, 0), (MARGIN, MARGIN)))
    return lateral_padded(padded, scaled, dilation, 3, MARGIN, fields.shape[3])


def lateral_y_twice(fields, scaled, dilation):
    rows = fields.shape[2]
    padded = padded_y(fields, 2 * MARGIN)
    middle = lateral_padded(padded, scaled, dilation, 2, MARGIN, rows + 2 * MARGIN)
    global_row = lax.axis_index("gy") * rows - MARGIN + jnp.arange(rows + 2 * MARGIN)
    inside = (global_row >= 0) & (global_row < rows * lax.axis_size("gy"))
    middle = jnp.where(inside[None, None, :, None], middle, 0.0)
    return lateral_padded(middle, scaled, dilation, 2, MARGIN, rows)


def plain_body(probe_fields, root_one, root_two, lateral_kernel_taps, dilations):
    roots = lax.all_gather(jnp.stack([root_one, root_two], 1), "gz", axis=0, tiled=True)
    first, second, gain = filter_coefficients(roots[:, 0], roots[:, 1])
    unity = jnp.ones_like(gain)
    first_next = jnp.concatenate([first[1:], jnp.zeros_like(first[:1])], 0)
    second_next = jnp.concatenate([second[2:], jnp.zeros_like(second[:2])], 0)
    scaled = normalised(lateral_kernel_taps)
    field = lateral_y_twice(probe_fields, scaled[1], dilations[1])
    field = lax.all_to_all(field, "gz", split_axis=2, concat_axis=1, tiled=True)
    field = depth_scan(field, first_next, second_next, unity, gain, True)
    field = lateral_x(field, scaled[0], dilations[0])
    field = lateral_x(field, scaled[0], dilations[0])
    field = depth_scan(field, first, second, gain, unity, False)
    return lax.all_to_all(field, "gz", split_axis=1, concat_axis=2, tiled=True)


def call(kernel, outs, scratch, scalars, arrays, cost):
    arrays = [pltpu.with_memory_space_constraint(a, pltpu.VMEM) for a in arrays]
    outs = [out if len(out) == 2 else (out, jnp.float32) for out in outs]
    return pl.pallas_call(
        kernel,
        out_shape=[pltpu.VMEM(shape, dtype) for shape, dtype in outs],
        in_specs=[pl.BlockSpec(memory_space=pltpu.SMEM)] * len(scalars)
        + [pl.BlockSpec(memory_space=pltpu.VMEM)] * len(arrays),
        out_specs=[pl.BlockSpec(memory_space=pltpu.VMEM)] * len(outs),
        scratch_shapes=[pltpu.VMEM(shape, jnp.float32) for shape in scratch],
        compiler_params=pltpu.CompilerParams(vmem_limit_bytes=24 << 20),
        cost_estimate=pl.CostEstimate(flops=cost, bytes_accessed=1 << 16, transcendentals=0),
    )(*scalars, *arrays)


def tap_vectors(taps, axis, shape):
    raw = [taps[axis, i] for i in range(RADIUS + 1)]
    total = raw[0] + 2.0 * functools.reduce(lambda a, b: a + b, raw[1:])
    scale = 1.0 / jnp.full(shape, total, jnp.float32)
    return [jnp.full(shape, tap, jnp.float32) * scale for tap in raw]


def split(value):
    high = value.astype(jnp.bfloat16)
    return high, (value - high.astype(jnp.float32)).astype(jnp.bfloat16)


def product(left, right):
    dot = functools.partial(jnp.dot, preferred_element_type=jnp.float32)
    return dot(left[0], right[0]) + (dot(left[0], right[1]) + dot(left[1], right[0]))


OFFSETS = range(-RADIUS, RADIUS + 1)


def double_taps(at, length, step, taps):
    sums = {}
    for a in OFFSETS:
        middle = at + a * step
        tap = jnp.where((middle >= 0) & (middle < length), taps[abs(a)], 0.0)
        for b in OFFSETS:
            sums[a + b] = sums.get(a + b, 0.0) + tap * taps[abs(b)]
    return sums


def fill_band(high, low, row_places, step, taps, begin, from_begin):
    part = 2 * SUB
    for i in range(0, high.shape[0], part):
        shape = (part, high.shape[1])
        at = lax.broadcasted_iota(jnp.int32, shape, 0) + (begin + i)
        apart = lax.broadcasted_iota(jnp.int32, shape, 1) + from_begin - at
        value = jnp.zeros(shape, jnp.float32)
        for o, total in double_taps(at, row_places, step, taps).items():
            value = jnp.where(apart == o * step, total, value)
        high[i : i + part], low[i : i + part] = split(value)


def load_kernel(
    x_ref, one_ref, two_ref, dilations_ref, taps_ref,
    whole, edge, roots, high, low, edge_high, edge_low, one, two, dilations, taps, sems,
):
    row_at, row_places = lax.axis_index("gy"), lax.axis_size("gy")
    planes, tiles = x_ref.shape[:2]
    depth, blocks = edge.shape[1:3]
    rows = tiles * SUB
    start = jnp.where(row_at == 0, tiles - depth, 0)
    copies = [
        pltpu.make_async_copy(x_ref.at[:, pl.ds(start, depth)], edge, sems.at[0]),
        pltpu.make_async_copy(one_ref, one, sems.at[1]),
        pltpu.make_async_copy(two_ref, two, sems.at[2]),
        pltpu.make_async_copy(dilations_ref, dilations, sems.at[3]),
        pltpu.make_async_copy(taps_ref, taps, sems.at[4]),
    ]
    copies += [
        pltpu.make_async_copy(x_ref.at[p], whole.at[p], sems.at[5 + p]) for p in range(planes)
    ]
    for copy in copies:
        copy.start()
    for copy in copies[1:5]:
        copy.wait()
    for p in range(planes):
        for b in range(blocks):
            lanes = slice(b * LANES, (b + 1) * LANES)
            roots[p, b : b + 1] = one[p : p + 1, lanes]
            roots[planes + p, b : b + 1] = two[p : p + 1, lanes]
    step, weights = dilations[1], tap_vectors(taps, 1, (1, 1))
    length, begin = rows * row_places, row_at * rows
    fill_band(high, low, length, step, weights, begin, begin)
    near = begin + jnp.where(row_at == 0, rows - 2 * MARGIN, 0)
    beyond = begin + jnp.where(row_at == 0, rows, -2 * MARGIN)
    fill_band(edge_high, edge_low, length, step, weights, near, beyond)
    copies[0].wait()
    for copy in copies[5:]:
        copy.wait()


def columns_of(ref, p, b, width):
    rows = ref.shape[1] * SUB
    return jnp.concatenate([ref[p, :, b + i].reshape(rows, LANES) for i in range(width)], axis=1)


def y_inner_kernel(groups, high, low, x_ref, pieces):
    planes, tiles, blocks = x_ref.shape[:3]
    chunks, width = tiles // groups, 2
    for p in range(planes):
        for b in range(0, blocks, width):
            value = product((high[...], low[...]), split(columns_of(x_ref, p, b, width)))
            for i in range(tiles):
                for w in range(width):
                    tile = value[i * SUB : (i + 1) * SUB, w * LANES : (w + 1) * LANES]
                    pieces[i // chunks, (p * chunks + i % chunks) * blocks + b + w] = tile


def y_outer_kernel(groups, tiles, high, low, edge, roots, other_roots, given, pieces):
    planes, halo, blocks = edge.shape[:3]
    chunks, width = tiles // groups, 2
    base = chunks * planes * blocks
    pieces[:, :base] = given[...]
    first = jnp.where(lax.axis_index("gy") == 0, (tiles - halo) // chunks, 0)
    for p in range(planes):
        for b in range(0, blocks, width):
            value = product((high[...], low[...]), split(columns_of(edge, p, b, width)))
            for i in range(halo):
                for w in range(width):
                    tile = value[i * SUB : (i + 1) * SUB, w * LANES : (w + 1) * LANES]
                    to, at = first + i // chunks, (p * chunks + i % chunks) * blocks
                    pieces[to, at + b + w] = given[to, at + b + w] + tile
    for i in range(groups):
        for r in range(2 * planes):
            pieces[i, base + r] = roots[r]
            pieces[i, base + 2 * planes + r] = other_roots[r]


def band_kernel(columns, dilations, taps, high, low):
    count, depth, width = high.shape
    step, taps = dilations[0], tap_vectors(taps, 0, (1, width))
    part = 2 * SUB
    lane = lax.broadcasted_iota(jnp.int32, (part, width), 1)
    row = lax.broadcasted_iota(jnp.int32, (part, width), 0)
    for n in range(count):
        at = lax.broadcasted_iota(jnp.int32, (1, width), 1) + n * width
        sums = double_taps(at, columns, step, taps)

        def rows_at(i, _):
            apart = row + (i * part - LANES) - lane
            value = jnp.zeros((part, width), jnp.float32)
            for o, total in sums.items():
                value = jnp.where(apart == o * step, total, value)
            at_rows = pl.ds(pl.multiple_of(i * part, part), part)
            high[n, at_rows], low[n, at_rows] = split(value)
            return 0

        lax.fori_loop(0, depth // part, rows_at, 0)


def x_twice(source, result, high, low):
    for n in range(high.shape[0]):
        depth, width = high.shape[1:]
        value = split(source[:, n * width : n * width + depth])
        result[:, n * width : (n + 1) * width] = product(value, (high[n], low[n]))


def add(a, b):
    return [x + y for x, y in zip(a, b)]


def times(ref, k, values):
    return [ref[k, b : b + 1] * value for b, value in enumerate(values)]


def tiles_of(ref, *at):
    return [ref[(*at, b)] for b in range(ref.shape[len(at)])]


def put(ref, values, *at):
    for b, value in enumerate(values):
        ref[(*at, b)] = value


def clear_sides(field):
    columns = field.shape[1] - 2 * LANES
    none = jnp.zeros((field.shape[0], LANES), jnp.float32)
    field[:, :LANES] = none
    field[:, LANES + columns :] = none


def row_tile(k):
    return pl.ds(pl.multiple_of(k * SUB, SUB), SUB)


def filter_back(count, planes, source, coefficients, field, start):
    first, second, gain = coefficients
    after, beyond = start

    def at(d, carry):
        for p in reversed(range(planes)):
            ahead, pending = carry
            k = d * planes + p
            value = ahead if source is None else add(source(d, p), ahead)
            for b, scaled in enumerate(times(gain, k, value)):
                field[row_tile(k), (b + 1) * LANES : (b + 2) * LANES] = scaled
            carry = (add(times(first, k, value), pending), times(second, k, value))
        return carry

    steps = count // planes
    return lax.fori_loop(0, steps, lambda i, c: at(steps - 1 - i, c), (after, beyond))


def filter_forth(count, planes, field, coefficients, start, finish):
    first, second, gain = coefficients

    def at(d, carry):
        for p in range(planes):
            latest, earlier = carry
            k = d * planes + p
            value = add(times(first, k, latest), times(second, k, earlier))
            if field is not None:
                blocks = len(value)
                there = [
                    field[row_tile(k), b * LANES : (b + 1) * LANES] for b in range(blocks)
                ]
                value = add(value, times(gain, k, there))
            finish(d, p, value)
            carry = (value, latest)
        return carry

    return lax.fori_loop(0, count // planes, at, start)


def store_coefficients(k, one, two, first, second, gain):
    first[k] = one + two
    second[k] = -one * two
    gain[k] = (1.0 - one) * (1.0 - two)


def local_kernel(groups, planes, chunks, chunk, *refs):
    if chunk == 0:
        pieces, high, low, local, message, *coefficients, field, middle = refs
    else:
        pieces, high, low, *coefficients, local, message, field, middle = refs
    half = lax.axis_index("gz") // groups
    blocks = message.shape[1]
    count = groups * planes
    own = coefficients[:3]
    if chunk == 0:
        base = chunks * planes * blocks
        for d in range(groups):
            for p in range(planes):
                k = d * planes + p
                one, two = (pieces[d, base + i * planes + p] for i in range(2))
                store_coefficients(k, one, two, *own)
                other_one, other_two = (pieces[d, base + (2 + i) * planes + p] for i in range(2))
                one = jnp.where(half == 0, one, other_one)
                two = jnp.where(half == 0, two, other_two)
                store_coefficients(k, one, two, *coefficients[3:])
    clear_sides(field)
    zeros = [field[0:SUB, 0:LANES]] * blocks

    def source(d, p):
        return [pieces[d, (p * chunks + chunk) * blocks + b] for b in range(blocks)]

    ahead, pending = filter_back(count, planes, source, own, field, (zeros, zeros))
    x_twice(field, middle, high, low)

    def finish(d, p, value):
        for b, v in enumerate(value):
            local[d, p * blocks + b] = v

    latest, earlier = filter_forth(count, planes, middle, own, (zeros, zeros), finish)
    for b in range(blocks):
        message[0, b] = jnp.where(half > 0, ahead[b], latest[b])
        message[1, b] = jnp.where(half > 0, pending[b], earlier[b])


def join_kernel(groups, planes, chunks, chunk, local, sent, received, high, low, *refs):
    own, lower, before = refs[:3], refs[3:6], refs[6:-4]
    out, carried, field, middle = refs[-4:]
    half = lax.axis_index("gz") // groups
    blocks = sent.shape[1]
    count = groups * planes
    for ref in before:
        out[...] = ref[...]
    for i in range(2):
        for b in range(blocks):
            carried[i, b] = jnp.where(half == 0, received[i, b], sent[i, b])
    clear_sides(field)
    zeros = [field[0:SUB, 0:LANES]] * blocks
    start = (tiles_of(carried, 0), tiles_of(carried, 1))
    filter_back(count, planes, None, lower, field, start)
    x_twice(field, middle, high, low)

    def finish(d, p, value):
        for b, v in enumerate(value):
            out[d, (p * chunks + chunk) * blocks + b] = v + local[d, p * blocks + b]

    latest, earlier = filter_forth(count, planes, middle, lower, (zeros, zeros), finish)
    put(carried, latest, 0)
    put(carried, earlier, 1)

    @pl.when(half > 0)
    def _():
        begin = (
            add(tiles_of(carried, 0), tiles_of(received, 0)),
            add(tiles_of(carried, 1), tiles_of(received, 1)),
        )
        filter_forth(count, planes, None, own, begin, finish)


def place_kernel(pieces, out, sem):
    groups, planes = pieces.shape[0], out.shape[0]
    each = pieces.shape[1] // planes
    for i in range(groups):
        for p in range(planes):
            pltpu.make_async_copy(
                pieces.at[i, pl.ds(p * each, each)], out.at[p, pl.ds(i * each, each)], sem
            ).start()
    pltpu.make_async_copy(out, out, sem).wait()


def grouped_body(probe_fields, root_one, root_two, lateral_kernel_taps, dilations):
    _, planes, rows, columns = probe_fields.shape
    places = lax.axis_size("gz")
    groups = places // 2
    tiles, blocks, count = rows // SUB, columns // LANES, groups * planes
    chunks = tiles // groups
    members = [list(range(groups)), list(range(groups, places))]
    scalars = [dilations, lateral_kernel_taps]

    def across(array, axis, m):
        return lax.ppermute(array, axis, [(i, i ^ m) for i in range(lax.axis_size(axis))])

    def exchange(array):
        return lax.all_to_all(
            array, "gz", split_axis=0, concat_axis=0, axis_index_groups=members, tiled=True
        )

    field = probe_fields.reshape(planes, tiles, SUB, blocks, LANES).transpose(0, 1, 3, 2, 4)
    tile, halo = (SUB, LANES), 2 * MARGIN // SUB
    hbm, vmem = pl.BlockSpec(memory_space=pltpu.HBM), pl.BlockSpec(memory_space=pltpu.VMEM)
    matrix = [pltpu.VMEM((rows, rows), jnp.bfloat16)] * 2
    edge_matrix = [pltpu.VMEM((2 * MARGIN, 2 * MARGIN), jnp.bfloat16)] * 2
    inputs = (field, root_one, root_two, dilations, lateral_kernel_taps)
    field, edge, roots, *matrices = pl.pallas_call(
        load_kernel,
        out_shape=[
            pltpu.VMEM((planes, tiles, blocks, *tile), jnp.float32),
            pltpu.VMEM((planes, halo, blocks, *tile), jnp.float32),
            pltpu.VMEM((2 * planes, *tile), jnp.float32),
            *matrix,
            *edge_matrix,
        ],
        in_specs=[hbm] * len(inputs),
        out_specs=[vmem] * 7,
        scratch_shapes=[
            pltpu.VMEM((planes, columns), jnp.float32),
            pltpu.VMEM((planes, columns), jnp.float32),
            pltpu.SMEM(dilations.shape, jnp.int32),
            pltpu.SMEM(lateral_kernel_taps.shape, jnp.float32),
            pltpu.SemaphoreType.DMA((5 + planes,)),
        ],
        compiler_params=pltpu.CompilerParams(vmem_limit_bytes=24 << 20),
    )(*[pltpu.with_memory_space_constraint(a, pltpu.HBM) for a in inputs])
    edge = across(edge, "gy", 1)
    other_roots = across(roots, "gz", groups)

    body_tiles = chunks * planes * blocks
    piece = (groups, body_tiles + 4 * planes, *tile)
    (pieces,) = call(
        functools.partial(y_inner_kernel, groups),
        [(groups, body_tiles, *tile)],
        [],
        [],
        [*matrices[:2], field],
        1 << 28,
    )
    (pieces,) = call(
        functools.partial(y_outer_kernel, groups, tiles),
        [piece],
        [],
        [],
        [*matrices[2:], edge, roots, other_roots, pieces],
        1 << 20,
    )
    pieces = exchange(pieces)

    width = 2 * LANES
    band = ((columns // width, 2 * width, width), jnp.bfloat16)
    high, low = call(
        functools.partial(band_kernel, columns), [band, band], [], scalars, [], 1 << 30
    )

    shared, scratch = (count, *tile), [(count * SUB, columns + 2 * LANES), (count * SUB, columns)]
    message, local = (2, blocks, *tile), (groups, planes * blocks, *tile)
    parts, coefficients = [], []
    for t in range(chunks):
        results = call(
            functools.partial(local_kernel, groups, planes, chunks, t),
            [local, message] + [shared] * (0 if t else 6),
            scratch,
            [],
            [pieces, high, low, *coefficients],
            1 << 28,
        )
        coefficients = coefficients or results[2:]
        parts.append((*results[:2], across(results[1], "gz", groups)))
    out = []
    for t, part in enumerate(parts):
        out = call(
            functools.partial(join_kernel, groups, planes, chunks, t),
            [(groups, body_tiles, *tile)],
            [message] + scratch,
            [],
            [*part, high, low, *coefficients, *out],
            1 << 28,
        )
    out = pl.pallas_call(
        place_kernel,
        out_shape=pltpu.HBM((planes, tiles * blocks, *tile), jnp.float32),
        in_specs=[vmem],
        out_specs=hbm,
        scratch_shapes=[pltpu.SemaphoreType.DMA],
        compiler_params=pltpu.CompilerParams(vmem_limit_bytes=24 << 20),
    )(pltpu.with_memory_space_constraint(exchange(out[0]), pltpu.VMEM))
    out = out.reshape(planes, tiles, blocks, *tile).transpose(0, 1, 3, 2, 4)
    return out.reshape(probe_fields.shape)


def body(*arrays):
    probes, planes, rows, columns = arrays[0].shape
    places, row_places = lax.axis_size("gz"), lax.axis_size("gy")
    fits = (
        probes == 1
        and row_places == 2
        and places >= 4
        and places & (places - 1) == 0
        and rows % (SUB * (places // 2)) == 0
        and rows >= 4 * MARGIN
        and columns == SUB * LANES
        and planes * places >= 4
    )
    return grouped_body(*arrays) if fits else plain_body(*arrays)


def solution(mesh):
    placed = (P(None, "gz", "gy", None), P("gz", None), P("gz", None), P(), P())
    return jax.shard_map(
        body, mesh=mesh, in_specs=placed, out_specs=P(None, "gz", "gy", None), check_vma=False
    )
```

```python
import functools

import jax
import jax.numpy as jnp
from jax import lax
from jax.experimental import pallas as pl
from jax.experimental.pallas import tpu as pltpu
from jax.sharding import PartitionSpec as P

RADIUS = 2
DMAX = 8
MARGIN = RADIUS * DMAX
LANES = 128
SUB = 8


def padded_y(array, width):
    size, length = lax.axis_size("gy"), array.shape[2]
    up = [(i, (i + 1) % size) for i in range(size - 1)]
    down = [(j, i) for i, j in up]
    last = lax.slice_in_dim(array, length - width, length, axis=2)
    leading = lax.slice_in_dim(array, 0, width, axis=2)
    before = lax.ppermute(last, "gy", up)
    after = lax.ppermute(leading, "gy", down)
    return jnp.concatenate([before, array, after], axis=2)


def filter_coefficients(root_one, root_two):
    first = root_one + root_two
    second = -root_one * root_two
    gain = (1.0 - root_one) * (1.0 - root_two)
    return (first, second, gain)


def depth_scan(fields, first, second, pre_gain, post_gain, reverse):
    moved = jnp.moveaxis(fields, 1, 0)
    zero = jnp.zeros(moved.shape[1:], jnp.float32)

    def advance(carry, inputs):
        latest, earlier = carry
        plane, coef_one, coef_two, before, after = inputs
        value = before * plane + coef_one * latest + coef_two * earlier
        return ((value, latest), after * value)

    _, outputs = lax.scan(
        advance, (zero, zero), (moved, first, second, pre_gain, post_gain), reverse=reverse
    )
    return jnp.moveaxis(outputs, 0, 1)


def normalised(weights):
    return weights / (weights[..., :1] + 2.0 * jnp.sum(weights[..., 1:], -1, keepdims=True))


def lateral_padded(padded, scaled, dilation, axis, margin, length):
    result = scaled[0] * lax.dynamic_slice_in_dim(padded, margin, length, axis)
    for offset_tap in range(1, scaled.shape[0]):
        offset = dilation * offset_tap
        upper = lax.dynamic_slice_in_dim(padded, margin + offset, length, axis)
        lower = lax.dynamic_slice_in_dim(padded, margin - offset, length, axis)
        result = result + scaled[offset_tap] * (upper + lower)
    return result


def lateral_x(fields, scaled, dilation):
    padded = jnp.pad(fields, ((0, 0), (0, 0), (0, 0), (MARGIN, MARGIN)))
    return lateral_padded(padded, scaled, dilation, 3, MARGIN, fields.shape[3])


def lateral_y_twice(fields, scaled, dilation):
    rows = fields.shape[2]
    padded = padded_y(fields, 2 * MARGIN)
    middle = lateral_padded(padded, scaled, dilation, 2, MARGIN, rows + 2 * MARGIN)
    global_row = lax.axis_index("gy") * rows - MARGIN + jnp.arange(rows + 2 * MARGIN)
    inside = (global_row >= 0) & (global_row < rows * lax.axis_size("gy"))
    middle = jnp.where(inside[None, None, :, None], middle, 0.0)
    return lateral_padded(middle, scaled, dilation, 2, MARGIN, rows)


def plain_body(probe_fields, root_one, root_two, lateral_kernel_taps, dilations):
    roots = lax.all_gather(jnp.stack([root_one, root_two], 1), "gz", axis=0, tiled=True)
    first, second, gain = filter_coefficients(roots[:, 0], roots[:, 1])
    unity = jnp.ones_like(gain)
    first_next = jnp.concatenate([first[1:], jnp.zeros_like(first[:1])], 0)
    second_next = jnp.concatenate([second[2:], jnp.zeros_like(second[:2])], 0)
    scaled = normalised(lateral_kernel_taps)
    field = lateral_y_twice(probe_fields, scaled[1], dilations[1])
    field = lax.all_to_all(field, "gz", split_axis=2, concat_axis=1, tiled=True)
    field = depth_scan(field, first_next, second_next, unity, gain, True)
    field = lateral_x(field, scaled[0], dilations[0])
    field = lateral_x(field, scaled[0], dilations[0])
    field = depth_scan(field, first, second, gain, unity, False)
    return lax.all_to_all(field, "gz", split_axis=1, concat_axis=2, tiled=True)


NO_COST = pl.CostEstimate(flops=0, bytes_accessed=0, transcendentals=0)


def call(kernel, outs, scratch, arrays):
    arrays = [pltpu.with_memory_space_constraint(a, pltpu.VMEM) for a in arrays]
    outs, scratch = (
        [item if len(item) == 2 and isinstance(item[0], tuple) else (item, jnp.float32) for item in items]
        for items in (outs, scratch)
    )
    return pl.pallas_call(
        kernel,
        out_shape=[pltpu.VMEM(shape, dtype) for shape, dtype in outs],
        in_specs=[pl.BlockSpec(memory_space=pltpu.VMEM)] * len(arrays),
        out_specs=[pl.BlockSpec(memory_space=pltpu.VMEM)] * len(outs),
        scratch_shapes=[pltpu.VMEM(shape, dtype) for shape, dtype in scratch],
        compiler_params=pltpu.CompilerParams(vmem_limit_bytes=24 << 20),
        cost_estimate=NO_COST,
    )(*arrays)


def tap_vectors(taps, axis, shape):
    raw = [taps[axis, i] for i in range(RADIUS + 1)]
    total = raw[0] + 2.0 * functools.reduce(lambda a, b: a + b, raw[1:])
    scale = 1.0 / jnp.full(shape, total, jnp.float32)
    return [jnp.full(shape, tap, jnp.float32) * scale for tap in raw]


def split(value):
    high = value.astype(jnp.bfloat16)
    return high, (value - high.astype(jnp.float32)).astype(jnp.bfloat16)


def product(left, right):
    dot = functools.partial(jnp.dot, preferred_element_type=jnp.float32)
    return dot(left[0], right[0]) + (dot(left[0], right[1]) + dot(left[1], right[0]))


OFFSETS = range(-RADIUS, RADIUS + 1)


def double_taps(at, length, step, taps):
    sums = {}
    for a in OFFSETS:
        middle = at + a * step
        tap = jnp.where((middle >= 0) & (middle < length), taps[abs(a)], 0.0)
        for b in OFFSETS:
            sums[a + b] = sums.get(a + b, 0.0) + tap * taps[abs(b)]
    return sums


def fill_band(high, low, row_places, step, taps, begin, from_begin):
    part = 2 * SUB
    for i in range(0, high.shape[0], part):
        shape = (part, high.shape[1])
        at = lax.broadcasted_iota(jnp.int32, shape, 0) + (begin + i)
        apart = lax.broadcasted_iota(jnp.int32, shape, 1) + from_begin - at
        value = jnp.zeros(shape, jnp.float32)
        for o, total in double_taps(at, row_places, step, taps).items():
            value = jnp.where(apart == o * step, total, value)
        high[i : i + part], low[i : i + part] = split(value)


def edge_kernel(x_ref, one_ref, two_ref, edge, roots, rows, sems):
    depth = edge.shape[1]
    start = jnp.where(lax.axis_index("gy") == 0, x_ref.shape[1] - depth, 0)
    copies = [
        pltpu.make_async_copy(one_ref, rows.at[0], sems.at[0]),
        pltpu.make_async_copy(two_ref, rows.at[1], sems.at[1]),
        pltpu.make_async_copy(x_ref.at[:, pl.ds(start, depth)], edge, sems.at[2]),
    ]
    for copy in copies:
        copy.start()
    copies[0].wait()
    copies[1].wait()
    planes, blocks = rows.shape[1], rows.shape[2] // LANES
    for i in range(2):
        for p in range(planes):
            for b in range(blocks):
                lanes = slice(b * LANES, (b + 1) * LANES)
                roots[i * planes + p, b : b + 1] = rows[i, p : p + 1, lanes]
    copies[2].wait()


def load_kernel(
    x_ref, dilations_ref, taps_ref, _,
    whole, high, low, edge_high, edge_low, x_step, x_taps, dilations, taps, sems,
):
    row_at, row_places = lax.axis_index("gy"), lax.axis_size("gy")
    planes, tiles = x_ref.shape[:2]
    rows = tiles * SUB
    copies = [
        pltpu.make_async_copy(dilations_ref, dilations, sems.at[0]),
        pltpu.make_async_copy(taps_ref, taps, sems.at[1]),
    ]
    copies += [
        pltpu.make_async_copy(x_ref.at[p], whole.at[p], sems.at[2 + p]) for p in range(planes)
    ]
    for copy in copies:
        copy.start()
    copies[0].wait()
    copies[1].wait()
    x_step[...] = jnp.full(x_step.shape, dilations[0], jnp.int32)
    for i, tap in enumerate(tap_vectors(taps, 0, (1, LANES))):
        x_taps[i : i + 1] = tap
    step, weights = dilations[1], tap_vectors(taps, 1, (1, 1))
    length, begin = rows * row_places, row_at * rows
    fill_band(high, low, length, step, weights, begin, begin)
    near = begin + jnp.where(row_at == 0, rows - 2 * MARGIN, 0)
    beyond = begin + jnp.where(row_at == 0, rows, -2 * MARGIN)
    fill_band(edge_high, edge_low, length, step, weights, near, beyond)
    for copy in copies[2:]:
        copy.wait()


def columns_of(ref, p, b, width):
    rows = ref.shape[1] * SUB
    return jnp.concatenate([ref[p, :, b + i].reshape(rows, LANES) for i in range(width)], axis=1)


def y_inner_kernel(groups, high, low, x_ref, pieces):
    planes, tiles, blocks = x_ref.shape[:3]
    chunks, width = tiles // groups, 2
    for p in range(planes):
        for b in range(0, blocks, width):
            value = product((high[...], low[...]), split(columns_of(x_ref, p, b, width)))
            for i in range(tiles):
                for w in range(width):
                    tile = value[i * SUB : (i + 1) * SUB, w * LANES : (w + 1) * LANES]
                    pieces[i // chunks, (p * chunks + i % chunks) * blocks + b + w] = tile


def y_outer_kernel(groups, tiles, high, low, edge, given, roots, other_roots, _, pieces):
    planes, halo, blocks = edge.shape[:3]
    chunks, width = tiles // groups, 2
    base = chunks * planes * blocks
    pieces[:, :base] = given[...]
    for i in range(groups):
        pieces[i, base : base + 2 * planes] = roots[...]
        pieces[i, base + 2 * planes :] = other_roots[...]
    first = jnp.where(lax.axis_index("gy") == 0, (tiles - halo) // chunks, 0)
    for p in range(planes):
        for b in range(0, blocks, width):
            value = product((high[...], low[...]), split(columns_of(edge, p, b, width)))
            for i in range(halo):
                for w in range(width):
                    tile = value[i * SUB : (i + 1) * SUB, w * LANES : (w + 1) * LANES]
                    to, at = first + i // chunks, (p * chunks + i % chunks) * blocks
                    pieces[to, at + b + w] = given[to, at + b + w] + tile


def band_kinds(count):
    kinds = sorted({0, min(1, count - 1), count - 1})
    return kinds, [0 if n == 0 else len(kinds) - 1 if n == count - 1 else 1 for n in range(count)]


def band_kernel(columns, x_step, x_taps, high, low):
    depth, width = high.shape[1:]
    step, taps = x_step[0:1], [x_taps[i : i + 1] for i in range(RADIUS + 1)]
    part, reach = 2 * SUB, 2 * MARGIN
    lane = lax.broadcasted_iota(jnp.int32, (part, LANES), 1)
    row = lax.broadcasted_iota(jnp.int32, (part, LANES), 0)
    high[...] = jnp.zeros(high.shape, high.dtype)
    low[...] = jnp.zeros(low.shape, low.dtype)
    for kind, n in enumerate(band_kinds(columns // width)[0]):
        for w in range(0, width, LANES):
            at = lax.broadcasted_iota(jnp.int32, (1, LANES), 1) + (n * width + w)
            sums = double_taps(at, columns, step, taps)
            lanes = slice(w, w + LANES)

            def rows_at(i, _):
                start = w + LANES - reach + i * part
                apart = row + (start - LANES - w) - lane
                value = jnp.zeros((part, LANES), jnp.float32)
                for o, total in sums.items():
                    value = jnp.where(apart == o * step, total, value)
                at_rows = pl.ds(pl.multiple_of(start, part), part)
                high[kind, at_rows, lanes], low[kind, at_rows, lanes] = split(value)
                return 0

            lax.fori_loop(0, (LANES + 2 * reach) // part, rows_at, 0, unroll=2)


def x_twice(source, result, high, low, parts):
    rows, (depth, width) = source.shape[0], high.shape[1:]
    parts[:rows], parts[rows:] = split(source[...])
    dot = functools.partial(jnp.dot, preferred_element_type=jnp.float32)
    for n, kind in enumerate(band_kinds(result.shape[1] // width)[1]):
        lanes = slice(n * width, n * width + depth)
        total = dot(parts[:, lanes], high[kind])
        total = total[:rows] + (total[rows:] + dot(parts[:rows, lanes], low[kind]))
        result[:, n * width : (n + 1) * width] = total


def add(a, b):
    return [x + y for x, y in zip(a, b)]


def times(ref, k, values):
    return [ref[k, b : b + 1] * value for b, value in enumerate(values)]


def tiles_of(ref, *at):
    return [ref[(*at, b)] for b in range(ref.shape[len(at)])]


def put(ref, values, *at):
    for b, value in enumerate(values):
        ref[(*at, b)] = value


def clear_sides(field):
    columns = field.shape[1] - 2 * LANES
    none = jnp.zeros((field.shape[0], LANES), jnp.float32)
    field[:, :LANES] = none
    field[:, LANES + columns :] = none


def row_tile(k):
    return pl.ds(pl.multiple_of(k * SUB, SUB), SUB)


def filter_back(count, planes, source, coefficients, field, start):
    first, second, gain = coefficients
    after, beyond = start

    def at(d, carry):
        for p in reversed(range(planes)):
            ahead, pending = carry
            k = d * planes + p
            value = ahead if source is None else add(source(d, p), ahead)
            for b, scaled in enumerate(times(gain, k, value)):
                field[row_tile(k), (b + 1) * LANES : (b + 2) * LANES] = scaled
            carry = (add(times(first, k, value), pending), times(second, k, value))
        return carry

    steps = count // planes
    return lax.fori_loop(0, steps, lambda i, c: at(steps - 1 - i, c), (after, beyond))


def filter_forth(count, planes, field, coefficients, start, finish):
    first, second, gain = coefficients

    def at(d, carry):
        for p in range(planes):
            latest, earlier = carry
            k = d * planes + p
            value = add(times(first, k, latest), times(second, k, earlier))
            if field is not None:
                blocks = len(value)
                there = [
                    field[row_tile(k), b * LANES : (b + 1) * LANES] for b in range(blocks)
                ]
                value = add(value, times(gain, k, there))
            finish(d, p, value)
            carry = (value, latest)
        return carry

    return lax.fori_loop(0, count // planes, at, start)


def store_coefficients(k, one, two, first, second, gain):
    first[k] = one + two
    second[k] = -one * two
    gain[k] = (1.0 - one) * (1.0 - two)


def local_kernel(groups, planes, chunks, chunk, *refs):
    if chunk == 0:
        pieces, high, low, local, message, *coefficients, field, middle, halves = refs
    else:
        pieces, high, low, *coefficients, local, message, field, middle, halves = refs
    half = lax.axis_index("gz") // groups
    blocks = message.shape[1]
    count = groups * planes
    own = coefficients[:3]
    if chunk == 0:
        base = chunks * planes * blocks
        for d in range(groups):
            for p in range(planes):
                k = d * planes + p
                one, two = (pieces[d, base + i * planes + p] for i in range(2))
                store_coefficients(k, one, two, *own)
                other_one, other_two = (pieces[d, base + (2 + i) * planes + p] for i in range(2))
                one = jnp.where(half == 0, one, other_one)
                two = jnp.where(half == 0, two, other_two)
                store_coefficients(k, one, two, *coefficients[3:])
    clear_sides(field)
    zeros = [field[0:SUB, 0:LANES]] * blocks

    def source(d, p):
        return [pieces[d, (p * chunks + chunk) * blocks + b] for b in range(blocks)]

    ahead, pending = filter_back(count, planes, source, own, field, (zeros, zeros))
    x_twice(field, middle, high, low, halves)

    def finish(d, p, value):
        for b, v in enumerate(value):
            local[d, p * blocks + b] = v

    latest, earlier = filter_forth(count, planes, middle, own, (zeros, zeros), finish)
    for b in range(blocks):
        message[0, b] = jnp.where(half > 0, ahead[b], latest[b])
        message[1, b] = jnp.where(half > 0, pending[b], earlier[b])


def join_kernel(groups, planes, chunks, chunk, local, sent, received, high, low, *refs):
    own, lower, before = refs[:3], refs[3:6], refs[6:-5]
    out, carried, field, middle, halves = refs[-5:]
    half = lax.axis_index("gz") // groups
    blocks = sent.shape[1]
    count = groups * planes
    for ref in before:
        out[...] = ref[...]
    for i in range(2):
        for b in range(blocks):
            carried[i, b] = jnp.where(half == 0, received[i, b], sent[i, b])
    clear_sides(field)
    zeros = [field[0:SUB, 0:LANES]] * blocks
    start = (tiles_of(carried, 0), tiles_of(carried, 1))
    filter_back(count, planes, None, lower, field, start)
    x_twice(field, middle, high, low, halves)

    def finish(d, p, value):
        for b, v in enumerate(value):
            out[d, (p * chunks + chunk) * blocks + b] = v + local[d, p * blocks + b]

    latest, earlier = filter_forth(count, planes, middle, lower, (zeros, zeros), finish)
    put(carried, latest, 0)
    put(carried, earlier, 1)

    @pl.when(half > 0)
    def _():
        begin = (
            add(tiles_of(carried, 0), tiles_of(received, 0)),
            add(tiles_of(carried, 1), tiles_of(received, 1)),
        )
        filter_forth(count, planes, None, own, begin, finish)


def place_kernel(pieces, out, sem):
    groups, planes = pieces.shape[0], out.shape[0]
    each = pieces.shape[1] // planes
    for i in range(groups):
        for p in range(planes):
            pltpu.make_async_copy(
                pieces.at[i, pl.ds(p * each, each)], out.at[p, pl.ds(i * each, each)], sem
            ).start()
    pltpu.make_async_copy(out, out, sem).wait()


def grouped_body(probe_fields, root_one, root_two, lateral_kernel_taps, dilations):
    _, planes, rows, columns = probe_fields.shape
    places = lax.axis_size("gz")
    groups = places // 2
    tiles, blocks, count = rows // SUB, columns // LANES, groups * planes
    chunks = tiles // groups
    members = [list(range(groups)), list(range(groups, places))]

    def across(array, axis, m):
        return lax.ppermute(array, axis, [(i, i ^ m) for i in range(lax.axis_size(axis))])

    def exchange(array):
        return lax.all_to_all(
            array, "gz", split_axis=0, concat_axis=0, axis_index_groups=members, tiled=True
        )

    field = probe_fields.reshape(planes, tiles, SUB, blocks, LANES).transpose(0, 1, 3, 2, 4)
    tile, halo = (SUB, LANES), 2 * MARGIN // SUB
    hbm, vmem = pl.BlockSpec(memory_space=pltpu.HBM), pl.BlockSpec(memory_space=pltpu.VMEM)
    matrix = [pltpu.VMEM((rows, rows), jnp.bfloat16)] * 2
    edge_matrix = [pltpu.VMEM((2 * MARGIN, 2 * MARGIN), jnp.bfloat16)] * 2
    params = pltpu.CompilerParams(vmem_limit_bytes=24 << 20)

    def in_hbm(*arrays):
        return [pltpu.with_memory_space_constraint(array, pltpu.HBM) for array in arrays]

    edge, roots = pl.pallas_call(
        edge_kernel,
        out_shape=[
            pltpu.VMEM((planes, halo, blocks, *tile), jnp.float32),
            pltpu.VMEM((2 * planes, *tile), jnp.float32),
        ],
        in_specs=[hbm] * 3,
        out_specs=[vmem] * 2,
        scratch_shapes=[
            pltpu.VMEM((2, planes, columns), jnp.float32),
            pltpu.SemaphoreType.DMA((3,)),
        ],
        compiler_params=params,
        cost_estimate=NO_COST,
    )(*in_hbm(field, root_one, root_two))
    field, *matrices, x_step, x_taps = pl.pallas_call(
        load_kernel,
        out_shape=[
            pltpu.VMEM((planes, tiles, blocks, *tile), jnp.float32),
            *matrix,
            *edge_matrix,
            pltpu.VMEM(tile, jnp.int32),
            pltpu.VMEM(tile, jnp.float32),
        ],
        in_specs=[hbm] * 3 + [vmem],
        out_specs=[vmem] * 7,
        scratch_shapes=[
            pltpu.SMEM(dilations.shape, jnp.int32),
            pltpu.SMEM(lateral_kernel_taps.shape, jnp.float32),
            pltpu.SemaphoreType.DMA((2 + planes,)),
        ],
        compiler_params=params,
        cost_estimate=NO_COST,
    )(
        *in_hbm(field, dilations, lateral_kernel_taps),
        pltpu.with_memory_space_constraint(roots, pltpu.VMEM),
    )
    other_roots = across(roots, "gz", groups)
    edge = across(edge, "gy", 1)

    width = 2 * LANES

    band = ((len(band_kinds(columns // width)[0]), 2 * width, width), jnp.bfloat16)
    high, low = call(
        functools.partial(band_kernel, columns), [band, band], [], [x_step, x_taps]
    )
    body_tiles = chunks * planes * blocks
    piece = (groups, body_tiles + 4 * planes, *tile)
    (pieces,) = call(
        functools.partial(y_inner_kernel, groups),
        [(groups, body_tiles, *tile)],
        [],
        [*matrices[:2], field],
    )
    (pieces,) = call(
        functools.partial(y_outer_kernel, groups, tiles),
        [piece],
        [],
        [*matrices[2:], edge, pieces, roots, other_roots, low],
    )
    pieces = exchange(pieces)

    all_rows, wide = count * SUB, columns + 2 * LANES
    shared = (count, *tile)
    scratch = [(all_rows, wide), (all_rows, columns), ((2 * all_rows, wide), jnp.bfloat16)]
    message, local = (2, blocks, *tile), (groups, planes * blocks, *tile)
    parts, coefficients = [], []
    for t in range(chunks):
        results = call(
            functools.partial(local_kernel, groups, planes, chunks, t),
            [local, message] + [shared] * (0 if t else 6),
            scratch,
            [pieces, high, low, *coefficients],
        )
        coefficients = coefficients or results[2:]
        parts.append((*results[:2], across(results[1], "gz", groups)))
    out = []
    for t, part in enumerate(parts):
        out = call(
            functools.partial(join_kernel, groups, planes, chunks, t),
            [(groups, body_tiles, *tile)],
            [message] + scratch,
            [*part, high, low, *coefficients, *out],
        )
    out = pl.pallas_call(
        place_kernel,
        out_shape=pltpu.HBM((planes, tiles * blocks, *tile), jnp.float32),
        in_specs=[vmem],
        out_specs=hbm,
        scratch_shapes=[pltpu.SemaphoreType.DMA],
        compiler_params=params,
    )(pltpu.with_memory_space_constraint(exchange(out[0]), pltpu.VMEM))
    out = out.reshape(planes, tiles, blocks, *tile).transpose(0, 1, 3, 2, 4)
    return out.reshape(probe_fields.shape)


def body(*arrays):
    probes, planes, rows, columns = arrays[0].shape
    places, row_places = lax.axis_size("gz"), lax.axis_size("gy")
    fits = (
        probes == 1
        and row_places == 2
        and places >= 4
        and places & (places - 1) == 0
        and rows % (SUB * (places // 2)) == 0
        and rows >= 4 * MARGIN
        and columns == SUB * LANES
        and planes * places >= 4
    )
    return grouped_body(*arrays) if fits else plain_body(*arrays)


def solution(mesh):
    placed = (P(None, "gz", "gy", None), P("gz", None), P("gz", None), P(), P())
    return jax.shard_map(
        body, mesh=mesh, in_specs=placed, out_specs=P(None, "gz", "gy", None), check_vma=False
    )
```

```python
import functools

import jax
import jax.numpy as jnp
from jax import lax
from jax.experimental import pallas as pl
from jax.experimental.pallas import tpu as pltpu
from jax.sharding import PartitionSpec as P

RADIUS = 2
DMAX = 8
MARGIN = RADIUS * DMAX
LANES = 128
SUB = 8


def padded_y(array, width):
    size, length = lax.axis_size("gy"), array.shape[2]
    up = [(i, (i + 1) % size) for i in range(size - 1)]
    down = [(j, i) for i, j in up]
    last = lax.slice_in_dim(array, length - width, length, axis=2)
    leading = lax.slice_in_dim(array, 0, width, axis=2)
    before = lax.ppermute(last, "gy", up)
    after = lax.ppermute(leading, "gy", down)
    return jnp.concatenate([before, array, after], axis=2)


def filter_coefficients(root_one, root_two):
    first = root_one + root_two
    second = -root_one * root_two
    gain = (1.0 - root_one) * (1.0 - root_two)
    return (first, second, gain)


def depth_scan(fields, first, second, pre_gain, post_gain, reverse):
    moved = jnp.moveaxis(fields, 1, 0)
    zero = jnp.zeros(moved.shape[1:], jnp.float32)

    def advance(carry, inputs):
        latest, earlier = carry
        plane, coef_one, coef_two, before, after = inputs
        value = before * plane + coef_one * latest + coef_two * earlier
        return ((value, latest), after * value)

    _, outputs = lax.scan(
        advance, (zero, zero), (moved, first, second, pre_gain, post_gain), reverse=reverse
    )
    return jnp.moveaxis(outputs, 0, 1)


def normalised(weights):
    return weights / (weights[..., :1] + 2.0 * jnp.sum(weights[..., 1:], -1, keepdims=True))


def lateral_padded(padded, scaled, dilation, axis, margin, length):
    result = scaled[0] * lax.dynamic_slice_in_dim(padded, margin, length, axis)
    for offset_tap in range(1, scaled.shape[0]):
        offset = dilation * offset_tap
        upper = lax.dynamic_slice_in_dim(padded, margin + offset, length, axis)
        lower = lax.dynamic_slice_in_dim(padded, margin - offset, length, axis)
        result = result + scaled[offset_tap] * (upper + lower)
    return result


def lateral_x(fields, scaled, dilation):
    padded = jnp.pad(fields, ((0, 0), (0, 0), (0, 0), (MARGIN, MARGIN)))
    return lateral_padded(padded, scaled, dilation, 3, MARGIN, fields.shape[3])


def lateral_y_twice(fields, scaled, dilation):
    rows = fields.shape[2]
    padded = padded_y(fields, 2 * MARGIN)
    middle = lateral_padded(padded, scaled, dilation, 2, MARGIN, rows + 2 * MARGIN)
    global_row = lax.axis_index("gy") * rows - MARGIN + jnp.arange(rows + 2 * MARGIN)
    inside = (global_row >= 0) & (global_row < rows * lax.axis_size("gy"))
    middle = jnp.where(inside[None, None, :, None], middle, 0.0)
    return lateral_padded(middle, scaled, dilation, 2, MARGIN, rows)


def plain_body(probe_fields, root_one, root_two, lateral_kernel_taps, dilations):
    roots = lax.all_gather(jnp.stack([root_one, root_two], 1), "gz", axis=0, tiled=True)
    first, second, gain = filter_coefficients(roots[:, 0], roots[:, 1])
    unity = jnp.ones_like(gain)
    first_next = jnp.concatenate([first[1:], jnp.zeros_like(first[:1])], 0)
    second_next = jnp.concatenate([second[2:], jnp.zeros_like(second[:2])], 0)
    scaled = normalised(lateral_kernel_taps)
    field = lateral_y_twice(probe_fields, scaled[1], dilations[1])
    field = lax.all_to_all(field, "gz", split_axis=2, concat_axis=1, tiled=True)
    field = depth_scan(field, first_next, second_next, unity, gain, True)
    field = lateral_x(field, scaled[0], dilations[0])
    field = lateral_x(field, scaled[0], dilations[0])
    field = depth_scan(field, first, second, gain, unity, False)
    return lax.all_to_all(field, "gz", split_axis=1, concat_axis=2, tiled=True)


NO_COST = pl.CostEstimate(flops=0, bytes_accessed=0, transcendentals=0)


def call(kernel, outs, scratch, arrays):
    arrays = [pltpu.with_memory_space_constraint(a, pltpu.VMEM) for a in arrays]
    outs, scratch = (
        [item if len(item) == 2 and isinstance(item[0], tuple) else (item, jnp.float32) for item in items]
        for items in (outs, scratch)
    )
    return pl.pallas_call(
        kernel,
        out_shape=[pltpu.VMEM(shape, dtype) for shape, dtype in outs],
        in_specs=[pl.BlockSpec(memory_space=pltpu.VMEM)] * len(arrays),
        out_specs=[pl.BlockSpec(memory_space=pltpu.VMEM)] * len(outs),
        scratch_shapes=[pltpu.VMEM(shape, dtype) for shape, dtype in scratch],
        compiler_params=pltpu.CompilerParams(vmem_limit_bytes=24 << 20),
        cost_estimate=NO_COST,
    )(*arrays)


def tap_vectors(taps, axis, shape):
    raw = [taps[axis, i] for i in range(RADIUS + 1)]
    total = raw[0] + 2.0 * functools.reduce(lambda a, b: a + b, raw[1:])
    scale = 1.0 / jnp.full(shape, total, jnp.float32)
    return [jnp.full(shape, tap, jnp.float32) * scale for tap in raw]


def split(value):
    high = value.astype(jnp.bfloat16)
    return high, (value - high.astype(jnp.float32)).astype(jnp.bfloat16)


def product(left, right):
    dot = functools.partial(jnp.dot, preferred_element_type=jnp.float32)
    return dot(left[0], right[0]) + (dot(left[0], right[1]) + dot(left[1], right[0]))


OFFSETS = range(-RADIUS, RADIUS + 1)


def double_taps(at, length, step, taps):
    sums = {}
    for a in OFFSETS:
        middle = at + a * step
        tap = jnp.where((middle >= 0) & (middle < length), taps[abs(a)], 0.0)
        for b in OFFSETS:
            sums[a + b] = sums.get(a + b, 0.0) + tap * taps[abs(b)]
    return sums


def fill_band(high, low, row_places, step, taps, begin, from_begin):
    part = 2 * SUB
    for i in range(0, high.shape[0], part):
        shape = (part, high.shape[1])
        at = lax.broadcasted_iota(jnp.int32, shape, 0) + (begin + i)
        apart = lax.broadcasted_iota(jnp.int32, shape, 1) + from_begin - at
        value = jnp.zeros(shape, jnp.float32)
        for o, total in double_taps(at, row_places, step, taps).items():
            value = jnp.where(apart == o * step, total, value)
        high[i : i + part], low[i : i + part] = split(value)


def edge_kernel(x_ref, one_ref, two_ref, edge, roots, rows, sems):
    depth = edge.shape[1]
    start = jnp.where(lax.axis_index("gy") == 0, x_ref.shape[1] - depth, 0)
    copies = [
        pltpu.make_async_copy(one_ref, rows.at[0], sems.at[0]),
        pltpu.make_async_copy(two_ref, rows.at[1], sems.at[1]),
        pltpu.make_async_copy(x_ref.at[:, pl.ds(start, depth)], edge, sems.at[2]),
    ]
    for copy in copies:
        copy.start()
    copies[0].wait()
    copies[1].wait()
    planes, blocks = rows.shape[1], rows.shape[2] // LANES
    for i in range(2):
        for p in range(planes):
            for b in range(blocks):
                lanes = slice(b * LANES, (b + 1) * LANES)
                roots[i * planes + p, b : b + 1] = rows[i, p : p + 1, lanes]
    copies[2].wait()


def load_kernel(
    x_ref, dilations_ref, taps_ref, _,
    whole, high, low, edge_high, edge_low, x_step, x_taps, dilations, taps, sems,
):
    row_at, row_places = lax.axis_index("gy"), lax.axis_size("gy")
    planes, tiles = x_ref.shape[:2]
    rows = tiles * SUB
    copies = [
        pltpu.make_async_copy(dilations_ref, dilations, sems.at[0]),
        pltpu.make_async_copy(taps_ref, taps, sems.at[1]),
    ]
    copies += [
        pltpu.make_async_copy(x_ref.at[p], whole.at[p], sems.at[2 + p]) for p in range(planes)
    ]
    for copy in copies:
        copy.start()
    copies[0].wait()
    copies[1].wait()
    x_step[...] = jnp.full(x_step.shape, dilations[0], jnp.int32)
    for i, tap in enumerate(tap_vectors(taps, 0, (1, LANES))):
        x_taps[i : i + 1] = tap
    step, weights = dilations[1], tap_vectors(taps, 1, (1, 1))
    length, begin = rows * row_places, row_at * rows
    fill_band(high, low, length, step, weights, begin, begin)
    near = begin + jnp.where(row_at == 0, rows - 2 * MARGIN, 0)
    beyond = begin + jnp.where(row_at == 0, rows, -2 * MARGIN)
    fill_band(edge_high, edge_low, length, step, weights, near, beyond)
    for copy in copies[2:]:
        copy.wait()


def columns_of(ref, p, b, width):
    rows = ref.shape[1] * SUB
    return jnp.concatenate([ref[p, :, b + i].reshape(rows, LANES) for i in range(width)], axis=1)


def y_inner_kernel(groups, high, low, x_ref, pieces):
    planes, tiles, blocks = x_ref.shape[:3]
    chunks, width = tiles // groups, 2
    for p in range(planes):
        for b in range(0, blocks, width):
            value = product((high[...], low[...]), split(columns_of(x_ref, p, b, width)))
            for i in range(tiles):
                for w in range(width):
                    tile = value[i * SUB : (i + 1) * SUB, w * LANES : (w + 1) * LANES]
                    pieces[i // chunks, (p * chunks + i % chunks) * blocks + b + w] = tile


def y_outer_kernel(groups, tiles, high, low, edge, given, roots, other_roots, _, pieces):
    planes, halo, blocks = edge.shape[:3]
    chunks, width = tiles // groups, 2
    base = chunks * planes * blocks
    pieces[:, :base] = given[...]
    for i in range(groups):
        pieces[i, base : base + 2 * planes] = roots[...]
        pieces[i, base + 2 * planes :] = other_roots[...]
    first = jnp.where(lax.axis_index("gy") == 0, (tiles - halo) // chunks, 0)
    for p in range(planes):
        for b in range(0, blocks, width):
            value = product((high[...], low[...]), split(columns_of(edge, p, b, width)))
            for i in range(halo):
                for w in range(width):
                    tile = value[i * SUB : (i + 1) * SUB, w * LANES : (w + 1) * LANES]
                    to, at = first + i // chunks, (p * chunks + i % chunks) * blocks
                    pieces[to, at + b + w] = given[to, at + b + w] + tile


def band_kinds(count):
    kinds = sorted({0, min(1, count - 1), count - 1})
    return kinds, [0 if n == 0 else len(kinds) - 1 if n == count - 1 else 1 for n in range(count)]


def band_kernel(columns, x_step, x_taps, high, low):
    depth, width = high.shape[1:]
    step, taps = x_step[0:1], [x_taps[i : i + 1] for i in range(RADIUS + 1)]
    part, reach = 2 * SUB, 2 * MARGIN
    lane = lax.broadcasted_iota(jnp.int32, (part, LANES), 1)
    row = lax.broadcasted_iota(jnp.int32, (part, LANES), 0)
    high[...] = jnp.zeros(high.shape, high.dtype)
    low[...] = jnp.zeros(low.shape, low.dtype)
    for kind, n in enumerate(band_kinds(columns // width)[0]):
        for w in range(0, width, LANES):
            at = lax.broadcasted_iota(jnp.int32, (1, LANES), 1) + (n * width + w)
            sums = double_taps(at, columns, step, taps)
            lanes = slice(w, w + LANES)

            def rows_at(i, _):
                start = w + LANES - reach + i * part
                apart = row + (start - LANES - w) - lane
                value = jnp.zeros((part, LANES), jnp.float32)
                for o, total in sums.items():
                    value = jnp.where(apart == o * step, total, value)
                at_rows = pl.ds(pl.multiple_of(start, part), part)
                high[kind, at_rows, lanes], low[kind, at_rows, lanes] = split(value)
                return 0

            lax.fori_loop(0, (LANES + 2 * reach) // part, rows_at, 0, unroll=2)


def x_twice(source, result, high, low, parts):
    rows, (depth, width) = source.shape[0], high.shape[1:]
    parts[:rows], parts[rows:] = split(source[...])
    dot = functools.partial(jnp.dot, preferred_element_type=jnp.float32)
    for n, kind in enumerate(band_kinds(result.shape[1] // width)[1]):
        lanes = slice(n * width, n * width + depth)
        total = dot(parts[:, lanes], high[kind])
        total = total[:rows] + (total[rows:] + dot(parts[:rows, lanes], low[kind]))
        result[:, n * width : (n + 1) * width] = total


def add(a, b):
    return [x + y for x, y in zip(a, b)]


def times(ref, k, values):
    return [ref[k, b : b + 1] * value for b, value in enumerate(values)]


def tiles_of(ref, *at):
    return [ref[(*at, b)] for b in range(ref.shape[len(at)])]


def put(ref, values, *at):
    for b, value in enumerate(values):
        ref[(*at, b)] = value


def clear_sides(field):
    columns = field.shape[1] - 2 * LANES
    none = jnp.zeros((field.shape[0], LANES), jnp.float32)
    field[:, :LANES] = none
    field[:, LANES + columns :] = none


def row_tile(k):
    return pl.ds(pl.multiple_of(k * SUB, SUB), SUB)


def filter_back(count, planes, source, coefficients, field, start):
    first, second, gain = coefficients
    after, beyond = start

    def at(d, carry):
        for p in reversed(range(planes)):
            ahead, pending = carry
            k = d * planes + p
            value = ahead if source is None else add(source(d, p), ahead)
            for b, scaled in enumerate(times(gain, k, value)):
                field[row_tile(k), (b + 1) * LANES : (b + 2) * LANES] = scaled
            carry = (add(times(first, k, value), pending), times(second, k, value))
        return carry

    steps = count // planes
    return lax.fori_loop(0, steps, lambda i, c: at(steps - 1 - i, c), (after, beyond))


def filter_forth(count, planes, field, coefficients, start, finish):
    first, second, gain = coefficients

    def at(d, carry):
        for p in range(planes):
            latest, earlier = carry
            k = d * planes + p
            value = add(times(first, k, latest), times(second, k, earlier))
            if field is not None:
                blocks = len(value)
                there = [
                    field[row_tile(k), b * LANES : (b + 1) * LANES] for b in range(blocks)
                ]
                value = add(value, times(gain, k, there))
            finish(d, p, value)
            carry = (value, latest)
        return carry

    return lax.fori_loop(0, count // planes, at, start)


def store_coefficients(k, one, two, first, second, gain):
    first[k] = one + two
    second[k] = -one * two
    gain[k] = (1.0 - one) * (1.0 - two)


def local_kernel(groups, planes, chunks, chunk, *refs):
    if chunk == 0:
        pieces, high, low, local, message, *coefficients, field, middle, halves = refs
    else:
        pieces, high, low, *coefficients, local, message, field, middle, halves = refs
    half = lax.axis_index("gz") // groups
    blocks = message.shape[1]
    count = groups * planes
    own = coefficients[:3]
    if chunk == 0:
        base = chunks * planes * blocks
        for d in range(groups):
            for p in range(planes):
                k = d * planes + p
                one, two = (pieces[d, base + i * planes + p] for i in range(2))
                store_coefficients(k, one, two, *own)
                other_one, other_two = (pieces[d, base + (2 + i) * planes + p] for i in range(2))
                one = jnp.where(half == 0, one, other_one)
                two = jnp.where(half == 0, two, other_two)
                store_coefficients(k, one, two, *coefficients[3:])
    clear_sides(field)
    zeros = [field[0:SUB, 0:LANES]] * blocks

    def source(d, p):
        return [pieces[d, (p * chunks + chunk) * blocks + b] for b in range(blocks)]

    ahead, pending = filter_back(count, planes, source, own, field, (zeros, zeros))
    x_twice(field, middle, high, low, halves)

    def finish(d, p, value):
        for b, v in enumerate(value):
            local[d, p * blocks + b] = v

    latest, earlier = filter_forth(count, planes, middle, own, (zeros, zeros), finish)
    for b in range(blocks):
        message[0, b] = jnp.where(half > 0, ahead[b], latest[b])
        message[1, b] = jnp.where(half > 0, pending[b], earlier[b])


def join_kernel(groups, planes, chunks, chunk, local, sent, received, high, low, *refs):
    own, lower, before = refs[:3], refs[3:6], refs[6:-5]
    out, carried, field, middle, halves = refs[-5:]
    half = lax.axis_index("gz") // groups
    blocks = sent.shape[1]
    count = groups * planes
    for ref in before:
        out[...] = ref[...]
    for i in range(2):
        for b in range(blocks):
            carried[i, b] = jnp.where(half == 0, received[i, b], sent[i, b])
    clear_sides(field)
    zeros = [field[0:SUB, 0:LANES]] * blocks
    start = (tiles_of(carried, 0), tiles_of(carried, 1))
    filter_back(count, planes, None, lower, field, start)
    x_twice(field, middle, high, low, halves)

    def finish(d, p, value):
        for b, v in enumerate(value):
            out[d, (p * chunks + chunk) * blocks + b] = v + local[d, p * blocks + b]

    latest, earlier = filter_forth(count, planes, middle, lower, (zeros, zeros), finish)
    put(carried, latest, 0)
    put(carried, earlier, 1)

    @pl.when(half > 0)
    def _():
        begin = (
            add(tiles_of(carried, 0), tiles_of(received, 0)),
            add(tiles_of(carried, 1), tiles_of(received, 1)),
        )
        filter_forth(count, planes, None, own, begin, finish)


def partner(pair):
    groups = lax.axis_size("gz") // 2
    m = jnp.where(lax.axis_index("gy") == 0, pair[0], pair[1])
    return (lax.axis_index("gz") % groups) ^ m


def split_kernel(pairs, pieces, *outs):
    for pair, out in zip(pairs, outs):
        out[...] = pieces[partner(pair)]


def merge_kernel(pairs, *refs):
    for pair, piece in zip(pairs, refs[:-1]):
        refs[-1][partner(pair)] = piece[...]


def place_kernel(pairs, *refs):
    pieces, (out, sems) = refs[: len(pairs)], refs[-2:]
    planes = out.shape[0]
    each = pieces[0].shape[0] // planes
    for i, (pair, piece) in enumerate(zip(pairs, pieces)):
        at = partner(pair) * each
        for p in range(planes):
            pltpu.make_async_copy(
                piece.at[pl.ds(p * each, each)], out.at[p, pl.ds(at, each)], sems.at[i]
            ).start()
    for i, piece in enumerate(pieces):
        pltpu.make_async_copy(piece, piece, sems.at[i]).wait()


def exchange_order(groups):
    order, last = [], groups - 1
    for m in sorted(range(1, last), key=lambda m: (m.bit_count(), m)):
        if m not in order:
            order += [m, last ^ m]
    return [m for i, m in enumerate(order) if m not in order[:i]] + [last]


def grouped_body(probe_fields, root_one, root_two, lateral_kernel_taps, dilations):
    _, planes, rows, columns = probe_fields.shape
    places = lax.axis_size("gz")
    groups = places // 2
    tiles, blocks, count = rows // SUB, columns // LANES, groups * planes
    chunks = tiles // groups

    def across(array, axis, m):
        return lax.ppermute(array, axis, [(i, i ^ m) for i in range(lax.axis_size(axis))])

    first = exchange_order(groups)
    second = [m ^ (groups - 1) or groups - 1 for m in first]
    pairs = [(0, 0), *zip(first, second)]

    def across_pair(array, pair):
        moves = [
            (2 * i + core, 2 * (i ^ m) + core) for i in range(places) for core, m in enumerate(pair)
        ]
        return lax.ppermute(array, ("gz", "gy"), moves)

    def exchange(array):
        kernel = functools.partial(split_kernel, pairs)
        parts = call(kernel, [array.shape[1:]] * groups, [], [array])
        return [parts[0]] + [across_pair(*part) for part in zip(parts[1:], pairs[1:])]

    field = probe_fields.reshape(planes, tiles, SUB, blocks, LANES).transpose(0, 1, 3, 2, 4)
    tile, halo = (SUB, LANES), 2 * MARGIN // SUB
    hbm, vmem = pl.BlockSpec(memory_space=pltpu.HBM), pl.BlockSpec(memory_space=pltpu.VMEM)
    matrix = [pltpu.VMEM((rows, rows), jnp.bfloat16)] * 2
    edge_matrix = [pltpu.VMEM((2 * MARGIN, 2 * MARGIN), jnp.bfloat16)] * 2
    params = pltpu.CompilerParams(vmem_limit_bytes=24 << 20)

    def in_hbm(*arrays):
        return [pltpu.with_memory_space_constraint(array, pltpu.HBM) for array in arrays]

    edge, roots = pl.pallas_call(
        edge_kernel,
        out_shape=[
            pltpu.VMEM((planes, halo, blocks, *tile), jnp.float32),
            pltpu.VMEM((2 * planes, *tile), jnp.float32),
        ],
        in_specs=[hbm] * 3,
        out_specs=[vmem] * 2,
        scratch_shapes=[
            pltpu.VMEM((2, planes, columns), jnp.float32),
            pltpu.SemaphoreType.DMA((3,)),
        ],
        compiler_params=params,
        cost_estimate=NO_COST,
    )(*in_hbm(field, root_one, root_two))
    field, *matrices, x_step, x_taps = pl.pallas_call(
        load_kernel,
        out_shape=[
            pltpu.VMEM((planes, tiles, blocks, *tile), jnp.float32),
            *matrix,
            *edge_matrix,
            pltpu.VMEM(tile, jnp.int32),
            pltpu.VMEM(tile, jnp.float32),
        ],
        in_specs=[hbm] * 3 + [vmem],
        out_specs=[vmem] * 7,
        scratch_shapes=[
            pltpu.SMEM(dilations.shape, jnp.int32),
            pltpu.SMEM(lateral_kernel_taps.shape, jnp.float32),
            pltpu.SemaphoreType.DMA((2 + planes,)),
        ],
        compiler_params=params,
        cost_estimate=NO_COST,
    )(
        *in_hbm(field, dilations, lateral_kernel_taps),
        pltpu.with_memory_space_constraint(roots, pltpu.VMEM),
    )
    other_roots = across(roots, "gz", groups)
    edge = across(edge, "gy", 1)

    width = 2 * LANES

    band = ((len(band_kinds(columns // width)[0]), 2 * width, width), jnp.bfloat16)
    high, low = call(
        functools.partial(band_kernel, columns), [band, band], [], [x_step, x_taps]
    )
    body_tiles = chunks * planes * blocks
    piece = (groups, body_tiles + 4 * planes, *tile)
    (pieces,) = call(
        functools.partial(y_inner_kernel, groups),
        [(groups, body_tiles, *tile)],
        [],
        [*matrices[:2], field],
    )
    (pieces,) = call(
        functools.partial(y_outer_kernel, groups, tiles),
        [piece],
        [],
        [*matrices[2:], edge, pieces, roots, other_roots, low],
    )
    kernel = functools.partial(merge_kernel, pairs)
    (pieces,) = call(kernel, [piece], [], exchange(pieces))

    all_rows, wide = count * SUB, columns + 2 * LANES
    shared = (count, *tile)
    scratch = [(all_rows, wide), (all_rows, columns), ((2 * all_rows, wide), jnp.bfloat16)]
    message, local = (2, blocks, *tile), (groups, planes * blocks, *tile)
    parts, coefficients = [], []
    for t in range(chunks):
        results = call(
            functools.partial(local_kernel, groups, planes, chunks, t),
            [local, message] + [shared] * (0 if t else 6),
            scratch,
            [pieces, high, low, *coefficients],
        )
        coefficients = coefficients or results[2:]
        parts.append((*results[:2], across(results[1], "gz", groups)))
    out = []
    for t, part in enumerate(parts):
        out = call(
            functools.partial(join_kernel, groups, planes, chunks, t),
            [(groups, body_tiles, *tile)],
            [message] + scratch,
            [*part, high, low, *coefficients, *out],
        )
    pieces = exchange(out[0])
    out, half = [], groups // 2 + 1
    for part in (slice(0, half), slice(half, groups)):
        arrays = [pltpu.with_memory_space_constraint(a, pltpu.VMEM) for a in pieces[part]]
        out = [
            pl.pallas_call(
                functools.partial(place_kernel, pairs[part]),
                out_shape=pltpu.HBM((planes, tiles * blocks, *tile), jnp.float32),
                in_specs=[vmem] * len(arrays) + [hbm] * len(out),
                out_specs=hbm,
                scratch_shapes=[pltpu.SemaphoreType.DMA((len(arrays),))],
                input_output_aliases={len(arrays): 0} if out else {},
                compiler_params=params,
                cost_estimate=NO_COST,
            )(*arrays, *out)
        ]
    (out,) = out
    out = out.reshape(planes, tiles, blocks, *tile).transpose(0, 1, 3, 2, 4)
    return out.reshape(probe_fields.shape)


def body(*arrays):
    probes, planes, rows, columns = arrays[0].shape
    places, row_places = lax.axis_size("gz"), lax.axis_size("gy")
    fits = (
        probes == 1
        and row_places == 2
        and places >= 4
        and places & (places - 1) == 0
        and rows % (SUB * (places // 2)) == 0
        and rows >= 4 * MARGIN
        and columns == SUB * LANES
        and planes * places >= 4
    )
    return grouped_body(*arrays) if fits else plain_body(*arrays)


def solution(mesh):
    placed = (P(None, "gz", "gy", None), P("gz", None), P("gz", None), P(), P())
    return jax.shard_map(
        body, mesh=mesh, in_specs=placed, out_specs=P(None, "gz", "gy", None), check_vma=False
    )
```

```python
import functools

import jax
import jax.numpy as jnp
from jax import lax
from jax.experimental import pallas as pl
from jax.experimental.pallas import tpu as pltpu
from jax.sharding import PartitionSpec as P

RADIUS = 2
DMAX = 8
MARGIN = RADIUS * DMAX
LANES = 128
SUB = 8


def padded_y(array, width):
    size, length = lax.axis_size("gy"), array.shape[2]
    up = [(i, (i + 1) % size) for i in range(size - 1)]
    down = [(j, i) for i, j in up]
    last = lax.slice_in_dim(array, length - width, length, axis=2)
    leading = lax.slice_in_dim(array, 0, width, axis=2)
    before = lax.ppermute(last, "gy", up)
    after = lax.ppermute(leading, "gy", down)
    return jnp.concatenate([before, array, after], axis=2)


def filter_coefficients(root_one, root_two):
    first = root_one + root_two
    second = -root_one * root_two
    gain = (1.0 - root_one) * (1.0 - root_two)
    return (first, second, gain)


def depth_scan(fields, first, second, pre_gain, post_gain, reverse):
    moved = jnp.moveaxis(fields, 1, 0)
    zero = jnp.zeros(moved.shape[1:], jnp.float32)

    def advance(carry, inputs):
        latest, earlier = carry
        plane, coef_one, coef_two, before, after = inputs
        value = before * plane + coef_one * latest + coef_two * earlier
        return ((value, latest), after * value)

    _, outputs = lax.scan(
        advance, (zero, zero), (moved, first, second, pre_gain, post_gain), reverse=reverse
    )
    return jnp.moveaxis(outputs, 0, 1)


def normalised(weights):
    return weights / (weights[..., :1] + 2.0 * jnp.sum(weights[..., 1:], -1, keepdims=True))


def lateral_padded(padded, scaled, dilation, axis, margin, length):
    result = scaled[0] * lax.dynamic_slice_in_dim(padded, margin, length, axis)
    for offset_tap in range(1, scaled.shape[0]):
        offset = dilation * offset_tap
        upper = lax.dynamic_slice_in_dim(padded, margin + offset, length, axis)
        lower = lax.dynamic_slice_in_dim(padded, margin - offset, length, axis)
        result = result + scaled[offset_tap] * (upper + lower)
    return result


def lateral_x(fields, scaled, dilation):
    padded = jnp.pad(fields, ((0, 0), (0, 0), (0, 0), (MARGIN, MARGIN)))
    return lateral_padded(padded, scaled, dilation, 3, MARGIN, fields.shape[3])


def lateral_y_twice(fields, scaled, dilation):
    rows = fields.shape[2]
    padded = padded_y(fields, 2 * MARGIN)
    middle = lateral_padded(padded, scaled, dilation, 2, MARGIN, rows + 2 * MARGIN)
    global_row = lax.axis_index("gy") * rows - MARGIN + jnp.arange(rows + 2 * MARGIN)
    inside = (global_row >= 0) & (global_row < rows * lax.axis_size("gy"))
    middle = jnp.where(inside[None, None, :, None], middle, 0.0)
    return lateral_padded(middle, scaled, dilation, 2, MARGIN, rows)


def plain_body(probe_fields, root_one, root_two, lateral_kernel_taps, dilations):
    roots = lax.all_gather(jnp.stack([root_one, root_two], 1), "gz", axis=0, tiled=True)
    first, second, gain = filter_coefficients(roots[:, 0], roots[:, 1])
    unity = jnp.ones_like(gain)
    first_next = jnp.concatenate([first[1:], jnp.zeros_like(first[:1])], 0)
    second_next = jnp.concatenate([second[2:], jnp.zeros_like(second[:2])], 0)
    scaled = normalised(lateral_kernel_taps)
    field = lateral_y_twice(probe_fields, scaled[1], dilations[1])
    field = lax.all_to_all(field, "gz", split_axis=2, concat_axis=1, tiled=True)
    field = depth_scan(field, first_next, second_next, unity, gain, True)
    field = lateral_x(field, scaled[0], dilations[0])
    field = lateral_x(field, scaled[0], dilations[0])
    field = depth_scan(field, first, second, gain, unity, False)
    return lax.all_to_all(field, "gz", split_axis=1, concat_axis=2, tiled=True)


NO_COST = pl.CostEstimate(flops=0, bytes_accessed=0, transcendentals=0)


def call(kernel, outs, scratch, arrays):
    arrays = [pltpu.with_memory_space_constraint(a, pltpu.VMEM) for a in arrays]
    outs, scratch = (
        [item if len(item) == 2 and isinstance(item[0], tuple) else (item, jnp.float32) for item in items]
        for items in (outs, scratch)
    )
    return pl.pallas_call(
        kernel,
        out_shape=[pltpu.VMEM(shape, dtype) for shape, dtype in outs],
        in_specs=[pl.BlockSpec(memory_space=pltpu.VMEM)] * len(arrays),
        out_specs=[pl.BlockSpec(memory_space=pltpu.VMEM)] * len(outs),
        scratch_shapes=[pltpu.VMEM(shape, dtype) for shape, dtype in scratch],
        compiler_params=pltpu.CompilerParams(vmem_limit_bytes=24 << 20),
        cost_estimate=NO_COST,
    )(*arrays)


def tap_vectors(taps, axis, shape):
    raw = [taps[axis, i] for i in range(RADIUS + 1)]
    total = raw[0] + 2.0 * functools.reduce(lambda a, b: a + b, raw[1:])
    scale = 1.0 / jnp.full(shape, total, jnp.float32)
    return [jnp.full(shape, tap, jnp.float32) * scale for tap in raw]


def split(value):
    high = value.astype(jnp.bfloat16)
    return high, (value - high.astype(jnp.float32)).astype(jnp.bfloat16)


def product(left, right):
    dot = functools.partial(jnp.dot, preferred_element_type=jnp.float32)
    return dot(left[0], right[0]) + (dot(left[0], right[1]) + dot(left[1], right[0]))


OFFSETS = range(-RADIUS, RADIUS + 1)


def double_taps(at, length, step, taps):
    sums = {}
    for a in OFFSETS:
        middle = at + a * step
        tap = jnp.where((middle >= 0) & (middle < length), taps[abs(a)], 0.0)
        for b in OFFSETS:
            sums[a + b] = sums.get(a + b, 0.0) + tap * taps[abs(b)]
    return sums


def fill_band(high, low, row_places, step, taps, begin, from_begin):
    part = 2 * SUB
    for i in range(0, high.shape[0], part):
        shape = (part, high.shape[1])
        at = lax.broadcasted_iota(jnp.int32, shape, 0) + (begin + i)
        apart = lax.broadcasted_iota(jnp.int32, shape, 1) + from_begin - at
        value = jnp.zeros(shape, jnp.float32)
        for o, total in double_taps(at, row_places, step, taps).items():
            value = jnp.where(apart == o * step, total, value)
        high[i : i + part], low[i : i + part] = split(value)


def edge_kernel(x_ref, one_ref, two_ref, edge, roots, rows, sems):
    depth = edge.shape[1]
    start = jnp.where(lax.axis_index("gy") == 0, x_ref.shape[1] - depth, 0)
    copies = [
        pltpu.make_async_copy(one_ref, rows.at[0], sems.at[0]),
        pltpu.make_async_copy(two_ref, rows.at[1], sems.at[1]),
        pltpu.make_async_copy(x_ref.at[:, pl.ds(start, depth)], edge, sems.at[2]),
    ]
    for copy in copies:
        copy.start()
    copies[0].wait()
    copies[1].wait()
    planes, blocks = rows.shape[1], rows.shape[2] // LANES
    for i in range(2):
        for p in range(planes):
            for b in range(blocks):
                lanes = slice(b * LANES, (b + 1) * LANES)
                roots[i * planes + p, b : b + 1] = rows[i, p : p + 1, lanes]
    copies[2].wait()


def load_kernel(
    x_ref, dilations_ref, taps_ref, _,
    whole, high, low, edge_high, edge_low, x_step, x_taps, dilations, taps, sems,
):
    row_at, row_places = lax.axis_index("gy"), lax.axis_size("gy")
    planes, tiles = x_ref.shape[:2]
    rows = tiles * SUB
    copies = [
        pltpu.make_async_copy(dilations_ref, dilations, sems.at[0]),
        pltpu.make_async_copy(taps_ref, taps, sems.at[1]),
    ]
    copies += [
        pltpu.make_async_copy(x_ref.at[p], whole.at[p], sems.at[2 + p]) for p in range(planes)
    ]
    for copy in copies:
        copy.start()
    copies[0].wait()
    copies[1].wait()
    x_step[...] = jnp.full(x_step.shape, dilations[0], jnp.int32)
    for i, tap in enumerate(tap_vectors(taps, 0, (1, LANES))):
        x_taps[i : i + 1] = tap
    step, weights = dilations[1], tap_vectors(taps, 1, (1, 1))
    length, begin = rows * row_places, row_at * rows
    fill_band(high, low, length, step, weights, begin, begin)
    near = begin + jnp.where(row_at == 0, rows - 2 * MARGIN, 0)
    beyond = begin + jnp.where(row_at == 0, rows, -2 * MARGIN)
    fill_band(edge_high, edge_low, length, step, weights, near, beyond)
    for copy in copies[2:]:
        copy.wait()


def columns_of(ref, p, b, width):
    rows = ref.shape[1] * SUB
    return jnp.concatenate([ref[p, :, b + i].reshape(rows, LANES) for i in range(width)], axis=1)


def y_inner_kernel(groups, high, low, x_ref, pieces):
    planes, tiles, blocks = x_ref.shape[:3]
    chunks, width = tiles // groups, 2
    for p in range(planes):
        for b in range(0, blocks, width):
            value = product((high[...], low[...]), split(columns_of(x_ref, p, b, width)))
            for i in range(tiles):
                for w in range(width):
                    tile = value[i * SUB : (i + 1) * SUB, w * LANES : (w + 1) * LANES]
                    pieces[i // chunks, (p * chunks + i % chunks) * blocks + b + w] = tile


def y_outer_kernel(groups, tiles, high, low, edge, given, roots, other_roots, _, pieces):
    planes, halo, blocks = edge.shape[:3]
    chunks, width = tiles // groups, 2
    base = chunks * planes * blocks
    pieces[:, :base] = given[...]
    for i in range(groups):
        pieces[i, base : base + 2 * planes] = roots[...]
        pieces[i, base + 2 * planes :] = other_roots[...]
    first = jnp.where(lax.axis_index("gy") == 0, (tiles - halo) // chunks, 0)
    for p in range(planes):
        for b in range(0, blocks, width):
            value = product((high[...], low[...]), split(columns_of(edge, p, b, width)))
            for i in range(halo):
                for w in range(width):
                    tile = value[i * SUB : (i + 1) * SUB, w * LANES : (w + 1) * LANES]
                    to, at = first + i // chunks, (p * chunks + i % chunks) * blocks
                    pieces[to, at + b + w] = given[to, at + b + w] + tile


def band_kinds(count):
    kinds = sorted({0, min(1, count - 1), count - 1})
    return kinds, [0 if n == 0 else len(kinds) - 1 if n == count - 1 else 1 for n in range(count)]


def band_kernel(columns, x_step, x_taps, high, low):
    depth, width = high.shape[1:]
    step, taps = x_step[0:1], [x_taps[i : i + 1] for i in range(RADIUS + 1)]
    part, reach = 2 * SUB, 2 * MARGIN
    lane = lax.broadcasted_iota(jnp.int32, (part, LANES), 1)
    row = lax.broadcasted_iota(jnp.int32, (part, LANES), 0)
    high[...] = jnp.zeros(high.shape, high.dtype)
    low[...] = jnp.zeros(low.shape, low.dtype)
    for kind, n in enumerate(band_kinds(columns // width)[0]):
        for w in range(0, width, LANES):
            at = lax.broadcasted_iota(jnp.int32, (1, LANES), 1) + (n * width + w)
            sums = double_taps(at, columns, step, taps)
            lanes = slice(w, w + LANES)

            def rows_at(i, _):
                start = w + LANES - reach + i * part
                apart = row + (start - LANES - w) - lane
                value = jnp.zeros((part, LANES), jnp.float32)
                for o, total in sums.items():
                    value = jnp.where(apart == o * step, total, value)
                at_rows = pl.ds(pl.multiple_of(start, part), part)
                high[kind, at_rows, lanes], low[kind, at_rows, lanes] = split(value)
                return 0

            lax.fori_loop(0, (LANES + 2 * reach) // part, rows_at, 0, unroll=2)


def x_twice(source, result, high, low, parts):
    rows, (depth, width) = source.shape[0], high.shape[1:]
    parts[:rows], parts[rows:] = split(source[...])
    dot = functools.partial(jnp.dot, preferred_element_type=jnp.float32)
    for n, kind in enumerate(band_kinds(result.shape[1] // width)[1]):
        lanes = slice(n * width, n * width + depth)
        total = dot(parts[:, lanes], high[kind])
        total = total[:rows] + (total[rows:] + dot(parts[:rows, lanes], low[kind]))
        result[:, n * width : (n + 1) * width] = total


def add(a, b):
    return [x + y for x, y in zip(a, b)]


def times(ref, k, values):
    return [ref[k, b : b + 1] * value for b, value in enumerate(values)]


def tiles_of(ref, *at):
    return [ref[(*at, b)] for b in range(ref.shape[len(at)])]


def put(ref, values, *at):
    for b, value in enumerate(values):
        ref[(*at, b)] = value


def clear_sides(field):
    columns = field.shape[1] - 2 * LANES
    none = jnp.zeros((field.shape[0], LANES), jnp.float32)
    field[:, :LANES] = none
    field[:, LANES + columns :] = none


def row_tile(k):
    return pl.ds(pl.multiple_of(k * SUB, SUB), SUB)


def filter_back(count, planes, source, coefficients, field, start):
    first, second, gain = coefficients
    after, beyond = start

    def at(d, carry):
        for p in reversed(range(planes)):
            ahead, pending = carry
            k = d * planes + p
            value = ahead if source is None else add(source(d, p), ahead)
            for b, scaled in enumerate(times(gain, k, value)):
                field[row_tile(k), (b + 1) * LANES : (b + 2) * LANES] = scaled
            carry = (add(times(first, k, value), pending), times(second, k, value))
        return carry

    steps = count // planes
    return lax.fori_loop(0, steps, lambda i, c: at(steps - 1 - i, c), (after, beyond))


def filter_forth(count, planes, field, coefficients, start, finish):
    first, second, gain = coefficients

    def at(d, carry):
        for p in range(planes):
            latest, earlier = carry
            k = d * planes + p
            value = add(times(first, k, latest), times(second, k, earlier))
            if field is not None:
                blocks = len(value)
                there = [
                    field[row_tile(k), b * LANES : (b + 1) * LANES] for b in range(blocks)
                ]
                value = add(value, times(gain, k, there))
            finish(d, p, value)
            carry = (value, latest)
        return carry

    return lax.fori_loop(0, count // planes, at, start)


def store_coefficients(k, one, two, first, second, gain):
    first[k] = one + two
    second[k] = -one * two
    gain[k] = (1.0 - one) * (1.0 - two)


def local_kernel(groups, planes, chunks, chunk, *refs):
    if chunk == 0:
        pieces, high, low, local, message, *coefficients, field, middle, halves = refs
    else:
        pieces, high, low, *coefficients, local, message, field, middle, halves = refs
    half = lax.axis_index("gz") // groups
    blocks = message.shape[1]
    count = groups * planes
    own = coefficients[:3]
    if chunk == 0:
        base = chunks * planes * blocks
        for d in range(groups):
            for p in range(planes):
                k = d * planes + p
                one, two = (pieces[d, base + i * planes + p] for i in range(2))
                store_coefficients(k, one, two, *own)
                other_one, other_two = (pieces[d, base + (2 + i) * planes + p] for i in range(2))
                one = jnp.where(half == 0, one, other_one)
                two = jnp.where(half == 0, two, other_two)
                store_coefficients(k, one, two, *coefficients[3:])
    clear_sides(field)
    zeros = [field[0:SUB, 0:LANES]] * blocks

    def source(d, p):
        return [pieces[d, (p * chunks + chunk) * blocks + b] for b in range(blocks)]

    ahead, pending = filter_back(count, planes, source, own, field, (zeros, zeros))
    x_twice(field, middle, high, low, halves)

    def finish(d, p, value):
        for b, v in enumerate(value):
            local[d, p * blocks + b] = v

    latest, earlier = filter_forth(count, planes, middle, own, (zeros, zeros), finish)
    for b in range(blocks):
        message[0, b] = jnp.where(half > 0, ahead[b], latest[b])
        message[1, b] = jnp.where(half > 0, pending[b], earlier[b])


def join_kernel(groups, planes, chunks, chunk, local, sent, received, high, low, *refs):
    own, lower, before = refs[:3], refs[3:6], refs[6:-5]
    out, carried, field, middle, halves = refs[-5:]
    half = lax.axis_index("gz") // groups
    blocks = sent.shape[1]
    count = groups * planes
    for ref in before:
        out[...] = ref[...]
    for i in range(2):
        for b in range(blocks):
            carried[i, b] = jnp.where(half == 0, received[i, b], sent[i, b])
    clear_sides(field)
    zeros = [field[0:SUB, 0:LANES]] * blocks
    start = (tiles_of(carried, 0), tiles_of(carried, 1))
    filter_back(count, planes, None, lower, field, start)
    x_twice(field, middle, high, low, halves)

    def finish(d, p, value):
        for b, v in enumerate(value):
            out[d, (p * chunks + chunk) * blocks + b] = v + local[d, p * blocks + b]

    latest, earlier = filter_forth(count, planes, middle, lower, (zeros, zeros), finish)
    put(carried, latest, 0)
    put(carried, earlier, 1)

    @pl.when(half > 0)
    def _():
        begin = (
            add(tiles_of(carried, 0), tiles_of(received, 0)),
            add(tiles_of(carried, 1), tiles_of(received, 1)),
        )
        filter_forth(count, planes, None, own, begin, finish)


def partner(pair):
    groups = lax.axis_size("gz") // 2
    m = jnp.where(lax.axis_index("gy") == 0, pair[0], pair[1])
    return (lax.axis_index("gz") % groups) ^ m


def split_kernel(pairs, pieces, *outs):
    for pair, out in zip(pairs, outs):
        out[...] = pieces[partner(pair)]


def merge_kernel(pairs, *refs):
    for pair, piece in zip(pairs, refs[:-1]):
        refs[-1][partner(pair)] = piece[...]


def place_kernel(pairs, *refs):
    pieces, (out, sems) = refs[: len(pairs)], refs[-2:]
    planes = out.shape[0]
    each = pieces[0].shape[0] // planes
    for i, (pair, piece) in enumerate(zip(pairs, pieces)):
        at = partner(pair) * each
        for p in range(planes):
            pltpu.make_async_copy(
                piece.at[pl.ds(p * each, each)], out.at[p, pl.ds(at, each)], sems.at[i]
            ).start()
    for i, piece in enumerate(pieces):
        pltpu.make_async_copy(piece, piece, sems.at[i]).wait()


def exchange_order(groups):
    order, last = [], groups - 1
    for m in sorted(range(1, last), key=lambda m: (m.bit_count(), m)):
        if m not in order:
            order += [m, last ^ m]
    return [m for i, m in enumerate(order) if m not in order[:i]] + [last]


def grouped_body(probe_fields, root_one, root_two, lateral_kernel_taps, dilations):
    _, planes, rows, columns = probe_fields.shape
    places = lax.axis_size("gz")
    groups = places // 2
    tiles, blocks, count = rows // SUB, columns // LANES, groups * planes
    chunks = tiles // groups

    def across(array, axis, m):
        return lax.ppermute(array, axis, [(i, i ^ m) for i in range(lax.axis_size(axis))])

    first = exchange_order(groups)
    second = [m ^ (groups - 1) or groups - 1 for m in first]
    pairs_in = [(0, 0), *zip(first, second)]
    pairs_out = [(m, m) for m in (0, *first)]

    def across_pair(array, pair):
        moves = [
            (2 * i + core, 2 * (i ^ m) + core) for i in range(places) for core, m in enumerate(pair)
        ]
        return lax.ppermute(array, ("gz", "gy"), moves)

    def exchange(array, pairs):
        kernel = functools.partial(split_kernel, pairs)
        parts = call(kernel, [array.shape[1:]] * groups, [], [array])
        return [parts[0]] + [across_pair(*part) for part in zip(parts[1:], pairs[1:])]

    field = probe_fields.reshape(planes, tiles, SUB, blocks, LANES).transpose(0, 1, 3, 2, 4)
    tile, halo = (SUB, LANES), 2 * MARGIN // SUB
    hbm, vmem = pl.BlockSpec(memory_space=pltpu.HBM), pl.BlockSpec(memory_space=pltpu.VMEM)
    matrix = [pltpu.VMEM((rows, rows), jnp.bfloat16)] * 2
    edge_matrix = [pltpu.VMEM((2 * MARGIN, 2 * MARGIN), jnp.bfloat16)] * 2
    params = pltpu.CompilerParams(vmem_limit_bytes=24 << 20)

    def in_hbm(*arrays):
        return [pltpu.with_memory_space_constraint(array, pltpu.HBM) for array in arrays]

    edge, roots = pl.pallas_call(
        edge_kernel,
        out_shape=[
            pltpu.VMEM((planes, halo, blocks, *tile), jnp.float32),
            pltpu.VMEM((2 * planes, *tile), jnp.float32),
        ],
        in_specs=[hbm] * 3,
        out_specs=[vmem] * 2,
        scratch_shapes=[
            pltpu.VMEM((2, planes, columns), jnp.float32),
            pltpu.SemaphoreType.DMA((3,)),
        ],
        compiler_params=params,
        cost_estimate=NO_COST,
    )(*in_hbm(field, root_one, root_two))
    field, *matrices, x_step, x_taps = pl.pallas_call(
        load_kernel,
        out_shape=[
            pltpu.VMEM((planes, tiles, blocks, *tile), jnp.float32),
            *matrix,
            *edge_matrix,
            pltpu.VMEM(tile, jnp.int32),
            pltpu.VMEM(tile, jnp.float32),
        ],
        in_specs=[hbm] * 3 + [vmem],
        out_specs=[vmem] * 7,
        scratch_shapes=[
            pltpu.SMEM(dilations.shape, jnp.int32),
            pltpu.SMEM(lateral_kernel_taps.shape, jnp.float32),
            pltpu.SemaphoreType.DMA((2 + planes,)),
        ],
        compiler_params=params,
        cost_estimate=NO_COST,
    )(
        *in_hbm(field, dilations, lateral_kernel_taps),
        pltpu.with_memory_space_constraint(roots, pltpu.VMEM),
    )
    other_roots = across(roots, "gz", groups)
    edge = across(edge, "gy", 1)

    width = 2 * LANES

    band = ((len(band_kinds(columns // width)[0]), 2 * width, width), jnp.bfloat16)
    high, low = call(
        functools.partial(band_kernel, columns), [band, band], [], [x_step, x_taps]
    )
    body_tiles = chunks * planes * blocks
    piece = (groups, body_tiles + 4 * planes, *tile)
    (pieces,) = call(
        functools.partial(y_inner_kernel, groups),
        [(groups, body_tiles, *tile)],
        [],
        [*matrices[:2], field],
    )
    (pieces,) = call(
        functools.partial(y_outer_kernel, groups, tiles),
        [piece],
        [],
        [*matrices[2:], edge, pieces, roots, other_roots, low],
    )
    kernel = functools.partial(merge_kernel, pairs_in)
    (pieces,) = call(kernel, [piece], [], exchange(pieces, pairs_in))

    all_rows, wide = count * SUB, columns + 2 * LANES
    shared = (count, *tile)
    scratch = [(all_rows, wide), (all_rows, columns), ((2 * all_rows, wide), jnp.bfloat16)]
    message, local = (2, blocks, *tile), (groups, planes * blocks, *tile)
    parts, coefficients = [], []
    for t in range(chunks):
        results = call(
            functools.partial(local_kernel, groups, planes, chunks, t),
            [local, message] + [shared] * (0 if t else 6),
            scratch,
            [pieces, high, low, *coefficients],
        )
        coefficients = coefficients or results[2:]
        parts.append((*results[:2], across(results[1], "gz", groups)))
    out = []
    for t, part in enumerate(parts):
        out = call(
            functools.partial(join_kernel, groups, planes, chunks, t),
            [(groups, body_tiles, *tile)],
            [message] + scratch,
            [*part, high, low, *coefficients, *out],
        )
    pieces = exchange(out[0], pairs_out)
    out, half = [], groups // 2 + 1
    for part in (slice(0, half), slice(half, groups)):
        arrays = [pltpu.with_memory_space_constraint(a, pltpu.VMEM) for a in pieces[part]]
        out = [
            pl.pallas_call(
                functools.partial(place_kernel, pairs_out[part]),
                out_shape=pltpu.HBM((planes, tiles * blocks, *tile), jnp.float32),
                in_specs=[vmem] * len(arrays) + [hbm] * len(out),
                out_specs=hbm,
                scratch_shapes=[pltpu.SemaphoreType.DMA((len(arrays),))],
                input_output_aliases={len(arrays): 0} if out else {},
                compiler_params=params,
                cost_estimate=NO_COST,
            )(*arrays, *out)
        ]
    (out,) = out
    out = out.reshape(planes, tiles, blocks, *tile).transpose(0, 1, 3, 2, 4)
    return out.reshape(probe_fields.shape)


def body(*arrays):
    probes, planes, rows, columns = arrays[0].shape
    places, row_places = lax.axis_size("gz"), lax.axis_size("gy")
    fits = (
        probes == 1
        and row_places == 2
        and places >= 4
        and places & (places - 1) == 0
        and rows % (SUB * (places // 2)) == 0
        and rows >= 4 * MARGIN
        and columns == SUB * LANES
        and planes * places >= 4
    )
    return grouped_body(*arrays) if fits else plain_body(*arrays)


def solution(mesh):
    placed = (P(None, "gz", "gy", None), P("gz", None), P("gz", None), P(), P())
    return jax.shard_map(
        body, mesh=mesh, in_specs=placed, out_specs=P(None, "gz", "gy", None), check_vma=False
    )
```

```python
import functools

import jax
import jax.numpy as jnp
from jax import lax
from jax.experimental import pallas as pl
from jax.experimental.pallas import tpu as pltpu
from jax.sharding import PartitionSpec as P

RADIUS = 2
DMAX = 8
MARGIN = RADIUS * DMAX
LANES = 128
SUB = 8


def padded_y(array, width):
    size, length = lax.axis_size("gy"), array.shape[2]
    up = [(i, (i + 1) % size) for i in range(size - 1)]
    down = [(j, i) for i, j in up]
    last = lax.slice_in_dim(array, length - width, length, axis=2)
    leading = lax.slice_in_dim(array, 0, width, axis=2)
    before = lax.ppermute(last, "gy", up)
    after = lax.ppermute(leading, "gy", down)
    return jnp.concatenate([before, array, after], axis=2)


def filter_coefficients(root_one, root_two):
    first = root_one + root_two
    second = -root_one * root_two
    gain = (1.0 - root_one) * (1.0 - root_two)
    return (first, second, gain)


def depth_scan(fields, first, second, pre_gain, post_gain, reverse):
    moved = jnp.moveaxis(fields, 1, 0)
    zero = jnp.zeros(moved.shape[1:], jnp.float32)

    def advance(carry, inputs):
        latest, earlier = carry
        plane, coef_one, coef_two, before, after = inputs
        value = before * plane + coef_one * latest + coef_two * earlier
        return ((value, latest), after * value)

    _, outputs = lax.scan(
        advance, (zero, zero), (moved, first, second, pre_gain, post_gain), reverse=reverse
    )
    return jnp.moveaxis(outputs, 0, 1)


def normalised(weights):
    return weights / (weights[..., :1] + 2.0 * jnp.sum(weights[..., 1:], -1, keepdims=True))


def lateral_padded(padded, scaled, dilation, axis, margin, length):
    result = scaled[0] * lax.dynamic_slice_in_dim(padded, margin, length, axis)
    for offset_tap in range(1, scaled.shape[0]):
        offset = dilation * offset_tap
        upper = lax.dynamic_slice_in_dim(padded, margin + offset, length, axis)
        lower = lax.dynamic_slice_in_dim(padded, margin - offset, length, axis)
        result = result + scaled[offset_tap] * (upper + lower)
    return result


def lateral_x(fields, scaled, dilation):
    padded = jnp.pad(fields, ((0, 0), (0, 0), (0, 0), (MARGIN, MARGIN)))
    return lateral_padded(padded, scaled, dilation, 3, MARGIN, fields.shape[3])


def lateral_y_twice(fields, scaled, dilation):
    rows = fields.shape[2]
    padded = padded_y(fields, 2 * MARGIN)
    middle = lateral_padded(padded, scaled, dilation, 2, MARGIN, rows + 2 * MARGIN)
    global_row = lax.axis_index("gy") * rows - MARGIN + jnp.arange(rows + 2 * MARGIN)
    inside = (global_row >= 0) & (global_row < rows * lax.axis_size("gy"))
    middle = jnp.where(inside[None, None, :, None], middle, 0.0)
    return lateral_padded(middle, scaled, dilation, 2, MARGIN, rows)


def plain_body(probe_fields, root_one, root_two, lateral_kernel_taps, dilations):
    roots = lax.all_gather(jnp.stack([root_one, root_two], 1), "gz", axis=0, tiled=True)
    first, second, gain = filter_coefficients(roots[:, 0], roots[:, 1])
    unity = jnp.ones_like(gain)
    first_next = jnp.concatenate([first[1:], jnp.zeros_like(first[:1])], 0)
    second_next = jnp.concatenate([second[2:], jnp.zeros_like(second[:2])], 0)
    scaled = normalised(lateral_kernel_taps)
    field = lateral_y_twice(probe_fields, scaled[1], dilations[1])
    field = lax.all_to_all(field, "gz", split_axis=2, concat_axis=1, tiled=True)
    field = depth_scan(field, first_next, second_next, unity, gain, True)
    field = lateral_x(field, scaled[0], dilations[0])
    field = lateral_x(field, scaled[0], dilations[0])
    field = depth_scan(field, first, second, gain, unity, False)
    return lax.all_to_all(field, "gz", split_axis=1, concat_axis=2, tiled=True)


NO_COST = pl.CostEstimate(flops=0, bytes_accessed=0, transcendentals=0)


def call(kernel, outs, scratch, arrays):
    arrays = [pltpu.with_memory_space_constraint(a, pltpu.VMEM) for a in arrays]
    outs, scratch = (
        [item if len(item) == 2 and isinstance(item[0], tuple) else (item, jnp.float32) for item in items]
        for items in (outs, scratch)
    )
    return pl.pallas_call(
        kernel,
        out_shape=[pltpu.VMEM(shape, dtype) for shape, dtype in outs],
        in_specs=[pl.BlockSpec(memory_space=pltpu.VMEM)] * len(arrays),
        out_specs=[pl.BlockSpec(memory_space=pltpu.VMEM)] * len(outs),
        scratch_shapes=[pltpu.VMEM(shape, dtype) for shape, dtype in scratch],
        compiler_params=pltpu.CompilerParams(vmem_limit_bytes=24 << 20),
        cost_estimate=NO_COST,
    )(*arrays)


def tap_vectors(taps, axis, shape):
    raw = [taps[axis, i] for i in range(RADIUS + 1)]
    total = raw[0] + 2.0 * functools.reduce(lambda a, b: a + b, raw[1:])
    scale = 1.0 / jnp.full(shape, total, jnp.float32)
    return [jnp.full(shape, tap, jnp.float32) * scale for tap in raw]


def split(value):
    high = value.astype(jnp.bfloat16)
    return high, (value - high.astype(jnp.float32)).astype(jnp.bfloat16)


def product(left, right):
    dot = functools.partial(jnp.dot, preferred_element_type=jnp.float32)
    return dot(left[0], right[0]) + (dot(left[0], right[1]) + dot(left[1], right[0]))


OFFSETS = range(-RADIUS, RADIUS + 1)


def double_taps(at, length, step, taps):
    sums = {}
    for a in OFFSETS:
        middle = at + a * step
        tap = jnp.where((middle >= 0) & (middle < length), taps[abs(a)], 0.0)
        for b in OFFSETS:
            sums[a + b] = sums.get(a + b, 0.0) + tap * taps[abs(b)]
    return sums


def fill_band(high, low, row_places, step, taps, begin, from_begin):
    part = 2 * SUB
    for i in range(0, high.shape[0], part):
        shape = (part, high.shape[1])
        at = lax.broadcasted_iota(jnp.int32, shape, 0) + (begin + i)
        apart = lax.broadcasted_iota(jnp.int32, shape, 1) + from_begin - at
        value = jnp.zeros(shape, jnp.float32)
        for o, total in double_taps(at, row_places, step, taps).items():
            value = jnp.where(apart == o * step, total, value)
        high[i : i + part], low[i : i + part] = split(value)


def edge_kernel(x_ref, one_ref, two_ref, edge, roots, rows, sems):
    depth = edge.shape[1]
    start = jnp.where(lax.axis_index("gy") == 0, x_ref.shape[1] - depth, 0)
    copies = [
        pltpu.make_async_copy(one_ref, rows.at[0], sems.at[0]),
        pltpu.make_async_copy(two_ref, rows.at[1], sems.at[1]),
        pltpu.make_async_copy(x_ref.at[:, pl.ds(start, depth)], edge, sems.at[2]),
    ]
    for copy in copies:
        copy.start()
    copies[0].wait()
    copies[1].wait()
    planes, blocks = rows.shape[1], rows.shape[2] // LANES
    for i in range(2):
        for p in range(planes):
            for b in range(blocks):
                lanes = slice(b * LANES, (b + 1) * LANES)
                roots[i * planes + p, b : b + 1] = rows[i, p : p + 1, lanes]
    copies[2].wait()


def load_kernel(
    x_ref, dilations_ref, taps_ref, _,
    whole, high, low, edge_high, edge_low, x_step, x_taps, dilations, taps, sems,
):
    row_at, row_places = lax.axis_index("gy"), lax.axis_size("gy")
    planes, tiles = x_ref.shape[:2]
    rows = tiles * SUB
    copies = [
        pltpu.make_async_copy(dilations_ref, dilations, sems.at[0]),
        pltpu.make_async_copy(taps_ref, taps, sems.at[1]),
    ]
    copies += [
        pltpu.make_async_copy(x_ref.at[p], whole.at[p], sems.at[2 + p]) for p in range(planes)
    ]
    for copy in copies:
        copy.start()
    copies[0].wait()
    copies[1].wait()
    x_step[...] = jnp.full(x_step.shape, dilations[0], jnp.int32)
    for i, tap in enumerate(tap_vectors(taps, 0, (1, LANES))):
        x_taps[i : i + 1] = tap
    step, weights = dilations[1], tap_vectors(taps, 1, (1, 1))
    length, begin = rows * row_places, row_at * rows
    fill_band(high, low, length, step, weights, begin, begin)
    near = begin + jnp.where(row_at == 0, rows - 2 * MARGIN, 0)
    beyond = begin + jnp.where(row_at == 0, rows, -2 * MARGIN)
    fill_band(edge_high, edge_low, length, step, weights, near, beyond)
    for copy in copies[2:]:
        copy.wait()


def columns_of(ref, p, b, width):
    rows = ref.shape[1] * SUB
    return jnp.concatenate([ref[p, :, b + i].reshape(rows, LANES) for i in range(width)], axis=1)


def y_inner_kernel(groups, high, low, x_ref, pieces):
    planes, tiles, blocks = x_ref.shape[:3]
    chunks, width = tiles // groups, 2
    for p in range(planes):
        for b in range(0, blocks, width):
            value = product((high[...], low[...]), split(columns_of(x_ref, p, b, width)))
            for i in range(tiles):
                for w in range(width):
                    tile = value[i * SUB : (i + 1) * SUB, w * LANES : (w + 1) * LANES]
                    pieces[i // chunks, (p * chunks + i % chunks) * blocks + b + w] = tile


def y_outer_kernel(groups, tiles, high, low, edge, given, roots, pieces):
    planes, halo, blocks = edge.shape[:3]
    chunks, width = tiles // groups, 2
    base = chunks * planes * blocks
    pieces[:, :base] = given[...]
    for i in range(groups):
        pieces[i, base:] = roots[...]
    first = jnp.where(lax.axis_index("gy") == 0, (tiles - halo) // chunks, 0)
    for p in range(planes):
        for b in range(0, blocks, width):
            value = product((high[...], low[...]), split(columns_of(edge, p, b, width)))
            for i in range(halo):
                for w in range(width):
                    tile = value[i * SUB : (i + 1) * SUB, w * LANES : (w + 1) * LANES]
                    to, at = first + i // chunks, (p * chunks + i % chunks) * blocks
                    pieces[to, at + b + w] = given[to, at + b + w] + tile


def band_kinds(count):
    kinds = sorted({0, min(1, count - 1), count - 1})
    return kinds, [0 if n == 0 else len(kinds) - 1 if n == count - 1 else 1 for n in range(count)]


def band_kernel(columns, x_step, x_taps, high, low):
    depth, width = high.shape[1:]
    step, taps = x_step[0:1], [x_taps[i : i + 1] for i in range(RADIUS + 1)]
    part, reach = 2 * SUB, 2 * MARGIN
    lane = lax.broadcasted_iota(jnp.int32, (part, LANES), 1)
    row = lax.broadcasted_iota(jnp.int32, (part, LANES), 0)
    high[...] = jnp.zeros(high.shape, high.dtype)
    low[...] = jnp.zeros(low.shape, low.dtype)
    for kind, n in enumerate(band_kinds(columns // width)[0]):
        for w in range(0, width, LANES):
            at = lax.broadcasted_iota(jnp.int32, (1, LANES), 1) + (n * width + w)
            sums = double_taps(at, columns, step, taps)
            lanes = slice(w, w + LANES)

            def rows_at(i, _):
                start = w + LANES - reach + i * part
                apart = row + (start - LANES - w) - lane
                value = jnp.zeros((part, LANES), jnp.float32)
                for o, total in sums.items():
                    value = jnp.where(apart == o * step, total, value)
                at_rows = pl.ds(pl.multiple_of(start, part), part)
                high[kind, at_rows, lanes], low[kind, at_rows, lanes] = split(value)
                return 0

            lax.fori_loop(0, (LANES + 2 * reach) // part, rows_at, 0, unroll=2)


def x_twice(source, result, high, low, parts):
    rows, (depth, width) = source.shape[0], high.shape[1:]
    parts[:rows], parts[rows:] = split(source[...])
    dot = functools.partial(jnp.dot, preferred_element_type=jnp.float32)
    for n, kind in enumerate(band_kinds(result.shape[1] // width)[1]):
        lanes = slice(n * width, n * width + depth)
        total = dot(parts[:, lanes], high[kind])
        total = total[:rows] + (total[rows:] + dot(parts[:rows, lanes], low[kind]))
        result[:, n * width : (n + 1) * width] = total


def add(a, b):
    return [x + y for x, y in zip(a, b)]


def times(ref, k, values):
    return [ref[k, b : b + 1] * value for b, value in enumerate(values)]


def tiles_of(ref, *at):
    return [ref[(*at, b)] for b in range(ref.shape[len(at)])]


def put(ref, values, *at):
    for b, value in enumerate(values):
        ref[(*at, b)] = value


def clear_sides(field):
    columns = field.shape[1] - 2 * LANES
    none = jnp.zeros((field.shape[0], LANES), jnp.float32)
    field[:, :LANES] = none
    field[:, LANES + columns :] = none


def row_tile(k):
    return pl.ds(pl.multiple_of(k * SUB, SUB), SUB)


def filter_back(count, planes, source, coefficients, field, start):
    first, second, gain = coefficients
    after, beyond = start

    def at(d, carry):
        for p in reversed(range(planes)):
            ahead, pending = carry
            k = d * planes + p
            value = ahead if source is None else add(source(d, p), ahead)
            for b, scaled in enumerate(times(gain, k, value)):
                field[row_tile(k), (b + 1) * LANES : (b + 2) * LANES] = scaled
            carry = (add(times(first, k, value), pending), times(second, k, value))
        return carry

    steps = count // planes
    return lax.fori_loop(0, steps, lambda i, c: at(steps - 1 - i, c), (after, beyond))


def filter_forth(count, planes, field, coefficients, start, finish):
    first, second, gain = coefficients

    def at(d, carry):
        for p in range(planes):
            latest, earlier = carry
            k = d * planes + p
            value = add(times(first, k, latest), times(second, k, earlier))
            if field is not None:
                blocks = len(value)
                there = [
                    field[row_tile(k), b * LANES : (b + 1) * LANES] for b in range(blocks)
                ]
                value = add(value, times(gain, k, there))
            finish(d, p, value)
            carry = (value, latest)
        return carry

    return lax.fori_loop(0, count // planes, at, start)


def store_coefficients(k, one, two, first, second, gain):
    first[k] = one + two
    second[k] = -one * two
    gain[k] = (1.0 - one) * (1.0 - two)


def hand_on_kernel(value, *refs):
    refs[-1][...] = value[...]


def own_kernel(base, pieces, first, second, gain, half_roots):
    groups = pieces.shape[0]
    planes = gain.shape[0] // groups
    row_at = lax.axis_index("gy")
    upper_rows = lax.broadcasted_iota(jnp.int32, (SUB, LANES), 0) < SUB // 2
    for d in range(groups):
        for p in range(planes):
            k = d * planes + p
            one, two = (pieces[d, base + i * planes + p] for i in range(2))
            store_coefficients(k, one, two, first, second, gain)
            front = jnp.where(upper_rows, one, pltpu.roll(two, SUB // 2, 0))
            back = jnp.where(upper_rows, pltpu.roll(one, SUB // 2, 0), two)
            half_roots[k] = jnp.where(row_at == 0, front, back)


def lower_kernel(groups, own_first, own_second, own_gain, mine, other, first, second, gain):
    half, row_at = lax.axis_index("gz") // groups, lax.axis_index("gy")

    @pl.when(half == 0)
    def _():
        first[...] = own_first[...]
        second[...] = own_second[...]
        gain[...] = own_gain[...]

    @pl.when(half > 0)
    def _():
        upper_rows = lax.broadcasted_iota(jnp.int32, (SUB, LANES), 0) < SUB // 2
        for k in range(gain.shape[0]):
            front = jnp.where(row_at == 0, mine[k], other[k])
            back = jnp.where(row_at == 0, other[k], mine[k])
            one = jnp.where(upper_rows, front, pltpu.roll(back, SUB // 2, 0))
            two = jnp.where(upper_rows, pltpu.roll(front, SUB // 2, 0), back)
            store_coefficients(k, one, two, first, second, gain)


def chunk_of(ref, chunk, chunks):
    rows = ref.shape[0] // chunks
    return ref.at[chunk * rows : (chunk + 1) * rows]


def local_kernel(
    groups, planes, chunks, pieces, high, low, first, second, gain,
    local, message, field, middle, parts,
):
    half = lax.axis_index("gz") // groups
    blocks = message.shape[2]
    count = groups * planes
    own = (first, second, gain)
    clear_sides(field)
    zeros = [field[0:SUB, 0:LANES]] * blocks
    carries = []
    for chunk in range(chunks):

        def source(d, p):
            return [pieces[d, (p * chunks + chunk) * blocks + b] for b in range(blocks)]

        rows = chunk_of(field, chunk, chunks)
        carries.append(filter_back(count, planes, source, own, rows, (zeros, zeros)))
        put(message, carries[-1][0], chunk, 0)
        put(message, carries[-1][1], chunk, 1)
    x_twice(field, middle, high, low, parts)
    for chunk in range(chunks):

        def finish(d, p, value):
            for b, v in enumerate(value):
                local[d, (p * chunks + chunk) * blocks + b] = v

        rows = chunk_of(middle, chunk, chunks)
        latest, earlier = filter_forth(count, planes, rows, own, (zeros, zeros), finish)

        @pl.when(half == 0)
        def _():
            put(message, latest, chunk, 0)
            put(message, earlier, chunk, 1)


def join_kernel(
    groups, planes, chunks, local, sent, received, high, low, *refs
):
    own, lower = refs[:3], refs[3:6]
    out, carried, field, middle, parts = refs[6:]
    half = lax.axis_index("gz") // groups
    blocks = sent.shape[2]
    count = groups * planes
    carried[...] = jnp.where(half == 0, received[...], sent[...])
    clear_sides(field)
    zeros = [field[0:SUB, 0:LANES]] * blocks
    for chunk in range(chunks):
        start = (tiles_of(carried, chunk, 0), tiles_of(carried, chunk, 1))
        filter_back(count, planes, None, lower, chunk_of(field, chunk, chunks), start)
    x_twice(field, middle, high, low, parts)
    for chunk in range(chunks):

        def finish(d, p, value):
            for b, v in enumerate(value):
                at = (p * chunks + chunk) * blocks + b
                out[d, at] = v + local[d, at]

        rows = chunk_of(middle, chunk, chunks)
        latest, earlier = filter_forth(count, planes, rows, lower, (zeros, zeros), finish)
        put(carried, latest, chunk, 0)
        put(carried, earlier, chunk, 1)

        @pl.when(half > 0)
        def _():
            begin = (
                add(tiles_of(carried, chunk, 0), tiles_of(received, chunk, 0)),
                add(tiles_of(carried, chunk, 1), tiles_of(received, chunk, 1)),
            )
            filter_forth(count, planes, None, own, begin, finish)


def partner(pair):
    groups = lax.axis_size("gz") // 2
    m = jnp.where(lax.axis_index("gy") == 0, pair[0], pair[1])
    return (lax.axis_index("gz") % groups) ^ m


def split_kernel(pairs, pieces, *outs):
    for pair, out in zip(pairs, outs):
        out[...] = pieces[partner(pair)]


def merge_kernel(pairs, *refs):
    for pair, piece in zip(pairs, refs[:-1]):
        refs[-1][partner(pair)] = piece[...]


def place_kernel(pairs, *refs):
    pieces, (out, sems) = refs[: len(pairs)], refs[-2:]
    planes = out.shape[0]
    each = pieces[0].shape[0] // planes
    for i, (pair, piece) in enumerate(zip(pairs, pieces)):
        at = partner(pair) * each
        for p in range(planes):
            pltpu.make_async_copy(
                piece.at[pl.ds(p * each, each)], out.at[p, pl.ds(at, each)], sems.at[i]
            ).start()
    for i, piece in enumerate(pieces):
        pltpu.make_async_copy(piece, piece, sems.at[i]).wait()


def exchange_order(groups):
    order, last = [], groups - 1
    for m in sorted(range(1, last), key=lambda m: (m.bit_count(), m)):
        if m not in order:
            order += [m, last ^ m]
    return [m for i, m in enumerate(order) if m not in order[:i]] + [last]


def grouped_body(probe_fields, root_one, root_two, lateral_kernel_taps, dilations):
    _, planes, rows, columns = probe_fields.shape
    places = lax.axis_size("gz")
    groups = places // 2
    tiles, blocks, count = rows // SUB, columns // LANES, groups * planes
    chunks = tiles // groups

    def across(array, axis, m):
        return lax.ppermute(array, axis, [(i, i ^ m) for i in range(lax.axis_size(axis))])

    first = exchange_order(groups)
    second = [m ^ (groups - 1) or groups - 1 for m in first]
    pairs_in = [(0, 0), *zip(first, second)]
    pairs_out = [(m, m) for m in (0, *first)]

    def across_pair(array, pair):
        moves = [
            (2 * i + core, 2 * (i ^ m) + core) for i in range(places) for core, m in enumerate(pair)
        ]
        return lax.ppermute(array, ("gz", "gy"), moves)

    def exchange(array, pairs):
        kernel = functools.partial(split_kernel, pairs)
        parts = call(kernel, [array.shape[1:]] * groups, [], [array])
        return [parts[0]] + [across_pair(*part) for part in zip(parts[1:], pairs[1:])]

    field = probe_fields.reshape(planes, tiles, SUB, blocks, LANES).transpose(0, 1, 3, 2, 4)
    tile, halo = (SUB, LANES), 2 * MARGIN // SUB
    hbm, vmem = pl.BlockSpec(memory_space=pltpu.HBM), pl.BlockSpec(memory_space=pltpu.VMEM)
    matrix = [pltpu.VMEM((rows, rows), jnp.bfloat16)] * 2
    edge_matrix = [pltpu.VMEM((2 * MARGIN, 2 * MARGIN), jnp.bfloat16)] * 2
    params = pltpu.CompilerParams(vmem_limit_bytes=24 << 20)

    def in_hbm(*arrays):
        return [pltpu.with_memory_space_constraint(array, pltpu.HBM) for array in arrays]

    edge, roots = pl.pallas_call(
        edge_kernel,
        out_shape=[
            pltpu.VMEM((planes, halo, blocks, *tile), jnp.float32),
            pltpu.VMEM((2 * planes, *tile), jnp.float32),
        ],
        in_specs=[hbm] * 3,
        out_specs=[vmem] * 2,
        scratch_shapes=[
            pltpu.VMEM((2, planes, columns), jnp.float32),
            pltpu.SemaphoreType.DMA((3,)),
        ],
        compiler_params=params,
        cost_estimate=NO_COST,
    )(*in_hbm(field, root_one, root_two))
    field, *matrices, x_step, x_taps = pl.pallas_call(
        load_kernel,
        out_shape=[
            pltpu.VMEM((planes, tiles, blocks, *tile), jnp.float32),
            *matrix,
            *edge_matrix,
            pltpu.VMEM(tile, jnp.int32),
            pltpu.VMEM(tile, jnp.float32),
        ],
        in_specs=[hbm] * 3 + [vmem],
        out_specs=[vmem] * 7,
        scratch_shapes=[
            pltpu.SMEM(dilations.shape, jnp.int32),
            pltpu.SMEM(lateral_kernel_taps.shape, jnp.float32),
            pltpu.SemaphoreType.DMA((2 + planes,)),
        ],
        compiler_params=params,
        cost_estimate=NO_COST,
    )(
        *in_hbm(field, dilations, lateral_kernel_taps),
        pltpu.with_memory_space_constraint(roots, pltpu.VMEM),
    )
    edge = across(edge, "gy", 1)

    width = 2 * LANES

    band = ((len(band_kinds(columns // width)[0]), 2 * width, width), jnp.bfloat16)
    high, low = call(
        functools.partial(band_kernel, columns), [band, band], [], [x_step, x_taps]
    )
    body_tiles = chunks * planes * blocks
    piece = (groups, body_tiles + 2 * planes, *tile)
    (pieces,) = call(
        functools.partial(y_inner_kernel, groups),
        [(groups, body_tiles, *tile)],
        [],
        [*matrices[:2], field],
    )
    (pieces,) = call(
        functools.partial(y_outer_kernel, groups, tiles),
        [piece],
        [],
        [*matrices[2:], edge, pieces, roots],
    )
    kernel = functools.partial(merge_kernel, pairs_in)
    (pieces,) = call(kernel, [piece], [], exchange(pieces, pairs_in))

    all_rows, wide = chunks * count * SUB, columns + 2 * LANES
    shared, message = (count, *tile), (chunks, 2, blocks, *tile)
    whole = (groups, body_tiles, *tile)
    scratch = [(all_rows, wide), (all_rows, columns), ((2 * all_rows, wide), jnp.bfloat16)]
    *own, mine = call(functools.partial(own_kernel, body_tiles), [shared] * 4, [], [pieces])
    mine = across(mine, "gz", groups)
    local, sent = call(
        functools.partial(local_kernel, groups, planes, chunks),
        [whole, message],
        scratch,
        [pieces, high, low, *own],
    )
    received = across(sent, "gz", groups)
    (mine,) = call(hand_on_kernel, [shared], [], [mine, *[sent]])
    other = across(mine, "gy", 1)
    lower = call(functools.partial(lower_kernel, groups), [shared] * 3, [], [*own, mine, other])
    (out,) = call(
        functools.partial(join_kernel, groups, planes, chunks),
        [whole],
        [message] + scratch,
        [local, sent, received, high, low, *own, *lower],
    )
    pieces = exchange(out, pairs_out)
    out, half = [], groups // 2 + 1
    for part in (slice(0, half), slice(half, groups)):
        arrays = [pltpu.with_memory_space_constraint(a, pltpu.VMEM) for a in pieces[part]]
        out = [
            pl.pallas_call(
                functools.partial(place_kernel, pairs_out[part]),
                out_shape=pltpu.HBM((planes, tiles * blocks, *tile), jnp.float32),
                in_specs=[vmem] * len(arrays) + [hbm] * len(out),
                out_specs=hbm,
                scratch_shapes=[pltpu.SemaphoreType.DMA((len(arrays),))],
                input_output_aliases={len(arrays): 0} if out else {},
                compiler_params=params,
                cost_estimate=NO_COST,
            )(*arrays, *out)
        ]
    (out,) = out
    out = out.reshape(planes, tiles, blocks, *tile).transpose(0, 1, 3, 2, 4)
    return out.reshape(probe_fields.shape)


def body(*arrays):
    probes, planes, rows, columns = arrays[0].shape
    places, row_places = lax.axis_size("gz"), lax.axis_size("gy")
    fits = (
        probes == 1
        and row_places == 2
        and places >= 4
        and places & (places - 1) == 0
        and rows % (SUB * (places // 2)) == 0
        and rows >= 4 * MARGIN
        and columns == SUB * LANES
        and planes * places >= 4
    )
    return grouped_body(*arrays) if fits else plain_body(*arrays)


def solution(mesh):
    placed = (P(None, "gz", "gy", None), P("gz", None), P("gz", None), P(), P())
    return jax.shard_map(
        body, mesh=mesh, in_specs=placed, out_specs=P(None, "gz", "gy", None), check_vma=False
    )
```

```python
import functools

import jax
import jax.numpy as jnp
from jax import lax
from jax.experimental import pallas as pl
from jax.experimental.pallas import tpu as pltpu
from jax.sharding import PartitionSpec as P

RADIUS = 2
DMAX = 8
MARGIN = RADIUS * DMAX
LANES = 128
SUB = 8


def padded_y(array, width):
    size, length = lax.axis_size("gy"), array.shape[2]
    up = [(i, (i + 1) % size) for i in range(size - 1)]
    down = [(j, i) for i, j in up]
    last = lax.slice_in_dim(array, length - width, length, axis=2)
    leading = lax.slice_in_dim(array, 0, width, axis=2)
    before = lax.ppermute(last, "gy", up)
    after = lax.ppermute(leading, "gy", down)
    return jnp.concatenate([before, array, after], axis=2)


def filter_coefficients(root_one, root_two):
    first = root_one + root_two
    second = -root_one * root_two
    gain = (1.0 - root_one) * (1.0 - root_two)
    return (first, second, gain)


def depth_scan(fields, first, second, pre_gain, post_gain, reverse):
    moved = jnp.moveaxis(fields, 1, 0)
    zero = jnp.zeros(moved.shape[1:], jnp.float32)

    def advance(carry, inputs):
        latest, earlier = carry
        plane, coef_one, coef_two, before, after = inputs
        value = before * plane + coef_one * latest + coef_two * earlier
        return ((value, latest), after * value)

    _, outputs = lax.scan(
        advance, (zero, zero), (moved, first, second, pre_gain, post_gain), reverse=reverse
    )
    return jnp.moveaxis(outputs, 0, 1)


def normalised(weights):
    return weights / (weights[..., :1] + 2.0 * jnp.sum(weights[..., 1:], -1, keepdims=True))


def lateral_padded(padded, scaled, dilation, axis, margin, length):
    result = scaled[0] * lax.dynamic_slice_in_dim(padded, margin, length, axis)
    for offset_tap in range(1, scaled.shape[0]):
        offset = dilation * offset_tap
        upper = lax.dynamic_slice_in_dim(padded, margin + offset, length, axis)
        lower = lax.dynamic_slice_in_dim(padded, margin - offset, length, axis)
        result = result + scaled[offset_tap] * (upper + lower)
    return result


def lateral_x(fields, scaled, dilation):
    padded = jnp.pad(fields, ((0, 0), (0, 0), (0, 0), (MARGIN, MARGIN)))
    return lateral_padded(padded, scaled, dilation, 3, MARGIN, fields.shape[3])


def lateral_y_twice(fields, scaled, dilation):
    rows = fields.shape[2]
    padded = padded_y(fields, 2 * MARGIN)
    middle = lateral_padded(padded, scaled, dilation, 2, MARGIN, rows + 2 * MARGIN)
    global_row = lax.axis_index("gy") * rows - MARGIN + jnp.arange(rows + 2 * MARGIN)
    inside = (global_row >= 0) & (global_row < rows * lax.axis_size("gy"))
    middle = jnp.where(inside[None, None, :, None], middle, 0.0)
    return lateral_padded(middle, scaled, dilation, 2, MARGIN, rows)


def plain_body(probe_fields, root_one, root_two, lateral_kernel_taps, dilations):
    roots = lax.all_gather(jnp.stack([root_one, root_two], 1), "gz", axis=0, tiled=True)
    first, second, gain = filter_coefficients(roots[:, 0], roots[:, 1])
    unity = jnp.ones_like(gain)
    first_next = jnp.concatenate([first[1:], jnp.zeros_like(first[:1])], 0)
    second_next = jnp.concatenate([second[2:], jnp.zeros_like(second[:2])], 0)
    scaled = normalised(lateral_kernel_taps)
    field = lateral_y_twice(probe_fields, scaled[1], dilations[1])
    field = lax.all_to_all(field, "gz", split_axis=2, concat_axis=1, tiled=True)
    field = depth_scan(field, first_next, second_next, unity, gain, True)
    field = lateral_x(field, scaled[0], dilations[0])
    field = lateral_x(field, scaled[0], dilations[0])
    field = depth_scan(field, first, second, gain, unity, False)
    return lax.all_to_all(field, "gz", split_axis=1, concat_axis=2, tiled=True)


NO_COST = pl.CostEstimate(flops=0, bytes_accessed=0, transcendentals=0)


def call(kernel, outs, scratch, arrays):
    arrays = [pltpu.with_memory_space_constraint(a, pltpu.VMEM) for a in arrays]
    outs, scratch = (
        [item if len(item) == 2 and isinstance(item[0], tuple) else (item, jnp.float32) for item in items]
        for items in (outs, scratch)
    )
    return pl.pallas_call(
        kernel,
        out_shape=[pltpu.VMEM(shape, dtype) for shape, dtype in outs],
        in_specs=[pl.BlockSpec(memory_space=pltpu.VMEM)] * len(arrays),
        out_specs=[pl.BlockSpec(memory_space=pltpu.VMEM)] * len(outs),
        scratch_shapes=[pltpu.VMEM(shape, dtype) for shape, dtype in scratch],
        compiler_params=pltpu.CompilerParams(vmem_limit_bytes=24 << 20),
        cost_estimate=NO_COST,
    )(*arrays)


def tap_vectors(taps, axis, shape):
    raw = [taps[axis, i] for i in range(RADIUS + 1)]
    total = raw[0] + 2.0 * functools.reduce(lambda a, b: a + b, raw[1:])
    scale = 1.0 / jnp.full(shape, total, jnp.float32)
    return [jnp.full(shape, tap, jnp.float32) * scale for tap in raw]


def split(value):
    high = value.astype(jnp.bfloat16)
    return high, (value - high.astype(jnp.float32)).astype(jnp.bfloat16)


def product(left, right):
    dot = functools.partial(jnp.dot, preferred_element_type=jnp.float32)
    return dot(left[0], right[0]) + (dot(left[0], right[1]) + dot(left[1], right[0]))


OFFSETS = range(-RADIUS, RADIUS + 1)


def double_taps(at, length, step, taps):
    sums = {}
    for a in OFFSETS:
        middle = at + a * step
        tap = jnp.where((middle >= 0) & (middle < length), taps[abs(a)], 0.0)
        for b in OFFSETS:
            sums[a + b] = sums.get(a + b, 0.0) + tap * taps[abs(b)]
    return sums


def fill_band(high, low, row_places, step, taps, begin, from_begin):
    part = 2 * SUB
    for i in range(0, high.shape[0], part):
        shape = (part, high.shape[1])
        at = lax.broadcasted_iota(jnp.int32, shape, 0) + (begin + i)
        apart = lax.broadcasted_iota(jnp.int32, shape, 1) + from_begin - at
        value = jnp.zeros(shape, jnp.float32)
        for o, total in double_taps(at, row_places, step, taps).items():
            value = jnp.where(apart == o * step, total, value)
        high[i : i + part], low[i : i + part] = split(value)


def edge_kernel(x_ref, one_ref, two_ref, edge, roots, rows, sems):
    depth = edge.shape[1]
    start = jnp.where(lax.axis_index("gy") == 0, x_ref.shape[1] - depth, 0)
    copies = [
        pltpu.make_async_copy(one_ref, rows.at[0], sems.at[0]),
        pltpu.make_async_copy(two_ref, rows.at[1], sems.at[1]),
        pltpu.make_async_copy(x_ref.at[:, pl.ds(start, depth)], edge, sems.at[2]),
    ]
    for copy in copies:
        copy.start()
    copies[0].wait()
    copies[1].wait()
    planes, blocks = rows.shape[1], rows.shape[2] // LANES
    for i in range(2):
        for p in range(planes):
            for b in range(blocks):
                lanes = slice(b * LANES, (b + 1) * LANES)
                roots[i * planes + p, b : b + 1] = rows[i, p : p + 1, lanes]
    copies[2].wait()


def load_kernel(
    x_ref, dilations_ref, taps_ref, _,
    whole, high, low, edge_high, edge_low, x_step, x_taps, dilations, taps, sems,
):
    row_at, row_places = lax.axis_index("gy"), lax.axis_size("gy")
    planes, tiles = x_ref.shape[:2]
    rows = tiles * SUB
    copies = [
        pltpu.make_async_copy(dilations_ref, dilations, sems.at[0]),
        pltpu.make_async_copy(taps_ref, taps, sems.at[1]),
    ]
    copies += [
        pltpu.make_async_copy(x_ref.at[p], whole.at[p], sems.at[2 + p]) for p in range(planes)
    ]
    for copy in copies:
        copy.start()
    copies[0].wait()
    copies[1].wait()
    x_step[...] = jnp.full(x_step.shape, dilations[0], jnp.int32)
    for i, tap in enumerate(tap_vectors(taps, 0, (1, LANES))):
        x_taps[i : i + 1] = tap
    step, weights = dilations[1], tap_vectors(taps, 1, (1, 1))
    length, begin = rows * row_places, row_at * rows
    fill_band(high, low, length, step, weights, begin, begin)
    near = begin + jnp.where(row_at == 0, rows - 2 * MARGIN, 0)
    beyond = begin + jnp.where(row_at == 0, rows, -2 * MARGIN)
    fill_band(edge_high, edge_low, length, step, weights, near, beyond)
    for copy in copies[2:]:
        copy.wait()


def columns_of(ref, p, b, width):
    rows = ref.shape[1] * SUB
    return jnp.concatenate([ref[p, :, b + i].reshape(rows, LANES) for i in range(width)], axis=1)


def y_inner_kernel(groups, high, low, x_ref, pieces):
    planes, tiles, blocks = x_ref.shape[:3]
    chunks, width = tiles // groups, 2
    for p in range(planes):
        for b in range(0, blocks, width):
            value = product((high[...], low[...]), split(columns_of(x_ref, p, b, width)))
            for i in range(tiles):
                for w in range(width):
                    tile = value[i * SUB : (i + 1) * SUB, w * LANES : (w + 1) * LANES]
                    pieces[i // chunks, (p * chunks + i % chunks) * blocks + b + w] = tile


def y_outer_kernel(groups, tiles, high, low, edge, given, roots, pieces):
    planes, halo, blocks = edge.shape[:3]
    chunks, width = tiles // groups, 2
    base = chunks * planes * blocks
    pieces[:, :base] = given[...]
    for i in range(groups):
        pieces[i, base:] = roots[...]
    first = jnp.where(lax.axis_index("gy") == 0, (tiles - halo) // chunks, 0)
    for p in range(planes):
        for b in range(0, blocks, width):
            value = product((high[...], low[...]), split(columns_of(edge, p, b, width)))
            for i in range(halo):
                for w in range(width):
                    tile = value[i * SUB : (i + 1) * SUB, w * LANES : (w + 1) * LANES]
                    to, at = first + i // chunks, (p * chunks + i % chunks) * blocks
                    pieces[to, at + b + w] = given[to, at + b + w] + tile


def band_kinds(count):
    kinds = sorted({0, min(1, count - 1), count - 1})
    return kinds, [0 if n == 0 else len(kinds) - 1 if n == count - 1 else 1 for n in range(count)]


def band_kernel(columns, x_step, x_taps, high, low):
    depth, width = high.shape[1:]
    step, taps = x_step[0:1], [x_taps[i : i + 1] for i in range(RADIUS + 1)]
    part, reach = 2 * SUB, 2 * MARGIN
    lane = lax.broadcasted_iota(jnp.int32, (part, LANES), 1)
    row = lax.broadcasted_iota(jnp.int32, (part, LANES), 0)
    high[...] = jnp.zeros(high.shape, high.dtype)
    low[...] = jnp.zeros(low.shape, low.dtype)
    for kind, n in enumerate(band_kinds(columns // width)[0]):
        for w in range(0, width, LANES):
            at = lax.broadcasted_iota(jnp.int32, (1, LANES), 1) + (n * width + w)
            sums = double_taps(at, columns, step, taps)
            lanes = slice(w, w + LANES)

            def rows_at(i, _):
                start = w + LANES - reach + i * part
                apart = row + (start - LANES - w) - lane
                value = jnp.zeros((part, LANES), jnp.float32)
                for o, total in sums.items():
                    value = jnp.where(apart == o * step, total, value)
                at_rows = pl.ds(pl.multiple_of(start, part), part)
                high[kind, at_rows, lanes], low[kind, at_rows, lanes] = split(value)
                return 0

            lax.fori_loop(0, (LANES + 2 * reach) // part, rows_at, 0, unroll=2)


def x_twice(source, result, high, low, parts):
    rows, (depth, width) = source.shape[0], high.shape[1:]
    parts[:rows], parts[rows:] = split(source[...])
    dot = functools.partial(jnp.dot, preferred_element_type=jnp.float32)
    for n, kind in enumerate(band_kinds(result.shape[1] // width)[1]):
        lanes = slice(n * width, n * width + depth)
        total = dot(parts[:, lanes], high[kind])
        total = total[:rows] + (total[rows:] + dot(parts[:rows, lanes], low[kind]))
        result[:, n * width : (n + 1) * width] = total


def add(a, b):
    return [x + y for x, y in zip(a, b)]


def times(ref, k, values):
    return [ref[k, b : b + 1] * value for b, value in enumerate(values)]


def tiles_of(ref, *at):
    return [ref[(*at, b)] for b in range(ref.shape[len(at)])]


def put(ref, values, *at):
    for b, value in enumerate(values):
        ref[(*at, b)] = value


def clear_sides(field):
    columns = field.shape[1] - 2 * LANES
    none = jnp.zeros((field.shape[0], LANES), jnp.float32)
    field[:, :LANES] = none
    field[:, LANES + columns :] = none


def row_tile(k):
    return pl.ds(pl.multiple_of(k * SUB, SUB), SUB)


def filter_back(count, planes, source, coefficients, field, start):
    first, second, gain = coefficients
    after, beyond = start

    def at(d, carry):
        for p in reversed(range(planes)):
            ahead, pending = carry
            k = d * planes + p
            value = ahead if source is None else add(source(d, p), ahead)
            for b, scaled in enumerate(times(gain, k, value)):
                field[row_tile(k), (b + 1) * LANES : (b + 2) * LANES] = scaled
            carry = (add(times(first, k, value), pending), times(second, k, value))
        return carry

    steps = count // planes
    return lax.fori_loop(0, steps, lambda i, c: at(steps - 1 - i, c), (after, beyond))


def filter_forth(count, planes, field, coefficients, start, finish):
    first, second, gain = coefficients

    def at(d, carry):
        for p in range(planes):
            latest, earlier = carry
            k = d * planes + p
            value = add(times(first, k, latest), times(second, k, earlier))
            if field is not None:
                blocks = len(value)
                there = [
                    field[row_tile(k), b * LANES : (b + 1) * LANES] for b in range(blocks)
                ]
                value = add(value, times(gain, k, there))
            finish(d, p, value)
            carry = (value, latest)
        return carry

    return lax.fori_loop(0, count // planes, at, start)


def store_coefficients(k, one, two, first, second, gain):
    first[k] = one + two
    second[k] = -one * two
    gain[k] = (1.0 - one) * (1.0 - two)


def hand_on_kernel(value, *refs):
    refs[-1][...] = value[...]


def own_kernel(base, pieces, first, second, gain, half_roots):
    groups = pieces.shape[0]
    planes = gain.shape[0] // groups
    row_at = lax.axis_index("gy")
    upper_rows = lax.broadcasted_iota(jnp.int32, (SUB, LANES), 0) < SUB // 2
    for d in range(groups):
        for p in range(planes):
            k = d * planes + p
            one, two = (pieces[d, base + i * planes + p] for i in range(2))
            store_coefficients(k, one, two, first, second, gain)
            front = jnp.where(upper_rows, one, pltpu.roll(two, SUB // 2, 0))
            back = jnp.where(upper_rows, pltpu.roll(one, SUB // 2, 0), two)
            half_roots[k] = jnp.where(row_at == 0, front, back)


def lower_kernel(groups, own_first, own_second, own_gain, mine, other, first, second, gain):
    half, row_at = lax.axis_index("gz") // groups, lax.axis_index("gy")

    @pl.when(half == 0)
    def _():
        first[...] = own_first[...]
        second[...] = own_second[...]
        gain[...] = own_gain[...]

    @pl.when(half > 0)
    def _():
        upper_rows = lax.broadcasted_iota(jnp.int32, (SUB, LANES), 0) < SUB // 2
        for k in range(gain.shape[0]):
            front = jnp.where(row_at == 0, mine[k], other[k])
            back = jnp.where(row_at == 0, other[k], mine[k])
            one = jnp.where(upper_rows, front, pltpu.roll(back, SUB // 2, 0))
            two = jnp.where(upper_rows, pltpu.roll(front, SUB // 2, 0), back)
            store_coefficients(k, one, two, first, second, gain)


def chunk_of(ref, chunk, chunks):
    rows = ref.shape[0] // chunks
    return ref.at[chunk * rows : (chunk + 1) * rows]


def local_kernel(
    groups, planes, chunks, pieces, high, low, first, second, gain,
    local, message, field, middle, parts,
):
    half = lax.axis_index("gz") // groups
    blocks = message.shape[2]
    count = groups * planes
    own = (first, second, gain)
    clear_sides(field)
    zeros = [field[0:SUB, 0:LANES]] * blocks
    carries = []
    for chunk in range(chunks):

        def source(d, p):
            return [pieces[d, (p * chunks + chunk) * blocks + b] for b in range(blocks)]

        rows = chunk_of(field, chunk, chunks)
        carries.append(filter_back(count, planes, source, own, rows, (zeros, zeros)))
        put(message, carries[-1][0], chunk, 0)
        put(message, carries[-1][1], chunk, 1)
    x_twice(field, middle, high, low, parts)
    for chunk in range(chunks):

        def finish(d, p, value):
            for b, v in enumerate(value):
                local[d, (p * chunks + chunk) * blocks + b] = v

        rows = chunk_of(middle, chunk, chunks)
        latest, earlier = filter_forth(count, planes, rows, own, (zeros, zeros), finish)

        @pl.when(half == 0)
        def _():
            put(message, latest, chunk, 0)
            put(message, earlier, chunk, 1)


def join_kernel(
    groups, planes, chunks, local, sent, received, high, low, *refs
):
    own, lower = refs[:3], refs[3:6]
    out, carried, field, middle, parts = refs[6:]
    half = lax.axis_index("gz") // groups
    blocks = sent.shape[2]
    count = groups * planes
    carried[...] = jnp.where(half == 0, received[...], sent[...])
    clear_sides(field)
    zeros = [field[0:SUB, 0:LANES]] * blocks
    for chunk in range(chunks):
        start = (tiles_of(carried, chunk, 0), tiles_of(carried, chunk, 1))
        filter_back(count, planes, None, lower, chunk_of(field, chunk, chunks), start)
    x_twice(field, middle, high, low, parts)
    for chunk in range(chunks):

        def finish(d, p, value):
            for b, v in enumerate(value):
                at = (p * chunks + chunk) * blocks + b
                out[d, at] = v + local[d, at]

        rows = chunk_of(middle, chunk, chunks)
        latest, earlier = filter_forth(count, planes, rows, lower, (zeros, zeros), finish)
        put(carried, latest, chunk, 0)
        put(carried, earlier, chunk, 1)

        @pl.when(half > 0)
        def _():
            begin = (
                add(tiles_of(carried, chunk, 0), tiles_of(received, chunk, 0)),
                add(tiles_of(carried, chunk, 1), tiles_of(received, chunk, 1)),
            )
            filter_forth(count, planes, None, own, begin, finish)


def partner(pair):
    groups = lax.axis_size("gz") // 2
    m = jnp.where(lax.axis_index("gy") == 0, pair[0], pair[1])
    return (lax.axis_index("gz") % groups) ^ m


def split_kernel(pairs, pieces, *outs):
    for pair, out in zip(pairs, outs):
        out[...] = pieces[partner(pair)]


def merge_kernel(pairs, *refs):
    for pair, piece in zip(pairs, refs[:-1]):
        refs[-1][partner(pair)] = piece[...]


def place_kernel(pairs, *refs):
    pieces, (out, sems) = refs[: len(pairs)], refs[-2:]
    planes = out.shape[0]
    each = pieces[0].shape[0] // planes
    for i, (pair, piece) in enumerate(zip(pairs, pieces)):
        at = partner(pair) * each
        for p in range(planes):
            pltpu.make_async_copy(
                piece.at[pl.ds(p * each, each)], out.at[p, pl.ds(at, each)], sems.at[i]
            ).start()
    for i, piece in enumerate(pieces):
        pltpu.make_async_copy(piece, piece, sems.at[i]).wait()


def exchange_order(groups):
    order, last = [], groups - 1
    for m in sorted(range(1, last), key=lambda m: (m.bit_count(), m)):
        if m not in order:
            order += [m, last ^ m]
    return [m for i, m in enumerate(order) if m not in order[:i]] + [last]


def grouped_body(probe_fields, root_one, root_two, lateral_kernel_taps, dilations):
    _, planes, rows, columns = probe_fields.shape
    places = lax.axis_size("gz")
    groups = places // 2
    tiles, blocks, count = rows // SUB, columns // LANES, groups * planes
    chunks = tiles // groups

    def across(array, axis, m):
        return lax.ppermute(array, axis, [(i, i ^ m) for i in range(lax.axis_size(axis))])

    first = exchange_order(groups)
    second = [m ^ (groups - 1) or groups - 1 for m in first]
    pairs_in = [(0, 0), *zip(first, second)]
    pairs_out = [(m, m) for m in (0, *first[-2::-1], first[-1])]

    def across_pair(array, pair):
        moves = [
            (2 * i + core, 2 * (i ^ m) + core) for i in range(places) for core, m in enumerate(pair)
        ]
        return lax.ppermute(array, ("gz", "gy"), moves)

    def exchange(array, pairs):
        kernel = functools.partial(split_kernel, pairs)
        parts = call(kernel, [array.shape[1:]] * groups, [], [array])
        return [parts[0]] + [across_pair(*part) for part in zip(parts[1:], pairs[1:])]

    field = probe_fields.reshape(planes, tiles, SUB, blocks, LANES).transpose(0, 1, 3, 2, 4)
    tile, halo = (SUB, LANES), 2 * MARGIN // SUB
    hbm, vmem = pl.BlockSpec(memory_space=pltpu.HBM), pl.BlockSpec(memory_space=pltpu.VMEM)
    matrix = [pltpu.VMEM((rows, rows), jnp.bfloat16)] * 2
    edge_matrix = [pltpu.VMEM((2 * MARGIN, 2 * MARGIN), jnp.bfloat16)] * 2
    params = pltpu.CompilerParams(vmem_limit_bytes=24 << 20)

    def in_hbm(*arrays):
        return [pltpu.with_memory_space_constraint(array, pltpu.HBM) for array in arrays]

    edge, roots = pl.pallas_call(
        edge_kernel,
        out_shape=[
            pltpu.VMEM((planes, halo, blocks, *tile), jnp.float32),
            pltpu.VMEM((2 * planes, *tile), jnp.float32),
        ],
        in_specs=[hbm] * 3,
        out_specs=[vmem] * 2,
        scratch_shapes=[
            pltpu.VMEM((2, planes, columns), jnp.float32),
            pltpu.SemaphoreType.DMA((3,)),
        ],
        compiler_params=params,
        cost_estimate=NO_COST,
    )(*in_hbm(field, root_one, root_two))
    field, *matrices, x_step, x_taps = pl.pallas_call(
        load_kernel,
        out_shape=[
            pltpu.VMEM((planes, tiles, blocks, *tile), jnp.float32),
            *matrix,
            *edge_matrix,
            pltpu.VMEM(tile, jnp.int32),
            pltpu.VMEM(tile, jnp.float32),
        ],
        in_specs=[hbm] * 3 + [vmem],
        out_specs=[vmem] * 7,
        scratch_shapes=[
            pltpu.SMEM(dilations.shape, jnp.int32),
            pltpu.SMEM(lateral_kernel_taps.shape, jnp.float32),
            pltpu.SemaphoreType.DMA((2 + planes,)),
        ],
        compiler_params=params,
        cost_estimate=NO_COST,
    )(
        *in_hbm(field, dilations, lateral_kernel_taps),
        pltpu.with_memory_space_constraint(roots, pltpu.VMEM),
    )
    edge = across(edge, "gy", 1)

    width = 2 * LANES

    band = ((len(band_kinds(columns // width)[0]), 2 * width, width), jnp.bfloat16)
    high, low = call(
        functools.partial(band_kernel, columns), [band, band], [], [x_step, x_taps]
    )
    body_tiles = chunks * planes * blocks
    piece = (groups, body_tiles + 2 * planes, *tile)
    (pieces,) = call(
        functools.partial(y_inner_kernel, groups),
        [(groups, body_tiles, *tile)],
        [],
        [*matrices[:2], field],
    )
    (pieces,) = call(
        functools.partial(y_outer_kernel, groups, tiles),
        [piece],
        [],
        [*matrices[2:], edge, pieces, roots],
    )
    kernel = functools.partial(merge_kernel, pairs_in)
    (pieces,) = call(kernel, [piece], [], exchange(pieces, pairs_in))

    all_rows, wide = chunks * count * SUB, columns + 2 * LANES
    shared, message = (count, *tile), (chunks, 2, blocks, *tile)
    whole = (groups, body_tiles, *tile)
    scratch = [(all_rows, wide), (all_rows, columns), ((2 * all_rows, wide), jnp.bfloat16)]
    *own, mine = call(functools.partial(own_kernel, body_tiles), [shared] * 4, [], [pieces])
    mine = across(mine, "gz", groups)
    local, sent = call(
        functools.partial(local_kernel, groups, planes, chunks),
        [whole, message],
        scratch,
        [pieces, high, low, *own],
    )
    received = across(sent, "gz", groups)
    (mine,) = call(hand_on_kernel, [shared], [], [mine, *[sent]])
    other = across(mine, "gy", 1)
    lower = call(functools.partial(lower_kernel, groups), [shared] * 3, [], [*own, mine, other])
    (out,) = call(
        functools.partial(join_kernel, groups, planes, chunks),
        [whole],
        [message] + scratch,
        [local, sent, received, high, low, *own, *lower],
    )
    pieces = exchange(out, pairs_out)
    out, half = [], groups // 2 + 1
    for part in (slice(0, half), slice(half, groups)):
        arrays = [pltpu.with_memory_space_constraint(a, pltpu.VMEM) for a in pieces[part]]
        out = [
            pl.pallas_call(
                functools.partial(place_kernel, pairs_out[part]),
                out_shape=pltpu.HBM((planes, tiles * blocks, *tile), jnp.float32),
                in_specs=[vmem] * len(arrays) + [hbm] * len(out),
                out_specs=hbm,
                scratch_shapes=[pltpu.SemaphoreType.DMA((len(arrays),))],
                input_output_aliases={len(arrays): 0} if out else {},
                compiler_params=params,
                cost_estimate=NO_COST,
            )(*arrays, *out)
        ]
    (out,) = out
    out = out.reshape(planes, tiles, blocks, *tile).transpose(0, 1, 3, 2, 4)
    return out.reshape(probe_fields.shape)


def body(*arrays):
    probes, planes, rows, columns = arrays[0].shape
    places, row_places = lax.axis_size("gz"), lax.axis_size("gy")
    fits = (
        probes == 1
        and row_places == 2
        and places >= 4
        and places & (places - 1) == 0
        and rows % (SUB * (places // 2)) == 0
        and rows >= 4 * MARGIN
        and columns == SUB * LANES
        and planes * places >= 4
    )
    return grouped_body(*arrays) if fits else plain_body(*arrays)


def solution(mesh):
    placed = (P(None, "gz", "gy", None), P("gz", None), P("gz", None), P(), P())
    return jax.shard_map(
        body, mesh=mesh, in_specs=placed, out_specs=P(None, "gz", "gy", None), check_vma=False
    )
```

```python
import functools

import jax
import jax.numpy as jnp
from jax import lax
from jax.experimental import pallas as pl
from jax.experimental.pallas import tpu as pltpu
from jax.sharding import PartitionSpec as P

RADIUS = 2
DMAX = 8
MARGIN = RADIUS * DMAX
LANES = 128
SUB = 8
LOADS = 4


def padded_y(array, width):
    size, length = lax.axis_size("gy"), array.shape[2]
    up = [(i, (i + 1) % size) for i in range(size - 1)]
    down = [(j, i) for i, j in up]
    last = lax.slice_in_dim(array, length - width, length, axis=2)
    leading = lax.slice_in_dim(array, 0, width, axis=2)
    before = lax.ppermute(last, "gy", up)
    after = lax.ppermute(leading, "gy", down)
    return jnp.concatenate([before, array, after], axis=2)


def filter_coefficients(root_one, root_two):
    first = root_one + root_two
    second = -root_one * root_two
    gain = (1.0 - root_one) * (1.0 - root_two)
    return (first, second, gain)


def depth_scan(fields, first, second, pre_gain, post_gain, reverse):
    moved = jnp.moveaxis(fields, 1, 0)
    zero = jnp.zeros(moved.shape[1:], jnp.float32)

    def advance(carry, inputs):
        latest, earlier = carry
        plane, coef_one, coef_two, before, after = inputs
        value = before * plane + coef_one * latest + coef_two * earlier
        return ((value, latest), after * value)

    _, outputs = lax.scan(
        advance, (zero, zero), (moved, first, second, pre_gain, post_gain), reverse=reverse
    )
    return jnp.moveaxis(outputs, 0, 1)


def normalised(weights):
    return weights / (weights[..., :1] + 2.0 * jnp.sum(weights[..., 1:], -1, keepdims=True))


def lateral_padded(padded, scaled, dilation, axis, margin, length):
    result = scaled[0] * lax.dynamic_slice_in_dim(padded, margin, length, axis)
    for offset_tap in range(1, scaled.shape[0]):
        offset = dilation * offset_tap
        upper = lax.dynamic_slice_in_dim(padded, margin + offset, length, axis)
        lower = lax.dynamic_slice_in_dim(padded, margin - offset, length, axis)
        result = result + scaled[offset_tap] * (upper + lower)
    return result


def lateral_x(fields, scaled, dilation):
    padded = jnp.pad(fields, ((0, 0), (0, 0), (0, 0), (MARGIN, MARGIN)))
    return lateral_padded(padded, scaled, dilation, 3, MARGIN, fields.shape[3])


def lateral_y_twice(fields, scaled, dilation):
    rows = fields.shape[2]
    padded = padded_y(fields, 2 * MARGIN)
    middle = lateral_padded(padded, scaled, dilation, 2, MARGIN, rows + 2 * MARGIN)
    global_row = lax.axis_index("gy") * rows - MARGIN + jnp.arange(rows + 2 * MARGIN)
    inside = (global_row >= 0) & (global_row < rows * lax.axis_size("gy"))
    middle = jnp.where(inside[None, None, :, None], middle, 0.0)
    return lateral_padded(middle, scaled, dilation, 2, MARGIN, rows)


def plain_body(probe_fields, root_one, root_two, lateral_kernel_taps, dilations):
    roots = lax.all_gather(jnp.stack([root_one, root_two], 1), "gz", axis=0, tiled=True)
    first, second, gain = filter_coefficients(roots[:, 0], roots[:, 1])
    unity = jnp.ones_like(gain)
    first_next = jnp.concatenate([first[1:], jnp.zeros_like(first[:1])], 0)
    second_next = jnp.concatenate([second[2:], jnp.zeros_like(second[:2])], 0)
    scaled = normalised(lateral_kernel_taps)
    field = lateral_y_twice(probe_fields, scaled[1], dilations[1])
    field = lax.all_to_all(field, "gz", split_axis=2, concat_axis=1, tiled=True)
    field = depth_scan(field, first_next, second_next, unity, gain, True)
    field = lateral_x(field, scaled[0], dilations[0])
    field = lateral_x(field, scaled[0], dilations[0])
    field = depth_scan(field, first, second, gain, unity, False)
    return lax.all_to_all(field, "gz", split_axis=1, concat_axis=2, tiled=True)


NO_COST = pl.CostEstimate(flops=0, bytes_accessed=0, transcendentals=0)


def call(kernel, outs, scratch, arrays):
    arrays = [pltpu.with_memory_space_constraint(a, pltpu.VMEM) for a in arrays]
    outs, scratch = (
        [item if len(item) == 2 and isinstance(item[0], tuple) else (item, jnp.float32) for item in items]
        for items in (outs, scratch)
    )
    return pl.pallas_call(
        kernel,
        out_shape=[pltpu.VMEM(shape, dtype) for shape, dtype in outs],
        in_specs=[pl.BlockSpec(memory_space=pltpu.VMEM)] * len(arrays),
        out_specs=[pl.BlockSpec(memory_space=pltpu.VMEM)] * len(outs),
        scratch_shapes=[pltpu.VMEM(shape, dtype) for shape, dtype in scratch],
        compiler_params=pltpu.CompilerParams(vmem_limit_bytes=24 << 20),
        cost_estimate=NO_COST,
    )(*arrays)


def tap_vectors(taps, axis, shape):
    raw = [taps[axis, i] for i in range(RADIUS + 1)]
    total = raw[0] + 2.0 * functools.reduce(lambda a, b: a + b, raw[1:])
    scale = 1.0 / jnp.full(shape, total, jnp.float32)
    return [jnp.full(shape, tap, jnp.float32) * scale for tap in raw]


def split(value):
    high = value.astype(jnp.bfloat16)
    return high, (value - high.astype(jnp.float32)).astype(jnp.bfloat16)


def product(left, right):
    dot = functools.partial(jnp.dot, preferred_element_type=jnp.float32)
    return dot(left[0], right[0]) + (dot(left[0], right[1]) + dot(left[1], right[0]))


OFFSETS = range(-RADIUS, RADIUS + 1)


def double_taps(at, length, step, taps):
    sums = {}
    for a in OFFSETS:
        middle = at + a * step
        tap = jnp.where((middle >= 0) & (middle < length), taps[abs(a)], 0.0)
        for b in OFFSETS:
            sums[a + b] = sums.get(a + b, 0.0) + tap * taps[abs(b)]
    return sums


def fill_band(high, low, row_places, step, taps, begin, from_begin):
    part = 2 * SUB
    for i in range(0, high.shape[0], part):
        shape = (part, high.shape[1])
        at = lax.broadcasted_iota(jnp.int32, shape, 0) + (begin + i)
        apart = lax.broadcasted_iota(jnp.int32, shape, 1) + from_begin - at
        value = jnp.zeros(shape, jnp.float32)
        for o, total in double_taps(at, row_places, step, taps).items():
            value = jnp.where(apart == o * step, total, value)
        high[i : i + part], low[i : i + part] = split(value)


def edge_kernel(x_ref, one_ref, two_ref, edge, roots, rows, sems):
    depth = edge.shape[1]
    start = jnp.where(lax.axis_index("gy") == 0, x_ref.shape[1] - depth, 0)
    copies = [
        pltpu.make_async_copy(one_ref, rows.at[0], sems.at[0]),
        pltpu.make_async_copy(two_ref, rows.at[1], sems.at[1]),
        pltpu.make_async_copy(x_ref.at[:, pl.ds(start, depth)], edge, sems.at[2]),
    ]
    for copy in copies:
        copy.start()
    copies[0].wait()
    copies[1].wait()
    planes, blocks = rows.shape[1], rows.shape[2] // LANES
    for i in range(2):
        for p in range(planes):
            for b in range(blocks):
                lanes = slice(b * LANES, (b + 1) * LANES)
                roots[i * planes + p, b : b + 1] = rows[i, p : p + 1, lanes]
    copies[2].wait()


def load_kernel(
    x_ref, dilations_ref, taps_ref, _,
    whole, high, low, edge_high, edge_low, x_step, x_taps, dilations, taps, sems,
):
    row_at, row_places = lax.axis_index("gy"), lax.axis_size("gy")
    planes, tiles = x_ref.shape[:2]
    rows, part = tiles * SUB, tiles // LOADS
    copies = [
        pltpu.make_async_copy(dilations_ref, dilations, sems.at[0]),
        pltpu.make_async_copy(taps_ref, taps, sems.at[1]),
    ]
    copies += [
        pltpu.make_async_copy(
            x_ref.at[p, i * part : (i + 1) * part],
            whole.at[p, i * part : (i + 1) * part],
            sems.at[2 + p * LOADS + i],
        )
        for p in range(planes)
        for i in range(LOADS)
    ]
    for copy in copies:
        copy.start()
    copies[0].wait()
    copies[1].wait()
    x_step[...] = jnp.full(x_step.shape, dilations[0], jnp.int32)
    for i, tap in enumerate(tap_vectors(taps, 0, (1, LANES))):
        x_taps[i : i + 1] = tap
    step, weights = dilations[1], tap_vectors(taps, 1, (1, 1))
    length, begin = rows * row_places, row_at * rows
    fill_band(high, low, length, step, weights, begin, begin)
    near = begin + jnp.where(row_at == 0, rows - 2 * MARGIN, 0)
    beyond = begin + jnp.where(row_at == 0, rows, -2 * MARGIN)
    fill_band(edge_high, edge_low, length, step, weights, near, beyond)
    for copy in copies[2:]:
        copy.wait()


def columns_of(ref, p, b, width):
    rows = ref.shape[1] * SUB
    return jnp.concatenate([ref[p, :, b + i].reshape(rows, LANES) for i in range(width)], axis=1)


def y_inner_kernel(groups, high, low, x_ref, pieces):
    planes, tiles, blocks = x_ref.shape[:3]
    chunks, width = tiles // groups, 2
    for p in range(planes):
        for b in range(0, blocks, width):
            value = product((high[...], low[...]), split(columns_of(x_ref, p, b, width)))
            for i in range(tiles):
                for w in range(width):
                    tile = value[i * SUB : (i + 1) * SUB, w * LANES : (w + 1) * LANES]
                    pieces[i // chunks, (p * chunks + i % chunks) * blocks + b + w] = tile


def y_outer_kernel(groups, tiles, high, low, edge, given, roots, pieces):
    planes, halo, blocks = edge.shape[:3]
    chunks, width = tiles // groups, 2
    base = chunks * planes * blocks
    pieces[:, :base] = given[...]
    for i in range(groups):
        pieces[i, base:] = roots[...]
    first = jnp.where(lax.axis_index("gy") == 0, (tiles - halo) // chunks, 0)
    for p in range(planes):
        for b in range(0, blocks, width):
            value = product((high[...], low[...]), split(columns_of(edge, p, b, width)))
            for i in range(halo):
                for w in range(width):
                    tile = value[i * SUB : (i + 1) * SUB, w * LANES : (w + 1) * LANES]
                    to, at = first + i // chunks, (p * chunks + i % chunks) * blocks
                    pieces[to, at + b + w] = given[to, at + b + w] + tile


def band_kinds(count):
    kinds = sorted({0, min(1, count - 1), count - 1})
    return kinds, [0 if n == 0 else len(kinds) - 1 if n == count - 1 else 1 for n in range(count)]


def band_kernel(columns, x_step, x_taps, high, low):
    depth, width = high.shape[1:]
    step, taps = x_step[0:1], [x_taps[i : i + 1] for i in range(RADIUS + 1)]
    part, reach = 2 * SUB, 2 * MARGIN
    lane = lax.broadcasted_iota(jnp.int32, (part, LANES), 1)
    row = lax.broadcasted_iota(jnp.int32, (part, LANES), 0)
    high[...] = jnp.zeros(high.shape, high.dtype)
    low[...] = jnp.zeros(low.shape, low.dtype)
    for kind, n in enumerate(band_kinds(columns // width)[0]):
        for w in range(0, width, LANES):
            at = lax.broadcasted_iota(jnp.int32, (1, LANES), 1) + (n * width + w)
            sums = double_taps(at, columns, step, taps)
            lanes = slice(w, w + LANES)

            def rows_at(i, _):
                start = w + LANES - reach + i * part
                apart = row + (start - LANES - w) - lane
                value = jnp.zeros((part, LANES), jnp.float32)
                for o, total in sums.items():
                    value = jnp.where(apart == o * step, total, value)
                at_rows = pl.ds(pl.multiple_of(start, part), part)
                high[kind, at_rows, lanes], low[kind, at_rows, lanes] = split(value)
                return 0

            lax.fori_loop(0, (LANES + 2 * reach) // part, rows_at, 0, unroll=2)


def x_twice(source, result, high, low, parts):
    rows, (depth, width) = source.shape[0], high.shape[1:]
    parts[:rows], parts[rows:] = split(source[...])
    dot = functools.partial(jnp.dot, preferred_element_type=jnp.float32)
    for n, kind in enumerate(band_kinds(result.shape[1] // width)[1]):
        lanes = slice(n * width, n * width + depth)
        total = dot(parts[:, lanes], high[kind])
        total = total[:rows] + (total[rows:] + dot(parts[:rows, lanes], low[kind]))
        result[:, n * width : (n + 1) * width] = total


def add(a, b):
    return [x + y for x, y in zip(a, b)]


def times(ref, k, values):
    return [ref[k, b : b + 1] * value for b, value in enumerate(values)]


def tiles_of(ref, *at):
    return [ref[(*at, b)] for b in range(ref.shape[len(at)])]


def put(ref, values, *at):
    for b, value in enumerate(values):
        ref[(*at, b)] = value


def clear_sides(field):
    columns = field.shape[1] - 2 * LANES
    none = jnp.zeros((field.shape[0], LANES), jnp.float32)
    field[:, :LANES] = none
    field[:, LANES + columns :] = none


def row_tile(k):
    return pl.ds(pl.multiple_of(k * SUB, SUB), SUB)


def filter_back(count, planes, source, coefficients, field, start):
    first, second, gain = coefficients
    after, beyond = start

    def at(d, carry):
        for p in reversed(range(planes)):
            ahead, pending = carry
            k = d * planes + p
            value = ahead if source is None else add(source(d, p), ahead)
            for b, scaled in enumerate(times(gain, k, value)):
                field[row_tile(k), (b + 1) * LANES : (b + 2) * LANES] = scaled
            carry = (add(times(first, k, value), pending), times(second, k, value))
        return carry

    steps = count // planes
    return lax.fori_loop(0, steps, lambda i, c: at(steps - 1 - i, c), (after, beyond))


def filter_forth(count, planes, field, coefficients, start, finish):
    first, second, gain = coefficients

    def at(d, carry):
        for p in range(planes):
            latest, earlier = carry
            k = d * planes + p
            value = add(times(first, k, latest), times(second, k, earlier))
            if field is not None:
                blocks = len(value)
                there = [
                    field[row_tile(k), b * LANES : (b + 1) * LANES] for b in range(blocks)
                ]
                value = add(value, times(gain, k, there))
            finish(d, p, value)
            carry = (value, latest)
        return carry

    return lax.fori_loop(0, count // planes, at, start)


def store_coefficients(k, one, two, first, second, gain):
    first[k] = one + two
    second[k] = -one * two
    gain[k] = (1.0 - one) * (1.0 - two)


def hand_on_kernel(value, *refs):
    refs[-1][...] = value[...]


def own_kernel(base, pieces, first, second, gain, half_roots):
    groups = pieces.shape[0]
    planes = gain.shape[0] // groups
    row_at = lax.axis_index("gy")
    upper_rows = lax.broadcasted_iota(jnp.int32, (SUB, LANES), 0) < SUB // 2
    for d in range(groups):
        for p in range(planes):
            k = d * planes + p
            one, two = (pieces[d, base + i * planes + p] for i in range(2))
            store_coefficients(k, one, two, first, second, gain)
            front = jnp.where(upper_rows, one, pltpu.roll(two, SUB // 2, 0))
            back = jnp.where(upper_rows, pltpu.roll(one, SUB // 2, 0), two)
            half_roots[k] = jnp.where(row_at == 0, front, back)


def lower_kernel(groups, own_first, own_second, own_gain, mine, other, first, second, gain):
    half, row_at = lax.axis_index("gz") // groups, lax.axis_index("gy")

    @pl.when(half == 0)
    def _():
        first[...] = own_first[...]
        second[...] = own_second[...]
        gain[...] = own_gain[...]

    @pl.when(half > 0)
    def _():
        upper_rows = lax.broadcasted_iota(jnp.int32, (SUB, LANES), 0) < SUB // 2
        for k in range(gain.shape[0]):
            front = jnp.where(row_at == 0, mine[k], other[k])
            back = jnp.where(row_at == 0, other[k], mine[k])
            one = jnp.where(upper_rows, front, pltpu.roll(back, SUB // 2, 0))
            two = jnp.where(upper_rows, pltpu.roll(front, SUB // 2, 0), back)
            store_coefficients(k, one, two, first, second, gain)


def chunk_of(ref, chunk, chunks):
    rows = ref.shape[0] // chunks
    return ref.at[chunk * rows : (chunk + 1) * rows]


def local_kernel(
    groups, planes, chunks, pieces, high, low, first, second, gain,
    local, message, field, middle, parts,
):
    half = lax.axis_index("gz") // groups
    blocks = message.shape[2]
    count = groups * planes
    own = (first, second, gain)
    clear_sides(field)
    zeros = [field[0:SUB, 0:LANES]] * blocks
    carries = []
    for chunk in range(chunks):

        def source(d, p):
            return [pieces[d, (p * chunks + chunk) * blocks + b] for b in range(blocks)]

        rows = chunk_of(field, chunk, chunks)
        carries.append(filter_back(count, planes, source, own, rows, (zeros, zeros)))
        put(message, carries[-1][0], chunk, 0)
        put(message, carries[-1][1], chunk, 1)
    x_twice(field, middle, high, low, parts)
    for chunk in range(chunks):

        def finish(d, p, value):
            for b, v in enumerate(value):
                local[d, (p * chunks + chunk) * blocks + b] = v

        rows = chunk_of(middle, chunk, chunks)
        latest, earlier = filter_forth(count, planes, rows, own, (zeros, zeros), finish)

        @pl.when(half == 0)
        def _():
            put(message, latest, chunk, 0)
            put(message, earlier, chunk, 1)


def join_kernel(
    groups, planes, chunks, local, sent, received, high, low, *refs
):
    own, lower = refs[:3], refs[3:6]
    out, carried, field, middle, parts = refs[6:]
    half = lax.axis_index("gz") // groups
    blocks = sent.shape[2]
    count = groups * planes
    carried[...] = jnp.where(half == 0, received[...], sent[...])
    clear_sides(field)
    zeros = [field[0:SUB, 0:LANES]] * blocks
    for chunk in range(chunks):
        start = (tiles_of(carried, chunk, 0), tiles_of(carried, chunk, 1))
        filter_back(count, planes, None, lower, chunk_of(field, chunk, chunks), start)
    x_twice(field, middle, high, low, parts)
    for chunk in range(chunks):

        def finish(d, p, value):
            for b, v in enumerate(value):
                at = (p * chunks + chunk) * blocks + b
                out[d, at] = v + local[d, at]

        rows = chunk_of(middle, chunk, chunks)
        latest, earlier = filter_forth(count, planes, rows, lower, (zeros, zeros), finish)
        put(carried, latest, chunk, 0)
        put(carried, earlier, chunk, 1)

        @pl.when(half > 0)
        def _():
            begin = (
                add(tiles_of(carried, chunk, 0), tiles_of(received, chunk, 0)),
                add(tiles_of(carried, chunk, 1), tiles_of(received, chunk, 1)),
            )
            filter_forth(count, planes, None, own, begin, finish)


def partner(pair):
    groups = lax.axis_size("gz") // 2
    m = jnp.where(lax.axis_index("gy") == 0, pair[0], pair[1])
    return (lax.axis_index("gz") % groups) ^ m


def split_kernel(pairs, pieces, *outs):
    for pair, out in zip(pairs, outs):
        out[...] = pieces[partner(pair)]


def merge_kernel(pairs, *refs):
    for pair, piece in zip(pairs, refs[:-1]):
        refs[-1][partner(pair)] = piece[...]


def place_kernel(pairs, *refs):
    pieces, (out, sems) = refs[: len(pairs)], refs[-2:]
    planes = out.shape[0]
    each = pieces[0].shape[0] // planes
    for i, (pair, piece) in enumerate(zip(pairs, pieces)):
        at = partner(pair) * each
        for p in range(planes):
            pltpu.make_async_copy(
                piece.at[pl.ds(p * each, each)], out.at[p, pl.ds(at, each)], sems.at[i]
            ).start()
    for i, piece in enumerate(pieces):
        pltpu.make_async_copy(piece, piece, sems.at[i]).wait()


def exchange_order(groups):
    order, last = [], groups - 1
    for m in sorted(range(1, last), key=lambda m: (m.bit_count(), m)):
        if m not in order:
            order += [m, last ^ m]
    return [m for i, m in enumerate(order) if m not in order[:i]] + [last]


def grouped_body(probe_fields, root_one, root_two, lateral_kernel_taps, dilations):
    _, planes, rows, columns = probe_fields.shape
    places = lax.axis_size("gz")
    groups = places // 2
    tiles, blocks, count = rows // SUB, columns // LANES, groups * planes
    chunks = tiles // groups

    def across(array, axis, m):
        return lax.ppermute(array, axis, [(i, i ^ m) for i in range(lax.axis_size(axis))])

    first = exchange_order(groups)
    second = [m ^ (groups - 1) or groups - 1 for m in first]
    pairs_in = [(0, 0), *zip(first, second)]
    pairs_out = [(m, m) for m in (0, *first[-2::-1], first[-1])]

    def across_pair(array, pair):
        moves = [
            (2 * i + core, 2 * (i ^ m) + core) for i in range(places) for core, m in enumerate(pair)
        ]
        return lax.ppermute(array, ("gz", "gy"), moves)

    def exchange(array, pairs):
        kernel = functools.partial(split_kernel, pairs)
        parts = call(kernel, [array.shape[1:]] * groups, [], [array])
        return [parts[0]] + [across_pair(*part) for part in zip(parts[1:], pairs[1:])]

    field = probe_fields.reshape(planes, tiles, SUB, blocks, LANES).transpose(0, 1, 3, 2, 4)
    tile, halo = (SUB, LANES), 2 * MARGIN // SUB
    hbm, vmem = pl.BlockSpec(memory_space=pltpu.HBM), pl.BlockSpec(memory_space=pltpu.VMEM)
    matrix = [pltpu.VMEM((rows, rows), jnp.bfloat16)] * 2
    edge_matrix = [pltpu.VMEM((2 * MARGIN, 2 * MARGIN), jnp.bfloat16)] * 2
    params = pltpu.CompilerParams(vmem_limit_bytes=24 << 20)

    def in_hbm(*arrays):
        return [pltpu.with_memory_space_constraint(array, pltpu.HBM) for array in arrays]

    edge, roots = pl.pallas_call(
        edge_kernel,
        out_shape=[
            pltpu.VMEM((planes, halo, blocks, *tile), jnp.float32),
            pltpu.VMEM((2 * planes, *tile), jnp.float32),
        ],
        in_specs=[hbm] * 3,
        out_specs=[vmem] * 2,
        scratch_shapes=[
            pltpu.VMEM((2, planes, columns), jnp.float32),
            pltpu.SemaphoreType.DMA((3,)),
        ],
        compiler_params=params,
        cost_estimate=NO_COST,
    )(*in_hbm(field, root_one, root_two))
    field, *matrices, x_step, x_taps = pl.pallas_call(
        load_kernel,
        out_shape=[
            pltpu.VMEM((planes, tiles, blocks, *tile), jnp.float32),
            *matrix,
            *edge_matrix,
            pltpu.VMEM(tile, jnp.int32),
            pltpu.VMEM(tile, jnp.float32),
        ],
        in_specs=[hbm] * 3 + [vmem],
        out_specs=[vmem] * 7,
        scratch_shapes=[
            pltpu.SMEM(dilations.shape, jnp.int32),
            pltpu.SMEM(lateral_kernel_taps.shape, jnp.float32),
            pltpu.SemaphoreType.DMA((2 + planes * LOADS,)),
        ],
        compiler_params=params,
        cost_estimate=NO_COST,
    )(
        *in_hbm(field, dilations, lateral_kernel_taps),
        pltpu.with_memory_space_constraint(roots, pltpu.VMEM),
    )
    edge = across(edge, "gy", 1)

    width = 2 * LANES

    band = ((len(band_kinds(columns // width)[0]), 2 * width, width), jnp.bfloat16)
    high, low = call(
        functools.partial(band_kernel, columns), [band, band], [], [x_step, x_taps]
    )
    body_tiles = chunks * planes * blocks
    piece = (groups, body_tiles + 2 * planes, *tile)
    (pieces,) = call(
        functools.partial(y_inner_kernel, groups),
        [(groups, body_tiles, *tile)],
        [],
        [*matrices[:2], field],
    )
    (pieces,) = call(
        functools.partial(y_outer_kernel, groups, tiles),
        [piece],
        [],
        [*matrices[2:], edge, pieces, roots],
    )
    kernel = functools.partial(merge_kernel, pairs_in)
    (pieces,) = call(kernel, [piece], [], exchange(pieces, pairs_in))

    all_rows, wide = chunks * count * SUB, columns + 2 * LANES
    shared, message = (count, *tile), (chunks, 2, blocks, *tile)
    whole = (groups, body_tiles, *tile)
    scratch = [(all_rows, wide), (all_rows, columns), ((2 * all_rows, wide), jnp.bfloat16)]
    *own, mine = call(functools.partial(own_kernel, body_tiles), [shared] * 4, [], [pieces])
    mine = across(mine, "gz", groups)
    local, sent = call(
        functools.partial(local_kernel, groups, planes, chunks),
        [whole, message],
        scratch,
        [pieces, high, low, *own],
    )
    received = across(sent, "gz", groups)
    (mine,) = call(hand_on_kernel, [shared], [], [mine, *[sent]])
    other = across(mine, "gy", 1)
    lower = call(functools.partial(lower_kernel, groups), [shared] * 3, [], [*own, mine, other])
    (out,) = call(
        functools.partial(join_kernel, groups, planes, chunks),
        [whole],
        [message] + scratch,
        [local, sent, received, high, low, *own, *lower],
    )
    pieces = exchange(out, pairs_out)
    out, half = [], groups // 2 + 1
    for part in (slice(0, half), slice(half, groups)):
        arrays = [pltpu.with_memory_space_constraint(a, pltpu.VMEM) for a in pieces[part]]
        out = [
            pl.pallas_call(
                functools.partial(place_kernel, pairs_out[part]),
                out_shape=pltpu.HBM((planes, tiles * blocks, *tile), jnp.float32),
                in_specs=[vmem] * len(arrays) + [hbm] * len(out),
                out_specs=hbm,
                scratch_shapes=[pltpu.SemaphoreType.DMA((len(arrays),))],
                input_output_aliases={len(arrays): 0} if out else {},
                compiler_params=params,
                cost_estimate=NO_COST,
            )(*arrays, *out)
        ]
    (out,) = out
    out = out.reshape(planes, tiles, blocks, *tile).transpose(0, 1, 3, 2, 4)
    return out.reshape(probe_fields.shape)


def body(*arrays):
    probes, planes, rows, columns = arrays[0].shape
    places, row_places = lax.axis_size("gz"), lax.axis_size("gy")
    fits = (
        probes == 1
        and row_places == 2
        and places >= 4
        and places & (places - 1) == 0
        and rows % (SUB * (places // 2)) == 0
        and rows >= 4 * MARGIN
        and rows % (SUB * LOADS) == 0
        and columns == SUB * LANES
        and planes * places >= 4
    )
    return grouped_body(*arrays) if fits else plain_body(*arrays)


def solution(mesh):
    placed = (P(None, "gz", "gy", None), P("gz", None), P("gz", None), P(), P())
    return jax.shard_map(
        body, mesh=mesh, in_specs=placed, out_specs=P(None, "gz", "gy", None), check_vma=False
    )
```
